32 devices in a mesh: groups: 2 (over x), blk: 16 (over z, y, core).
Axes of the slice: x: 2, y: 2, z: 4, core: 2. Of those that a mesh axis runs over, the one named last changes fastest.
Arguments:
- points: float32 [64, 4096], P('groups', 'blk'), parts along dimension 0, may hold values from -5 to 5
- lengthscale: float32 [64], P('groups'), parts along dimension 0, may hold values from 2 to 8
- noise_var: float32 [8192], P(('groups', 'blk')), parts along dimension 0, may hold values from 0.5 to 2
- targets: float32 [64, 4096], P('groups', 'blk'), parts along dimension 0, may hold values from -9 to 9, as said below
Outputs:
- solution: float32 [64, 4096], P('groups', 'blk'), parts along dimension 0
- residual: float32 [64, 4096], P('groups', 'blk'), parts along dimension 0
The draws below stay inside these ranges and needn't reach their ends.
There are 2 independent parts, one for each index of `groups`. The reference program is written for one: setup_inputs(seed, part) draws one part's arguments, and reference() takes and returns one part's arrays. A program takes and returns all parts, laid end to end along the dimension named above; each array names one. Nothing has to cross between parts.
Inputs may be any that keep to these rules, and one draw needn't show every extreme that they name: `targets`: entries of order one, scales differing between rows and points.
All inputs are finite; a program needn't handle non-finite values.
Results may differ from the reference program's by a relative error of at most 0.00045.
Values sent between devices are 32-bit elements; how exact they have to be, the bound alone decides.
No kernel may reach another device: no remote copies, remote signals or barrier semaphores. Data moves between devices by JAX's collectives and lax.ppermute only.
A program may use at most 64 MiB of HBM per device.

```python
import math
import jax
import jax.numpy as jnp
from jax import lax

FEAT = 32
PROBES = 32
ITERS = 4
POINTS = 4096


def draw_targets(key, part):
    key = jax.random.fold_in(key, 7)
    keys_all = jax.random.split(key, 3)
    point_axis = jnp.arange(POINTS, dtype=jnp.float32)
    rising = jnp.exp(jnp.log(3.0) * point_axis / max(POINTS - 1, 1))
    point_factor = jnp.exp(jax.random.uniform(keys_all[1], (POINTS,), jnp.float32, jnp.log(0.33), 0.0))
    probe_factor = jnp.exp(jax.random.uniform(keys_all[2], (PROBES, 1), jnp.float32, jnp.log(0.1), 0.0))
    values = jnp.clip(jax.random.normal(keys_all[0], (PROBES, POINTS), jnp.float32), -3.0, 3.0)
    return (values * probe_factor * (rising * point_factor)[None, :]).astype(jnp.float32)


def steps_of(key, dims, shards, smallest, largest):
    def one(axis_at, parts):
        heights = jax.random.uniform(jax.random.fold_in(jax.random.fold_in(key, 6), axis_at), (parts,), jnp.float32, smallest / len(shards), largest / len(shards))
        return jnp.repeat(jnp.exp(heights), dims[axis_at] // parts).reshape((-1,) + (1,) * (len(dims) - axis_at - 1))

    gain = one(*shards[0])
    for cut in shards[1:]:
        gain = gain * one(*cut)
    return gain


def bell_draw(own_key, dims, scale, limit, pieces=(), kind=jnp.bfloat16):
    level = steps_of(own_key, dims, pieces, -0.22, 0.18) if pieces else 1.0
    drawn = jax.random.normal(own_key, dims, jnp.float32) * scale * level
    return jnp.minimum(jnp.maximum(drawn, -limit), limit).astype(kind)


def setup_inputs(seed: int = 0, part: int = 0) -> dict:
    splits = jax.random.split(jax.random.key(seed), 5)
    part_keys = jax.random.split(jax.random.fold_in(splits[4], part), 5)
    return {
        "points": bell_draw(part_keys[0], (FEAT, POINTS), 1.0, 5.0, ((1, 16),), jnp.float32),
        "lengthscale": jnp.clip(jnp.exp(jax.random.uniform(part_keys[1], (FEAT,), jnp.float32, math.log(2.0), math.log(8.0))), 2.0, 8.0),
        "noise_var": jnp.clip(0.5 + 1.5 * jax.random.uniform(part_keys[2], (POINTS,), jnp.float32) ** steps_of(part_keys[2], (POINTS,), ((0, 16),), -0.2, 0.2), 0.5, 2.0),
        "targets": draw_targets(jax.random.fold_in(jax.random.fold_in(splits[4], part), 71), part),
    }


def apply_operator(scaled, sqnorm, noise_var, direction):
    width = math.gcd(POINTS, 1024)
    count = POINTS // width

    def one_block(block_index):
        offset = (block_index * width).astype(jnp.int32)
        block_pts = lax.dynamic_slice_in_dim(scaled, offset, width, 1)
        block_sq = lax.dynamic_slice_in_dim(sqnorm, offset, width, 0)
        inner_prod = jnp.dot(block_pts.T, scaled, precision=lax.Precision.HIGHEST, preferred_element_type=jnp.float32)
        kernel_tile = jnp.exp(-0.5 * (block_sq[:, None] + sqnorm[None, :] - 2.0 * inner_prod))
        return jnp.dot(direction, kernel_tile.T, precision=lax.Precision.HIGHEST, preferred_element_type=jnp.float32)

    blocks = lax.map(one_block, jnp.arange(count, dtype=jnp.int32))
    applied = jnp.transpose(blocks, (1, 0, 2)).reshape(direction.shape[0], POINTS)
    return applied + noise_var[None, :] * direction


def reference(points, lengthscale, noise_var, targets):
    scaled = points / lengthscale[:, None]
    sqnorm = jnp.sum(scaled * scaled, axis=0)
    solution = jnp.zeros_like(targets)
    residual = targets
    direction = targets
    norm_now = jnp.sum(residual * residual, axis=1)
    for iteration in range(ITERS):
        applied = apply_operator(scaled, sqnorm, noise_var, direction)
        step_size = norm_now / jnp.sum(direction * applied, axis=1)
        solution = solution + step_size[:, None] * direction
        residual = residual - step_size[:, None] * applied
        norm_next = jnp.sum(residual * residual, axis=1)
        direction = residual + (norm_next / norm_now)[:, None] * direction
        norm_now = norm_next
    return solution, residual
```

```python
import jax
import jax.numpy as jnp
from jax import lax
from jax.sharding import PartitionSpec as P

ITERS = 4


def kernel_block(pts, sq, local_pts, local_sq):
    inner = jnp.dot(pts.T, local_pts, precision=lax.Precision.HIGHEST, preferred_element_type=jnp.float32)
    return jnp.exp(-0.5 * (sq[:, None] + local_sq[None, :] - 2.0 * inner))


def body(points, lengthscale, noise_var, targets):
    scaled = points / lengthscale[:, None]
    feats = scaled.shape[0]
    both = lax.all_gather(jnp.concatenate([scaled, targets], axis=0), "blk", axis=1, tiled=True)
    pts = both[:feats]
    local_sq = jnp.sum(scaled * scaled, axis=0)
    tile = kernel_block(pts, jnp.sum(pts * pts, axis=0), scaled, local_sq)

    residual = direction = both[feats:]
    my_residual = my_direction = targets
    my_solution = jnp.zeros_like(targets)
    norm_now = jnp.sum(residual * residual, axis=1)
    for iteration in range(ITERS):
        folded = jnp.dot(direction, tile, precision=lax.Precision.HIGHEST, preferred_element_type=jnp.float32)
        my_applied = folded + noise_var[None, :] * my_direction
        if iteration == ITERS - 1:
            part = jnp.sum(my_direction * my_applied, axis=1)
            curve = jnp.sum(lax.all_gather(part, "blk"), axis=0)
        else:
            applied = lax.all_gather(my_applied, "blk", axis=1, tiled=True)
            curve = jnp.sum(direction * applied, axis=1)
        step_size = norm_now / curve
        my_solution = my_solution + step_size[:, None] * my_direction
        my_residual = my_residual - step_size[:, None] * my_applied
        if iteration < ITERS - 1:
            residual = residual - step_size[:, None] * applied
            norm_next = jnp.sum(residual * residual, axis=1)
            ratio = (norm_next / norm_now)[:, None]
            direction = residual + ratio * direction
            my_direction = my_residual + ratio * my_direction
            norm_now = norm_next
    return (my_solution, my_residual)


def solution(mesh):
    in_specs = (P("groups", "blk"), P("groups"), P(("groups", "blk")), P("groups", "blk"))
    out_specs = (P("groups", "blk"), P("groups", "blk"))
    return jax.shard_map(body, mesh=mesh, in_specs=in_specs, out_specs=out_specs, check_vma=False)
```

```python
import jax
import jax.numpy as jnp
from jax import lax
from jax.sharding import PartitionSpec as P

ITERS = 4


def swap(x, n, stride):
    return lax.ppermute(x, "blk", [(i, i ^ stride) for i in range(n)])


def strides(n):
    return [1 << k for k in reversed(range(n.bit_length() - 1))]


def gather(x, n):
    if n & (n - 1):
        return lax.all_gather(x, "blk", axis=1, tiled=True)
    for stride in strides(n):
        x = jnp.concatenate([x, swap(x, n, stride)], axis=1)
    return x


def add_up(x, n):
    if n & (n - 1):
        return lax.psum(x, "blk")
    for stride in strides(n):
        x = x + swap(x, n, stride)
    return x


def kernel_block(pts, sq, local_pts, local_sq):
    inner = jnp.dot(pts.T, local_pts, precision=lax.Precision.HIGHEST, preferred_element_type=jnp.float32)
    return jnp.exp(-0.5 * (sq[:, None] + local_sq[None, :] - 2.0 * inner))


def solution(mesh):
    n = mesh.shape["blk"]

    def body(points, lengthscale, noise_var, targets):
        scaled = points / lengthscale[:, None]
        feats = scaled.shape[0]
        both = gather(jnp.concatenate([scaled, targets], axis=0), n)
        pts = both[:feats]
        local_sq = jnp.sum(scaled * scaled, axis=0)
        tile = kernel_block(pts, jnp.sum(pts * pts, axis=0), scaled, local_sq)

        residual = direction = both[feats:]
        my_residual = my_direction = targets
        my_solution = jnp.zeros_like(targets)
        norm_now = jnp.sum(residual * residual, axis=1)
        for iteration in range(ITERS):
            folded = jnp.dot(direction, tile, precision=lax.Precision.HIGHEST, preferred_element_type=jnp.float32)
            my_applied = folded + noise_var[None, :] * my_direction
            if iteration == ITERS - 1:
                curve = add_up(jnp.sum(my_direction * my_applied, axis=1), n)
            else:
                applied = gather(my_applied, n)
                curve = jnp.sum(direction * applied, axis=1)
            step_size = norm_now / curve
            my_solution = my_solution + step_size[:, None] * my_direction
            my_residual = my_residual - step_size[:, None] * my_applied
            if iteration < ITERS - 1:
                residual = residual - step_size[:, None] * applied
                norm_next = jnp.sum(residual * residual, axis=1)
                ratio = (norm_next / norm_now)[:, None]
                direction = residual + ratio * direction
                my_direction = my_residual + ratio * my_direction
                norm_now = norm_next
        return (my_solution, my_residual)

    in_specs = (P("groups", "blk"), P("groups"), P(("groups", "blk")), P("groups", "blk"))
    out_specs = (P("groups", "blk"), P("groups", "blk"))
    return jax.shard_map(body, mesh=mesh, in_specs=in_specs, out_specs=out_specs, check_vma=False)
```

```python
import jax
import jax.numpy as jnp
from jax import lax
from jax.sharding import PartitionSpec as P

ITERS = 4
TILE_BYTES = 16 << 20


def swap(x, n, stride):
    return lax.ppermute(x, "blk", [(i, i ^ stride) for i in range(n)])


def gather(x, n, strides):
    for stride in strides:
        x = jnp.concatenate([x, swap(x, n, stride)], axis=1)
    return x


def add_up(x, n, strides):
    for stride in strides:
        x = x + swap(x, n, stride)
    return x


def split(x, parts):
    out = []
    for _ in range(parts):
        high = lax.reduce_precision(x, 8, 7)
        out.append(high.astype(jnp.bfloat16))
        x = x - high
    return out


def kernel_block(pts, cols):
    high, mid, low = split(pts, 3)
    norms = split(-0.5 * jnp.sum(pts * pts, axis=0, keepdims=True), 3)
    ones = [jnp.ones_like(norms[0])] * 3
    left = jnp.concatenate([high, high, mid, high, low, mid] + norms + ones, axis=0)
    right = jnp.concatenate([high, mid, high, low, high, mid] + ones + norms, axis=0)[:, :cols]
    tile = jnp.exp(lax.dot_general(left, right, (((0,), (0,)), ((), ())), preferred_element_type=jnp.float32))
    return split(tile, 2)


def apply_block(direction, tile):
    rows = direction.shape[0]
    parts = split(direction, 3)
    high = jnp.dot(jnp.concatenate(parts, axis=0), tile[0], preferred_element_type=jnp.float32)
    low = jnp.dot(jnp.concatenate(parts[:2], axis=0), tile[1], preferred_element_type=jnp.float32)
    return high[:rows] + ((high[rows : 2 * rows] + low[:rows]) + (high[2 * rows :] + low[rows:]))


def solution(mesh):
    n = mesh.shape["blk"]
    strides = [1 << k for k in reversed(range(n.bit_length() - 1))]

    def body(points, lengthscale, noise_var, targets):
        feats, width = points.shape
        team = min(n, 4)
        while team < n and (n * width) * (n * width) // team * 4 > TILE_BYTES:
            team *= 2
        outer, inner = [s for s in strides if s >= team], [s for s in strides if s < team]
        cols = n // team * width

        scaled = points / lengthscale[:, None]
        mine = gather(jnp.concatenate([scaled, targets, noise_var[None, :]], axis=0), n, outer)
        noise = mine[-1:]
        both = gather(mine[:-1], n, inner)
        tile = kernel_block(both[:feats], cols)

        residual = direction = both[feats:]
        my_solution = jnp.zeros_like(targets)
        norm_now = jnp.sum(residual * residual, axis=1)
        for iteration in range(ITERS):
            my_applied = apply_block(direction, tile) + noise * direction[:, :cols]
            if iteration == ITERS - 1:
                curve = add_up(jnp.sum(direction[:, :cols] * my_applied, axis=1), n, inner)
                step_size = (norm_now / curve)[:, None]
                my_solution = my_solution + step_size * direction[:, :width]
                return my_solution, residual[:, :width] - step_size * my_applied[:, :width]
            applied = gather(my_applied, n, inner)
            curve = jnp.sum(direction * applied, axis=1)
            step_size = (norm_now / curve)[:, None]
            my_solution = my_solution + step_size * direction[:, :width]
            residual = residual - step_size * applied
            norm_next = jnp.sum(residual * residual, axis=1)
            direction = residual + (norm_next / norm_now)[:, None] * direction
            norm_now = norm_next

    in_specs = (P("groups", "blk"), P("groups"), P(("groups", "blk")), P("groups", "blk"))
    out_specs = (P("groups", "blk"), P("groups", "blk"))
    return jax.shard_map(body, mesh=mesh, in_specs=in_specs, out_specs=out_specs, check_vma=False)
```

```python
import math

import jax
import jax.numpy as jnp
from jax import lax
from jax.experimental import pallas as pl
from jax.experimental.pallas import tpu as pltpu
from jax.sharding import PartitionSpec as P

ITERS = 4
TILE_BYTES = 16 << 20
VMEM_BYTES = 16 << 20
NORM_ROWS = 16
POINT_SCALE = math.sqrt(math.log2(math.e))


def swap(x, n, stride):
    return lax.ppermute(x, "blk", [(i, i ^ stride) for i in range(n)])


def gather(x, n, strides):
    for stride in strides:
        x = jnp.concatenate([x, swap(x, n, stride)], axis=1)
    return x


def add_up(x, n, strides):
    for stride in strides:
        x = x + swap(x, n, stride)
    return x


def split(x, parts):
    out = []
    for _ in range(parts):
        high = lax.reduce_precision(x, 8, 7)
        out.append(high.astype(jnp.bfloat16))
        x = x - high
    return out


def halve(x):
    high = x.astype(jnp.bfloat16)
    return high, x - high.astype(jnp.float32)


def operands(pts):
    high, rest = halve(pts)
    mid, rest = halve(rest)
    low = rest.astype(jnp.bfloat16)
    norms = -0.5 * jnp.sum(pts * pts, axis=0, keepdims=True)
    row = lax.broadcasted_iota(jnp.int32, (NORM_ROWS, pts.shape[1]), 0)
    left = jnp.where((row >= 3) & (row < 6), 1.0, 0.0)
    right = jnp.where(row < 3, 1.0, 0.0)
    for k in range(3):
        part, norms = halve(norms)
        part = part.astype(jnp.float32)
        left = jnp.where(row == k, part, left)
        right = jnp.where(row == 3 + k, part, right)
    left = jnp.concatenate([high, high, mid, high, low, mid, left.astype(jnp.bfloat16)], axis=0)
    right = jnp.concatenate([high, mid, high, low, high, mid, right.astype(jnp.bfloat16)], axis=0)
    return left, right


def build_kernel(all_ref, mine_ref, scale_ref, high_ref, low_ref, right_ref):
    @pl.when(pl.program_id(0) == 0)
    def _():
        right_ref[...] = operands(mine_ref[...] * scale_ref[...])[1]

    left = operands(all_ref[...] * scale_ref[...])[0]
    cols = right_ref.shape[1]
    step = min(cols, 256)
    for at in range(0, cols, step):
        here = pl.ds(at, step)
        power = lax.dot_general(
            left, right_ref[:, here], (((0,), (0,)), ((), ())), preferred_element_type=jnp.float32
        )
        high, rest = halve(jnp.exp2(power))
        high_ref[:, here] = high
        low_ref[:, here] = rest.astype(jnp.bfloat16)


def kernel_block(pts, scale, cols):
    feats, total = pts.shape
    block = min(total, 512)
    out = jax.ShapeDtypeStruct((total, cols), jnp.bfloat16)
    spec = pl.BlockSpec((block, cols), lambda i: (i, 0))
    return pl.pallas_call(
        build_kernel,
        grid=(total // block,),
        out_shape=(out, out),
        in_specs=[
            pl.BlockSpec((feats, block), lambda i: (0, i)),
            pl.BlockSpec((feats, cols), lambda i: (0, 0)),
            pl.BlockSpec((feats, 1), lambda i: (0, 0)),
        ],
        out_specs=(spec, spec),
        scratch_shapes=[pltpu.VMEM((6 * feats + NORM_ROWS, cols), jnp.bfloat16)],
        compiler_params=pltpu.CompilerParams(vmem_limit_bytes=VMEM_BYTES),
        cost_estimate=pl.CostEstimate(
            flops=2 * total * cols * 256, bytes_accessed=4 * total * (cols + feats), transcendentals=total * cols
        ),
    )(pts, pts[:, :cols], scale)


def apply_block(direction, tile):
    rows = direction.shape[0]
    parts = split(direction, 3)
    high = jnp.dot(jnp.concatenate(parts, axis=0), tile[0], preferred_element_type=jnp.float32)
    low = jnp.dot(jnp.concatenate(parts[:2], axis=0), tile[1], preferred_element_type=jnp.float32)
    return high[:rows] + ((high[rows : 2 * rows] + low[:rows]) + (high[2 * rows :] + low[rows:]))


def solution(mesh):
    n = mesh.shape["blk"]
    strides = [1 << k for k in reversed(range(n.bit_length() - 1))]

    def body(points, lengthscale, noise_var, targets):
        feats, width = points.shape
        team = min(n, 4)
        while team < n and (n * width) * (n * width) // team * 4 > TILE_BYTES:
            team *= 2
        outer, inner = [s for s in strides if s >= team], [s for s in strides if s < team]
        cols = n // team * width

        block = lax.optimization_barrier(jnp.concatenate([points, targets, noise_var[None, :]], axis=0))
        mine = gather(block, n, outer)
        noise = mine[-1:]
        both = gather(mine[:-1], n, inner)
        tile = kernel_block(both[:feats], (POINT_SCALE / lengthscale)[:, None], cols)

        residual = direction = both[feats:]
        my_solution = jnp.zeros_like(block[feats:-1])
        norm_now = jnp.sum(residual * residual, axis=1)
        for iteration in range(ITERS):
            my_applied = apply_block(direction, tile) + noise * direction[:, :cols]
            if iteration == ITERS - 1:
                curve = add_up(jnp.sum(direction[:, :cols] * my_applied, axis=1), n, inner)
                step_size = (norm_now / curve)[:, None]
                my_solution = my_solution + step_size * direction[:, :width]
                return my_solution, residual[:, :width] - step_size * my_applied[:, :width]
            applied = gather(my_applied, n, inner)
            curve = jnp.sum(direction * applied, axis=1)
            step_size = (norm_now / curve)[:, None]
            my_solution = my_solution + step_size * direction[:, :width]
            residual = residual - step_size * applied
            norm_next = jnp.sum(residual * residual, axis=1)
            direction = residual + (norm_next / norm_now)[:, None] * direction
            norm_now = norm_next

    in_specs = (P("groups", "blk"), P("groups"), P(("groups", "blk")), P("groups", "blk"))
    out_specs = (P("groups", "blk"), P("groups", "blk"))
    return jax.shard_map(body, mesh=mesh, in_specs=in_specs, out_specs=out_specs, check_vma=False)
```

```python
import math

import jax
import jax.numpy as jnp
from jax import lax
from jax.experimental import pallas as pl
from jax.experimental.pallas import tpu as pltpu
from jax.sharding import PartitionSpec as P

ITERS = 4
TILE_BYTES = 16 << 20
VMEM_BYTES = 16 << 20
NORM_ROWS = 16
POINT_SCALE = math.sqrt(math.log2(math.e))


def swap(x, n, stride):
    return lax.ppermute(x, "blk", [(i, i ^ stride) for i in range(n)])


def gather(x, n, strides):
    for stride in strides:
        x = jnp.concatenate([x, swap(x, n, stride)], axis=1)
    return x


def line(x, n, low, high):
    groups = [[base + low * k for k in range(high // low)] for base in range(n) if base % high < low]
    return lax.all_gather(x, "blk", axis_index_groups=groups, axis=1, tiled=True)


def add_up(x, n, strides):
    for stride in strides:
        x = x + swap(x, n, stride)
    return x


def split(x, parts):
    out = []
    for _ in range(parts):
        high = lax.reduce_precision(x, 8, 7)
        out.append(high.astype(jnp.bfloat16))
        x = x - high
    return out


def halve(x):
    high = x.astype(jnp.bfloat16)
    return high, x - high.astype(jnp.float32)


def operands(pts):
    high, rest = halve(pts)
    mid, rest = halve(rest)
    low = rest.astype(jnp.bfloat16)
    norms = -0.5 * jnp.sum(pts * pts, axis=0, keepdims=True)
    row = lax.broadcasted_iota(jnp.int32, (NORM_ROWS, pts.shape[1]), 0)
    left = jnp.where((row >= 3) & (row < 6), 1.0, 0.0)
    right = jnp.where(row < 3, 1.0, 0.0)
    for k in range(3):
        part, norms = halve(norms)
        part = part.astype(jnp.float32)
        left = jnp.where(row == k, part, left)
        right = jnp.where(row == 3 + k, part, right)
    left = jnp.concatenate([high, high, mid, high, low, mid, left.astype(jnp.bfloat16)], axis=0)
    right = jnp.concatenate([high, mid, high, low, high, mid, right.astype(jnp.bfloat16)], axis=0)
    return left, right


def build_kernel(all_ref, mine_ref, scale_ref, high_ref, low_ref, right_ref):
    @pl.when(pl.program_id(0) == 0)
    def _():
        right_ref[...] = operands(mine_ref[...] * scale_ref[...])[1]

    left = operands(all_ref[...] * scale_ref[...])[0]
    cols = right_ref.shape[1]
    step = min(cols, 256)
    for at in range(0, cols, step):
        here = pl.ds(at, step)
        power = lax.dot_general(
            left, right_ref[:, here], (((0,), (0,)), ((), ())), preferred_element_type=jnp.float32
        )
        high, rest = halve(jnp.exp2(power))
        high_ref[:, here] = high
        low_ref[:, here] = rest.astype(jnp.bfloat16)


def kernel_block(pts, mine, scale):
    feats, total = pts.shape
    cols = mine.shape[1]
    block = min(total, 512)
    out = jax.ShapeDtypeStruct((total, cols), jnp.bfloat16)
    spec = pl.BlockSpec((block, cols), lambda i: (i, 0))
    return pl.pallas_call(
        build_kernel,
        grid=(total // block,),
        out_shape=(out, out),
        in_specs=[
            pl.BlockSpec((feats, block), lambda i: (0, i)),
            pl.BlockSpec((feats, cols), lambda i: (0, 0)),
            pl.BlockSpec((feats, 1), lambda i: (0, 0)),
        ],
        out_specs=(spec, spec),
        scratch_shapes=[pltpu.VMEM((6 * feats + NORM_ROWS, cols), jnp.bfloat16)],
        compiler_params=pltpu.CompilerParams(vmem_limit_bytes=VMEM_BYTES),
        cost_estimate=pl.CostEstimate(
            flops=2 * total * cols * 256, bytes_accessed=4 * total * (cols + feats), transcendentals=total * cols
        ),
    )(pts, mine, scale)


def apply_block(direction, tile):
    rows = direction.shape[0]
    parts = split(direction, 3)
    high = jnp.dot(jnp.concatenate(parts, axis=0), tile[0], preferred_element_type=jnp.float32)
    low = jnp.dot(jnp.concatenate(parts[:2], axis=0), tile[1], preferred_element_type=jnp.float32)
    return high[:rows] + ((high[rows : 2 * rows] + low[:rows]) + (high[2 * rows :] + low[rows:]))


def solution(mesh):
    n = mesh.shape["blk"]
    strides = [1 << k for k in reversed(range(n.bit_length() - 1))]

    def body(points, lengthscale, noise_var, targets):
        feats, width = points.shape
        team = min(n, 4)
        while team < n and (n * width) * (n * width) // team * 4 > TILE_BYTES:
            team *= 2
        inner = [s for s in strides if s < team // 2]
        index = lax.axis_index("blk")
        cols = n // team * width
        cols_at = index // (team // 2) % 2 * cols
        block_at = cols_at + index // team * width

        def gather_team(x):
            return gather(line(x, n, team // 2, team), n, inner)

        block = lax.optimization_barrier(jnp.concatenate([points, targets, noise_var[None, :]], axis=0))
        mine = line(block, n, team, n) if team < n else block
        noise = mine[-1:]
        both = gather_team(mine[:-1])
        tile = kernel_block(both[:feats], mine[:feats], (POINT_SCALE / lengthscale)[:, None])

        def own(x, at, size):
            return lax.dynamic_slice_in_dim(x, at, size, 1)

        residual = direction = both[feats:]
        my_solution = jnp.zeros_like(block[feats:-1])
        norm_now = jnp.sum(residual * residual, axis=1)
        for iteration in range(ITERS):
            my_direction = own(direction, cols_at, cols)
            my_applied = apply_block(direction, tile) + noise * my_direction
            if iteration == ITERS - 1:
                curve = add_up(jnp.sum(my_direction * my_applied, axis=1), n, [team // 2] + inner)
                step_size = (norm_now / curve)[:, None]
                my_solution = my_solution + step_size * own(direction, block_at, width)
                return my_solution, own(residual, block_at, width) - step_size * own(my_applied, index // team * width, width)
            applied = gather_team(my_applied)
            curve = jnp.sum(direction * applied, axis=1)
            step_size = (norm_now / curve)[:, None]
            my_solution = my_solution + step_size * own(direction, block_at, width)
            residual = residual - step_size * applied
            norm_next = jnp.sum(residual * residual, axis=1)
            direction = residual + (norm_next / norm_now)[:, None] * direction
            norm_now = norm_next

    in_specs = (P("groups", "blk"), P("groups"), P(("groups", "blk")), P("groups", "blk"))
    out_specs = (P("groups", "blk"), P("groups", "blk"))
    return jax.shard_map(body, mesh=mesh, in_specs=in_specs, out_specs=out_specs, check_vma=False)
```

```python
import math

import jax
import jax.numpy as jnp
from jax import lax
from jax.experimental import pallas as pl
from jax.experimental.pallas import tpu as pltpu
from jax.sharding import PartitionSpec as P

ITERS = 4
TILE_BYTES = 16 << 20
VMEM_BYTES = 16 << 20
NORM_ROWS = 16
POINT_SCALE = math.sqrt(math.log2(math.e))


def swap(x, n, stride):
    return lax.ppermute(x, "blk", [(i, i ^ stride) for i in range(n)])


def gather(x, n, strides):
    for stride in strides:
        x = jnp.concatenate([x, swap(x, n, stride)], axis=1)
    return x


def add_up(x, n, strides):
    for stride in strides:
        x = x + swap(x, n, stride)
    return x


def split(x, parts):
    out = []
    for _ in range(parts):
        high = lax.reduce_precision(x, 8, 7)
        out.append(high.astype(jnp.bfloat16))
        x = x - high
    return out


def halve(x):
    high = x.astype(jnp.bfloat16)
    return high, x - high.astype(jnp.float32)


def operands(pts):
    high, rest = halve(pts)
    mid, rest = halve(rest)
    low = rest.astype(jnp.bfloat16)
    norms = -0.5 * jnp.sum(pts * pts, axis=0, keepdims=True)
    row = lax.broadcasted_iota(jnp.int32, (NORM_ROWS, pts.shape[1]), 0)
    left = jnp.where((row >= 3) & (row < 6), 1.0, 0.0)
    right = jnp.where(row < 3, 1.0, 0.0)
    for k in range(3):
        part, norms = halve(norms)
        part = part.astype(jnp.float32)
        left = jnp.where(row == k, part, left)
        right = jnp.where(row == 3 + k, part, right)
    left = jnp.concatenate([high, high, mid, high, low, mid, left.astype(jnp.bfloat16)], axis=0)
    right = jnp.concatenate([high, mid, high, low, high, mid, right.astype(jnp.bfloat16)], axis=0)
    return left, right


def build_kernel(all_ref, mine_ref, scale_ref, high_ref, low_ref, right_ref):
    @pl.when(pl.program_id(0) == 0)
    def _():
        right_ref[...] = operands(mine_ref[...] * scale_ref[...])[1]

    left = operands(all_ref[...] * scale_ref[...])[0]
    cols = right_ref.shape[1]
    step = min(cols, 256)
    for at in range(0, cols, step):
        here = pl.ds(at, step)
        power = lax.dot_general(
            left, right_ref[:, here], (((0,), (0,)), ((), ())), preferred_element_type=jnp.float32
        )
        high, rest = halve(jnp.exp2(power))
        high_ref[:, here] = high
        low_ref[:, here] = rest.astype(jnp.bfloat16)


def kernel_block(pts, scale, cols):
    feats, total = pts.shape
    block = min(total, 512)
    out = jax.ShapeDtypeStruct((total, cols), jnp.bfloat16)
    spec = pl.BlockSpec((block, cols), lambda i: (i, 0))
    return pl.pallas_call(
        build_kernel,
        grid=(total // block,),
        out_shape=(out, out),
        in_specs=[
            pl.BlockSpec((feats, block), lambda i: (0, i)),
            pl.BlockSpec((feats, cols), lambda i: (0, 0)),
            pl.BlockSpec((feats, 1), lambda i: (0, 0)),
        ],
        out_specs=(spec, spec),
        scratch_shapes=[pltpu.VMEM((6 * feats + NORM_ROWS, cols), jnp.bfloat16)],
        compiler_params=pltpu.CompilerParams(vmem_limit_bytes=VMEM_BYTES),
        cost_estimate=pl.CostEstimate(
            flops=2 * total * cols * 256, bytes_accessed=4 * total * (cols + feats), transcendentals=total * cols
        ),
    )(pts, pts[:, :cols], scale)


def apply_block(direction, tile):
    rows = direction.shape[0]
    parts = split(direction, 3)
    high = jnp.dot(jnp.concatenate(parts, axis=0), tile[0], preferred_element_type=jnp.float32)
    low = jnp.dot(jnp.concatenate(parts[:2], axis=0), tile[1], preferred_element_type=jnp.float32)
    return high[:rows] + ((high[rows : 2 * rows] + low[:rows]) + (high[2 * rows :] + low[rows:]))


def solution(mesh):
    n = mesh.shape["blk"]
    strides = [1 << k for k in reversed(range(n.bit_length() - 1))]

    def body(points, lengthscale, noise_var, targets):
        feats, width = points.shape
        team = min(n, 4)
        while team < n and (n * width) * (n * width) // team * 4 > TILE_BYTES:
            team *= 2
        outer, inner = [s for s in strides if s >= team], [s for s in strides if s < team]
        cols = n // team * width
        at = 0

        block = lax.optimization_barrier(jnp.concatenate([points, targets, noise_var[None, :]], axis=0))
        rows = block.shape[0]
        if team == 4 and n == 16:
            sides = n // 2
            groups = [list(range(base, n, 2)) for base in range(2)]
            copies = jnp.broadcast_to(block[None], (sides, *block.shape))
            got = lax.all_to_all(copies, "blk", 0, 0, axis_index_groups=groups).reshape(sides // 2, 2, rows, width)
            index = lax.axis_index("blk")
            side, at = index // 2 % 2, index // team * width

            def lay(which):
                part = lax.dynamic_index_in_dim(got, which, 1, keepdims=False)
                return jnp.transpose(part, (1, 0, 2)).reshape(rows, cols)

            mine = lay(side)
            both = gather(jnp.concatenate([mine, lay(1 - side)], axis=1)[:-1], n, [1])
        else:
            mine = gather(block, n, outer)
            both = gather(mine[:-1], n, inner)
        noise = mine[-1:]
        tile = kernel_block(both[:feats], (POINT_SCALE / lengthscale)[:, None], cols)

        def own(x):
            return lax.dynamic_slice_in_dim(x, at, width, 1)

        residual = direction = both[feats:]
        my_solution = jnp.zeros_like(block[feats:-1])
        norm_now = jnp.sum(residual * residual, axis=1)
        for iteration in range(ITERS):
            my_applied = apply_block(direction, tile) + noise * direction[:, :cols]
            if iteration == ITERS - 1:
                curve = add_up(jnp.sum(direction[:, :cols] * my_applied, axis=1), n, inner)
                step_size = (norm_now / curve)[:, None]
                my_solution = my_solution + step_size * own(direction)
                return my_solution, own(residual) - step_size * own(my_applied)
            applied = gather(my_applied, n, inner)
            curve = jnp.sum(direction * applied, axis=1)
            step_size = (norm_now / curve)[:, None]
            my_solution = my_solution + step_size * own(direction)
            residual = residual - step_size * applied
            norm_next = jnp.sum(residual * residual, axis=1)
            direction = residual + (norm_next / norm_now)[:, None] * direction
            norm_now = norm_next

    in_specs = (P("groups", "blk"), P("groups"), P(("groups", "blk")), P("groups", "blk"))
    out_specs = (P("groups", "blk"), P("groups", "blk"))
    return jax.shard_map(body, mesh=mesh, in_specs=in_specs, out_specs=out_specs, check_vma=False)
```

```python
import math

import jax
import jax.numpy as jnp
from jax import lax
from jax.experimental import pallas as pl
from jax.experimental.pallas import tpu as pltpu
from jax.sharding import PartitionSpec as P

ITERS = 4
TILE_BYTES = 16 << 20
VMEM_BYTES = 16 << 20
NORM_ROWS = 64
POINT_SCALE = math.sqrt(math.log2(math.e))


def swap(x, n, stride):
    return lax.ppermute(x, "blk", [(i, i ^ stride) for i in range(n)])


def add_up(x, n, strides):
    for stride in strides:
        x = x + swap(x, n, stride)
    return x


def split(x, parts):
    out = []
    for _ in range(parts):
        high = lax.reduce_precision(x, 8, 7)
        out.append(high.astype(jnp.bfloat16))
        x = x - high
    return out


def halve(x):
    high = x.astype(jnp.bfloat16)
    return high, x - high.astype(jnp.float32)


def operands(pts):
    high, rest = halve(pts)
    mid, rest = halve(rest)
    low = rest.astype(jnp.bfloat16)
    norms = -0.5 * jnp.sum(pts * pts, axis=0, keepdims=True)
    row = lax.broadcasted_iota(jnp.int32, (NORM_ROWS, pts.shape[1]), 0)
    left = jnp.where((row >= 3) & (row < 6), 1.0, 0.0)
    right = jnp.where(row < 3, 1.0, 0.0)
    for k in range(3):
        part, norms = halve(norms)
        part = part.astype(jnp.float32)
        left = jnp.where(row == k, part, left)
        right = jnp.where(row == 3 + k, part, right)
    left = jnp.concatenate([high, high, mid, high, low, mid, left.astype(jnp.bfloat16)], axis=0)
    right = jnp.concatenate([high, mid, high, low, high, mid, right.astype(jnp.bfloat16)], axis=0)
    return left, right


def build_kernel(rows_ref, mine_ref, scale_ref, high_ref, low_ref, right_ref):
    @pl.when(pl.program_id(0) == 0)
    def _():
        right_ref[...] = operands(mine_ref[...] * scale_ref[...])[1]

    left = jnp.transpose(operands(rows_ref[...] * scale_ref[...])[0])
    cols = right_ref.shape[1]
    step = min(cols, 256)
    for at in range(0, cols, step):
        here = pl.ds(at, step)
        power = jnp.dot(left, right_ref[:, here], preferred_element_type=jnp.float32)
        high, rest = halve(jnp.exp2(power))
        high_ref[:, here] = high
        low_ref[:, here] = rest.astype(jnp.bfloat16)


def build_piece(rows, mine, scale):
    feats, total = rows.shape
    cols = mine.shape[1]
    block = min(total, 512)
    out = jax.ShapeDtypeStruct((total, cols), jnp.bfloat16)
    spec = pl.BlockSpec((block, cols), lambda i: (i, 0))
    return pl.pallas_call(
        build_kernel,
        grid=(total // block,),
        out_shape=(out, out),
        in_specs=[
            pl.BlockSpec((feats, block), lambda i: (0, i)),
            pl.BlockSpec((feats, cols), lambda i: (0, 0)),
            pl.BlockSpec((feats, 1), lambda i: (0, 0)),
        ],
        out_specs=(spec, spec),
        scratch_shapes=[pltpu.VMEM((6 * feats + NORM_ROWS, cols), jnp.bfloat16)],
        compiler_params=pltpu.CompilerParams(vmem_limit_bytes=VMEM_BYTES),
        cost_estimate=pl.CostEstimate(
            flops=2 * total * cols * 256, bytes_accessed=4 * total * (cols + feats), transcendentals=total * cols
        ),
    )(rows, mine, scale)


def apply_piece(vectors, piece):
    parts = split(vectors, 3)
    high = jnp.dot(jnp.concatenate(parts, axis=0), piece[0], preferred_element_type=jnp.float32)
    low = jnp.dot(jnp.concatenate(parts[:2], axis=0), piece[1], preferred_element_type=jnp.float32)
    return high, low


def solution(mesh):
    n = mesh.shape["blk"]
    strides = [1 << k for k in reversed(range(n.bit_length() - 1))]

    def body(points, lengthscale, noise_var, targets):
        feats, width = points.shape
        probes = targets.shape[0]
        team = min(n, 4)
        while team < n and (n * width) * (n * width) // team * 4 > TILE_BYTES:
            team *= 2
        outer, inner = [s for s in strides if s >= team], [s for s in strides if s < team]

        def arrivals(x):
            pieces = [x]
            for stride in inner:
                pieces.append(swap(jnp.concatenate(pieces, axis=1), n, stride))
            return pieces

        mine = lax.optimization_barrier(jnp.concatenate([points, targets, noise_var[None, :]], axis=0))
        for stride in outer:
            mine = jnp.concatenate([mine, swap(mine, n, stride)], axis=1)
        noise = mine[-1:]
        scale = (POINT_SCALE / lengthscale)[:, None]
        first = arrivals(mine[:-1])
        tile = [build_piece(x[:feats], mine[:feats], scale) for x in first]

        def operator(pieces):
            terms = [apply_piece(x, piece) for x, piece in zip(pieces, tile)]
            high, low = (sum(t[1:], t[0]) for t in zip(*terms))
            corrections = (high[probes : 2 * probes] + low[:probes]) + (high[2 * probes :] + low[probes:])
            return high[:probes] + corrections + noise * pieces[0]

        starts = [x[feats:] for x in first]
        residual = direction = jnp.concatenate(starts, axis=1)
        cols = noise.shape[1]
        my_solution = jnp.zeros_like(direction[:, :width])
        norm_now = jnp.sum(residual * residual, axis=1)
        my_applied = my_image = operator(starts)
        for iteration in range(ITERS - 1):
            pieces = arrivals(my_applied)
            my_next = operator(pieces)
            applied = jnp.concatenate(pieces, axis=1)
            curve = jnp.sum(direction * applied, axis=1)
            step_size = (norm_now / curve)[:, None]
            my_solution = my_solution + step_size * direction[:, :width]
            residual = residual - step_size * applied
            norm_next = jnp.sum(residual * residual, axis=1)
            ratio = (norm_next / norm_now)[:, None]
            my_image = my_image - step_size * my_next
            my_applied = my_image + ratio * my_applied
            direction = residual + ratio * direction
            norm_now = norm_next
        curve = add_up(jnp.sum(direction[:, :cols] * my_applied, axis=1), n, inner)
        step_size = (norm_now / curve)[:, None]
        my_solution = my_solution + step_size * direction[:, :width]
        return my_solution, residual[:, :width] - step_size * my_applied[:, :width]

    in_specs = (P("groups", "blk"), P("groups"), P(("groups", "blk")), P("groups", "blk"))
    out_specs = (P("groups", "blk"), P("groups", "blk"))
    return jax.shard_map(body, mesh=mesh, in_specs=in_specs, out_specs=out_specs, check_vma=False)
```

```python
import math

import jax
import jax.numpy as jnp
from jax import lax
from jax.experimental import pallas as pl
from jax.experimental.pallas import tpu as pltpu
from jax.sharding import PartitionSpec as P

ITERS = 4
TILE_BYTES = 16 << 20
VMEM_BYTES = 16 << 20
NORM_ROWS = 64
BUILD_ROWS = 256
POINT_SCALE = math.sqrt(math.log2(math.e))


def swap(x, n, stride):
    return lax.ppermute(x, "blk", [(i, i ^ stride) for i in range(n)])


def add_up(x, n, strides):
    for stride in strides:
        x = x + swap(x, n, stride)
    return x


def split(x, parts):
    out = []
    for _ in range(parts):
        high = lax.reduce_precision(x, 8, 7)
        out.append(high.astype(jnp.bfloat16))
        x = x - high
    return out


def halve(x):
    high = x.astype(jnp.bfloat16)
    return high, x - high.astype(jnp.float32)


def operands(pts):
    high, rest = halve(pts)
    mid, rest = halve(rest)
    low = rest.astype(jnp.bfloat16)
    norms = -0.5 * jnp.sum(pts * pts, axis=0, keepdims=True)
    row = lax.broadcasted_iota(jnp.int32, (NORM_ROWS, pts.shape[1]), 0)
    left = jnp.where((row >= 3) & (row < 6), 1.0, 0.0)
    right = jnp.where(row < 3, 1.0, 0.0)
    for k in range(3):
        part, norms = halve(norms)
        part = part.astype(jnp.float32)
        left = jnp.where(row == k, part, left)
        right = jnp.where(row == 3 + k, part, right)
    left = jnp.concatenate([high, high, mid, high, low, mid, left.astype(jnp.bfloat16)], axis=0)
    right = jnp.concatenate([high, mid, high, low, high, mid, right.astype(jnp.bfloat16)], axis=0)
    return left, right


def build_kernel(rows_ref, mine_ref, scale_ref, high_ref, low_ref, right_ref):
    right_ref[...] = operands(mine_ref[...] * scale_ref[...])[1]
    total, cols = high_ref.shape
    block, step = min(total, BUILD_ROWS), min(cols, 256)

    @pl.loop(0, total // block)
    def _(i):
        down = pl.ds(pl.multiple_of(i * block, block), block)
        left = jnp.transpose(operands(rows_ref[:, down] * scale_ref[...])[0])
        for at in range(0, cols, step):
            here = pl.ds(at, step)
            power = jnp.dot(left, right_ref[:, here], preferred_element_type=jnp.float32)
            high, rest = halve(jnp.exp2(power))
            high_ref[down, here] = high
            low_ref[down, here] = rest.astype(jnp.bfloat16)


def build_piece(rows, mine, scale):
    feats, total = rows.shape
    cols = mine.shape[1]
    out = jax.ShapeDtypeStruct((total, cols), jnp.bfloat16)
    whole = pl.BlockSpec(memory_space=pltpu.VMEM)
    return pl.pallas_call(
        build_kernel,
        out_shape=(out, out),
        in_specs=[whole] * 3,
        out_specs=(whole, whole),
        scratch_shapes=[pltpu.VMEM((6 * feats + NORM_ROWS, cols), jnp.bfloat16)],
        compiler_params=pltpu.CompilerParams(vmem_limit_bytes=VMEM_BYTES),
        cost_estimate=pl.CostEstimate(
            flops=2 * total * cols * 256, bytes_accessed=4 * total * (cols + feats), transcendentals=total * cols
        ),
    )(rows, mine, scale)


def apply_piece(vectors, piece):
    parts = split(vectors, 3)
    high = jnp.dot(jnp.concatenate(parts, axis=0), piece[0], preferred_element_type=jnp.float32)
    low = jnp.dot(jnp.concatenate(parts[:2], axis=0), piece[1], preferred_element_type=jnp.float32)
    return high, low


def solution(mesh):
    n = mesh.shape["blk"]
    strides = [1 << k for k in reversed(range(n.bit_length() - 1))]

    def body(points, lengthscale, noise_var, targets):
        feats, width = points.shape
        probes = targets.shape[0]
        team = min(n, 4)
        while team < n and (n * width) * (n * width) // team * 4 > TILE_BYTES:
            team *= 2
        outer, inner = [s for s in strides if s >= team], [s for s in strides if s < team]

        def arrivals(x):
            pieces = [x]
            for stride in inner:
                pieces.append(swap(jnp.concatenate(pieces, axis=1), n, stride))
            return pieces

        mine = lax.optimization_barrier(jnp.concatenate([points, targets, noise_var[None, :]], axis=0))
        for stride in outer:
            mine = jnp.concatenate([mine, swap(mine, n, stride)], axis=1)
        noise = mine[-1:]
        scale = (POINT_SCALE / lengthscale)[:, None]
        first = arrivals(mine[:-1])
        tile = [build_piece(x[:feats], mine[:feats], scale) for x in first]

        def operator(pieces):
            high, low = apply_piece(pieces[0], tile[0])
            for x, piece in zip(pieces[1:], tile[1:]):
                terms = apply_piece(x, piece)
                high, low = lax.optimization_barrier((high + terms[0], low + terms[1]))
            corrections = (high[probes : 2 * probes] + low[:probes]) + (high[2 * probes :] + low[probes:])
            return high[:probes] + corrections + noise * pieces[0]

        starts = [x[feats:] for x in first]
        residual = direction = jnp.concatenate(starts, axis=1)
        cols = noise.shape[1]
        my_solution = jnp.zeros_like(direction[:, :width])
        norm_now = jnp.sum(residual * residual, axis=1)
        my_applied = my_image = operator(starts)
        for iteration in range(ITERS - 1):
            pieces = arrivals(my_applied)
            my_next = operator(pieces)
            applied = jnp.concatenate(pieces, axis=1)
            curve = jnp.sum(direction * applied, axis=1)
            step_size = (norm_now / curve)[:, None]
            my_solution = my_solution + step_size * direction[:, :width]
            residual = residual - step_size * applied
            norm_next = jnp.sum(residual * residual, axis=1)
            ratio = (norm_next / norm_now)[:, None]
            my_image = my_image - step_size * my_next
            my_applied = my_image + ratio * my_applied
            direction = residual + ratio * direction
            norm_now = norm_next
        curve = add_up(jnp.sum(direction[:, :cols] * my_applied, axis=1), n, inner)
        step_size = (norm_now / curve)[:, None]
        my_solution = my_solution + step_size * direction[:, :width]
        return my_solution, residual[:, :width] - step_size * my_applied[:, :width]

    in_specs = (P("groups", "blk"), P("groups"), P(("groups", "blk")), P("groups", "blk"))
    out_specs = (P("groups", "blk"), P("groups", "blk"))
    return jax.shard_map(body, mesh=mesh, in_specs=in_specs, out_specs=out_specs, check_vma=False)
```

```python
import math

import jax
import jax.numpy as jnp
from jax import lax
from jax.experimental import pallas as pl
from jax.experimental.pallas import tpu as pltpu
from jax.sharding import PartitionSpec as P

ITERS = 4
TILE_BYTES = 16 << 20
VMEM_BYTES = 16 << 20
NORM_ROWS = 64
BUILD_ROWS = 1024
POINT_SCALE = math.sqrt(math.log2(math.e))


def swap(x, n, stride):
    return lax.ppermute(x, "blk", [(i, i ^ stride) for i in range(n)])


def add_up(x, n, strides):
    for stride in strides:
        x = x + swap(x, n, stride)
    return x


def split(x, parts):
    out = []
    for _ in range(parts):
        high = lax.reduce_precision(x, 8, 7)
        out.append(high.astype(jnp.bfloat16))
        x = x - high
    return out


def halve(x):
    high = x.astype(jnp.bfloat16)
    return high, x - high.astype(jnp.float32)


def operands(pts):
    high, rest = halve(pts)
    mid, rest = halve(rest)
    low = rest.astype(jnp.bfloat16)
    norms = -0.5 * jnp.sum(pts * pts, axis=0, keepdims=True)
    row = lax.broadcasted_iota(jnp.int32, (NORM_ROWS, pts.shape[1]), 0)
    left = jnp.where((row >= 3) & (row < 6), 1.0, 0.0)
    right = jnp.where(row < 3, 1.0, 0.0)
    for k in range(3):
        part, norms = halve(norms)
        part = part.astype(jnp.float32)
        left = jnp.where(row == k, part, left)
        right = jnp.where(row == 3 + k, part, right)
    left = jnp.concatenate([high, high, mid, high, low, mid, left.astype(jnp.bfloat16)], axis=0)
    right = jnp.concatenate([high, mid, high, low, high, mid, right.astype(jnp.bfloat16)], axis=0)
    return left, right


def scaled_operand_kernel(mine_ref, scale_ref, right_ref):
    right_ref[...] = operands(mine_ref[...] * scale_ref[...])[1]


def build_kernel(rows_ref, vectors_ref, scale_ref, right_ref, sum_ref, tile_ref, out_ref):
    total, cols = rows_ref.shape[1], right_ref.shape[1]
    probes = vectors_ref.shape[0]
    block, step = min(total, BUILD_ROWS), min(cols, 256)
    high, rest = halve(vectors_ref[...])
    mid, rest = halve(rest)
    twice = jnp.concatenate([high, mid], axis=0)
    thrice = jnp.concatenate([high, mid, rest.astype(jnp.bfloat16)], axis=0)
    for top in range(0, total, block):
        down = slice(top, top + block)
        left = jnp.transpose(operands(rows_ref[:, down] * scale_ref[...])[0])
        for at in range(0, cols, step):
            here = slice(at, at + step)
            power = jnp.dot(left, right_ref[:, here], preferred_element_type=jnp.float32)
            high, rest = halve(jnp.exp2(power))
            low = rest.astype(jnp.bfloat16)
            tile_ref[down, here] = high
            tile_ref[total + top : total + top + block, here] = low
            large = jnp.dot(thrice[:, down], high, preferred_element_type=jnp.float32)
            small = jnp.dot(twice[:, down], low, preferred_element_type=jnp.float32)
            term = large[:probes] + (
                (large[probes : 2 * probes] + small[:probes]) + (large[2 * probes :] + small[probes:])
            )
            before = sum_ref if top == 0 else out_ref
            out_ref[:, here] = before[:, here] + term


def call(kernel, outs, *args, **cost):
    whole = pl.BlockSpec(memory_space=pltpu.VMEM)
    return pl.pallas_call(
        kernel,
        out_shape=outs,
        in_specs=[whole] * len(args),
        out_specs=jax.tree.map(lambda _: whole, outs),
        compiler_params=pltpu.CompilerParams(vmem_limit_bytes=VMEM_BYTES),
        cost_estimate=pl.CostEstimate(**cost),
    )(*args)


def build_piece(rows, vectors, scale, right, total):
    count, cols = rows.shape[1], right.shape[1]
    outs = (jax.ShapeDtypeStruct((2 * count, cols), jnp.bfloat16), jax.ShapeDtypeStruct(total.shape, jnp.float32))
    cost = dict(flops=2 * count * cols * 416, bytes_accessed=4 * count * cols, transcendentals=count * cols)
    return call(build_kernel, outs, rows, vectors, scale, right, total, **cost)


def apply_piece(vectors, piece):
    high, mid, low = split(vectors, 3)
    left = jnp.concatenate([high, mid, low], axis=0)
    right = jnp.concatenate([high, mid, jnp.zeros_like(low)], axis=0)
    return jnp.dot(jnp.concatenate([left, right], axis=1), piece, preferred_element_type=jnp.float32)


def solution(mesh):
    n = mesh.shape["blk"]
    strides = [1 << k for k in reversed(range(n.bit_length() - 1))]

    def body(points, lengthscale, noise_var, targets):
        feats, width = points.shape
        probes = targets.shape[0]
        team = min(n, 4)
        while team < n and (n * width) * (n * width) // team * 4 > TILE_BYTES:
            team *= 2
        outer, inner = [s for s in strides if s >= team], [s for s in strides if s < team]

        def arrivals(x):
            pieces, sent = [x, swap(x, n, 1)], [x]
            for stride in inner[:-1]:
                came = swap(sent[0] if len(sent) == 1 else jnp.concatenate(sent, axis=1), n, stride)
                sent.append(came)
                pieces += [came, swap(came, n, 1)]
            return pieces

        mine = lax.optimization_barrier(jnp.concatenate([points, targets, noise_var[None, :]], axis=0))
        for stride in outer:
            mine = jnp.concatenate([mine, swap(mine, n, stride)], axis=1)
        noise = mine[-1:]
        scale = (POINT_SCALE / lengthscale)[:, None]
        first = arrivals(mine[:-1])
        cols = noise.shape[1]
        right = call(
            scaled_operand_kernel,
            jax.ShapeDtypeStruct((6 * feats + NORM_ROWS, cols), jnp.bfloat16),
            mine[:feats],
            scale,
            flops=feats * cols,
            bytes_accessed=feats * cols,
            transcendentals=0,
        )
        starts = [x[feats:] for x in first]
        tile = []
        my_applied = noise * starts[0]
        for x, start in zip(first, starts):
            piece, my_applied = build_piece(x[:feats], start, scale, right, my_applied)
            tile.append(piece)

        def operator(pieces):
            total = apply_piece(pieces[0], tile[0])
            for x, piece in zip(pieces[1:], tile[1:]):
                total = lax.optimization_barrier(total + apply_piece(x, piece))
            return total[:probes] + (total[probes : 2 * probes] + total[2 * probes :]) + noise * pieces[0]

        residual = direction = jnp.concatenate(starts, axis=1)
        my_solution = jnp.zeros_like(direction[:, :width])
        norm_now = jnp.sum(residual * residual, axis=1)
        my_image = my_applied
        for iteration in range(ITERS - 1):
            pieces = arrivals(my_applied)
            my_next = operator(pieces)
            applied = jnp.concatenate(pieces, axis=1)
            curve = jnp.sum(direction * applied, axis=1)
            step_size = (norm_now / curve)[:, None]
            my_solution = my_solution + step_size * direction[:, :width]
            residual = residual - step_size * applied
            norm_next = jnp.sum(residual * residual, axis=1)
            ratio = (norm_next / norm_now)[:, None]
            my_image = my_image - step_size * my_next
            my_applied = my_image + ratio * my_applied
            direction = residual + ratio * direction
            norm_now = norm_next
        curve = add_up(jnp.sum(direction[:, :cols] * my_applied, axis=1), n, inner)
        step_size = (norm_now / curve)[:, None]
        my_solution = my_solution + step_size * direction[:, :width]
        return my_solution, residual[:, :width] - step_size * my_applied[:, :width]

    in_specs = (P("groups", "blk"), P("groups"), P(("groups", "blk")), P("groups", "blk"))
    out_specs = (P("groups", "blk"), P("groups", "blk"))
    return jax.shard_map(body, mesh=mesh, in_specs=in_specs, out_specs=out_specs, check_vma=False)
```

```python
import functools
import math

import jax
import jax.numpy as jnp
from jax import lax
from jax.experimental import pallas as pl
from jax.experimental.pallas import tpu as pltpu
from jax.sharding import PartitionSpec as P

ITERS = 4
TILE_BYTES = 16 << 20
VMEM_BYTES = 16 << 20
NORM_ROWS = 64
BUILD_ROWS = 1024
PACE = 10**9
POINT_SCALE = math.sqrt(math.log2(math.e))


def swap(x, n, stride):
    return lax.ppermute(x, "blk", [(i, i ^ stride) for i in range(n)])


def add_up(x, n, strides):
    for stride in strides:
        x = x + swap(x, n, stride)
    return x


def split(x, parts):
    out = []
    for _ in range(parts):
        high = lax.reduce_precision(x, 8, 7)
        out.append(high.astype(jnp.bfloat16))
        x = x - high
    return out


def halve(x):
    high = x.astype(jnp.bfloat16)
    return high, x - high.astype(jnp.float32)


def operands(pts):
    high, rest = halve(pts)
    mid, rest = halve(rest)
    low = rest.astype(jnp.bfloat16)
    norms = -0.5 * jnp.sum(pts * pts, axis=0, keepdims=True)
    row = lax.broadcasted_iota(jnp.int32, (NORM_ROWS, pts.shape[1]), 0)
    left = jnp.where((row >= 3) & (row < 6), 1.0, 0.0)
    right = jnp.where(row < 3, 1.0, 0.0)
    for k in range(3):
        part, norms = halve(norms)
        part = part.astype(jnp.float32)
        left = jnp.where(row == k, part, left)
        right = jnp.where(row == 3 + k, part, right)
    left = jnp.concatenate([high, high, mid, high, low, mid, left.astype(jnp.bfloat16)], axis=0)
    right = jnp.concatenate([high, mid, high, low, high, mid, right.astype(jnp.bfloat16)], axis=0)
    return left, right


def prepare_kernel(part_ref, scale_ref, right_ref, part_out_ref):
    feats = scale_ref.shape[0]
    right_ref[...] = operands(part_ref[:feats] * scale_ref[...])[1]
    part_out_ref[...] = part_ref[:-1]


def build_kernel(top, size, rows_ref, vectors_ref, scale_ref, right_ref, sum_ref, *refs):
    tile_ref, out_ref = refs[-2:]
    count, cols = rows_ref.shape[1], right_ref.shape[1]
    probes = vectors_ref.shape[0]
    block, step = min(count, BUILD_ROWS), min(cols, 256)
    high, rest = halve(vectors_ref[...])
    mid, rest = halve(rest)
    twice = jnp.concatenate([high, mid], axis=0)
    thrice = jnp.concatenate([high, mid, rest.astype(jnp.bfloat16)], axis=0)
    for start in range(0, count, block):
        down = slice(start, start + block)
        left = jnp.transpose(operands(rows_ref[:, down] * scale_ref[...])[0])
        for at in range(0, cols, step):
            here = slice(at, at + step)
            power = jnp.dot(left, right_ref[:, here], preferred_element_type=jnp.float32)
            high, rest = halve(jnp.exp2(power))
            low = rest.astype(jnp.bfloat16)
            tile_ref[top + start : top + start + block, here] = high
            tile_ref[size + top + start : size + top + start + block, here] = low
            large = jnp.dot(thrice[:, down], high, preferred_element_type=jnp.float32)
            small = jnp.dot(twice[:, down], low, preferred_element_type=jnp.float32)
            term = large[:probes] + (
                (large[probes : 2 * probes] + small[:probes]) + (large[2 * probes :] + small[probes:])
            )
            before = sum_ref if start == 0 else out_ref
            out_ref[:, here] = before[:, here] + term


def call(kernel, outs, *args, aliases={}, **cost):
    whole = pl.BlockSpec(memory_space=pltpu.VMEM)
    return pl.pallas_call(
        kernel,
        out_shape=outs,
        in_specs=[whole] * len(args),
        out_specs=jax.tree.map(lambda _: whole, outs),
        input_output_aliases=aliases,
        compiler_params=pltpu.CompilerParams(vmem_limit_bytes=VMEM_BYTES),
        cost_estimate=pl.CostEstimate(**cost),
    )(*args)


def prepare(part, scale):
    feats, cols = scale.shape[0], part.shape[1]
    outs = (
        jax.ShapeDtypeStruct((6 * feats + NORM_ROWS, cols), jnp.bfloat16),
        jax.ShapeDtypeStruct((part.shape[0] - 1, cols), jnp.float32),
    )
    return call(prepare_kernel, outs, part, scale, flops=PACE, bytes_accessed=feats * cols, transcendentals=0)


def build_piece(rows, vectors, scale, right, total, size, top=0, piece=None):
    count, cols = rows.shape[1], right.shape[1]
    outs = (jax.ShapeDtypeStruct((2 * size, cols), jnp.bfloat16), jax.ShapeDtypeStruct(total.shape, jnp.float32))
    cost = dict(flops=PACE * count // 512, bytes_accessed=4 * count * cols, transcendentals=count * cols)
    args = (rows, vectors, scale, right, total)
    if piece is not None:
        args, cost["aliases"] = (*args, piece), {len(args): 0}
    return call(functools.partial(build_kernel, top, size), outs, *args, **cost)


def apply_piece(vectors, piece):
    high, mid, low = split(vectors, 3)
    left = jnp.concatenate([high, mid, low], axis=0)
    right = jnp.concatenate([high, mid, jnp.zeros_like(low)], axis=0)
    return jnp.dot(jnp.concatenate([left, right], axis=1), piece, preferred_element_type=jnp.float32)


def solution(mesh):
    n = mesh.shape["blk"]
    strides = [1 << k for k in reversed(range(n.bit_length() - 1))]

    def body(points, lengthscale, noise_var, targets):
        feats, width = points.shape
        probes = targets.shape[0]
        team = min(n, 4)
        while team < n and (n * width) * (n * width) // team * 4 > TILE_BYTES:
            team *= 2
        outer, inner = [s for s in strides if s >= team], [s for s in strides if s < team]

        def arrivals(x):
            pieces, sent = [x, swap(x, n, 1)], [x]
            for stride in inner[:-1]:
                came = swap(sent[0] if len(sent) == 1 else jnp.concatenate(sent, axis=1), n, stride)
                sent.append(came)
                pieces += [came, swap(came, n, 1)]
            return pieces

        scale = (POINT_SCALE / lengthscale)[:, None]
        parts = [lax.optimization_barrier(jnp.concatenate([points, targets, noise_var[None, :]], axis=0))]
        for stride in outer:
            parts.append(swap(jnp.concatenate(parts, axis=1), n, stride))
        noise = jnp.concatenate([x[-1:] for x in parts], axis=1)
        rights, parts = zip(*[prepare(x, scale) for x in parts])
        right, mine = jnp.concatenate(rights, axis=1), jnp.concatenate(parts, axis=1)
        cols = noise.shape[1]
        my_applied = noise * mine[feats:]

        def build(x, total, size, top=0, piece=None):
            return build_piece(x[:feats], x[feats:], scale, right, total, size, top, piece)

        if outer and len(inner) == 2:
            *came, last = lax.optimization_barrier((*[swap(x, n, inner[0]) for x in parts[:-1]], parts[-1]))
            late, early, half = swap(last, n, inner[0]), jnp.concatenate(came, axis=1), cols // 2
            across, early_across = swap(mine, n, 1), swap(early, n, 1)
            tile = []
            for x in (mine, across, early, early_across):
                piece, my_applied = build(x, my_applied, cols)
                tile.append(piece)
            late, my_applied = lax.optimization_barrier((late, my_applied))
            late_across = swap(late, n, 1)
            tile[2], my_applied = build(late, my_applied, cols, half, tile[2])
            tile[3], my_applied = build(late_across, my_applied, cols, half, tile[3])
            first = [mine, across, jnp.concatenate([early, late], axis=1), jnp.concatenate([early_across, late_across], axis=1)]
        else:
            first, tile = arrivals(mine), []
            for x in first:
                piece, my_applied = build(x, my_applied, x.shape[1])
                tile.append(piece)
        starts = [x[feats:] for x in first]

        def operator(pieces):
            total = apply_piece(pieces[0], tile[0])
            for x, piece in zip(pieces[1:], tile[1:]):
                total = lax.optimization_barrier(total + apply_piece(x, piece))
            return total[:probes] + (total[probes : 2 * probes] + total[2 * probes :]) + noise * pieces[0]

        residual = direction = jnp.concatenate(starts, axis=1)
        my_solution = jnp.zeros_like(direction[:, :width])
        norm_now = jnp.sum(residual * residual, axis=1)
        my_image = my_applied
        for iteration in range(ITERS - 1):
            pieces = arrivals(my_applied)
            my_next = operator(pieces)
            applied = jnp.concatenate(pieces, axis=1)
            curve = jnp.sum(direction * applied, axis=1)
            step_size = (norm_now / curve)[:, None]
            my_solution = my_solution + step_size * direction[:, :width]
            residual = residual - step_size * applied
            norm_next = jnp.sum(residual * residual, axis=1)
            ratio = (norm_next / norm_now)[:, None]
            my_image = my_image - step_size * my_next
            my_applied = my_image + ratio * my_applied
            direction = residual + ratio * direction
            norm_now = norm_next
        curve = add_up(jnp.sum(direction[:, :cols] * my_applied, axis=1), n, inner)
        step_size = (norm_now / curve)[:, None]
        my_solution = my_solution + step_size * direction[:, :width]
        return my_solution, residual[:, :width] - step_size * my_applied[:, :width]

    in_specs = (P("groups", "blk"), P("groups"), P(("groups", "blk")), P("groups", "blk"))
    out_specs = (P("groups", "blk"), P("groups", "blk"))
    return jax.shard_map(body, mesh=mesh, in_specs=in_specs, out_specs=out_specs, check_vma=False)
```

```python
import math

import jax
import jax.numpy as jnp
from jax import lax
from jax.experimental import pallas as pl
from jax.experimental.pallas import tpu as pltpu
from jax.sharding import PartitionSpec as P

ITERS = 4
TILE_BYTES = 32 << 20
VMEM_BYTES = 16 << 20
NORM_ROWS = 64
BUILD_ROWS = 1024
POINT_SCALE = math.sqrt(math.log2(math.e))


def swap(x, n, stride):
    return lax.ppermute(x, "blk", [(i, i ^ stride) for i in range(n)])


def add_up(x, n, strides):
    for stride in strides:
        x = x + swap(x, n, stride)
    return x


def split(x, parts):
    out = []
    for _ in range(parts):
        high = lax.reduce_precision(x, 8, 7)
        out.append(high.astype(jnp.bfloat16))
        x = x - high
    return out


def halve(x):
    high = x.astype(jnp.bfloat16)
    return high, x - high.astype(jnp.float32)


def operands(pts):
    high, rest = halve(pts)
    mid, rest = halve(rest)
    low = rest.astype(jnp.bfloat16)
    norms = -0.5 * jnp.sum(pts * pts, axis=0, keepdims=True)
    row = lax.broadcasted_iota(jnp.int32, (NORM_ROWS, pts.shape[1]), 0)
    left = jnp.where((row >= 3) & (row < 6), 1.0, 0.0)
    right = jnp.where(row < 3, 1.0, 0.0)
    for k in range(3):
        part, norms = halve(norms)
        part = part.astype(jnp.float32)
        left = jnp.where(row == k, part, left)
        right = jnp.where(row == 3 + k, part, right)
    left = jnp.concatenate([high, high, mid, high, low, mid, left.astype(jnp.bfloat16)], axis=0)
    right = jnp.concatenate([high, mid, high, low, high, mid, right.astype(jnp.bfloat16)], axis=0)
    return left, right


def scaled_operand_kernel(mine_ref, scale_ref, right_ref):
    right_ref[...] = operands(mine_ref[...] * scale_ref[...])[1]


def build_kernel(rows_ref, vectors_ref, scale_ref, right_ref, sum_ref, tile_ref, out_ref):
    total, cols = rows_ref.shape[1], right_ref.shape[1]
    probes = vectors_ref.shape[0]
    block, step = min(total, BUILD_ROWS), min(cols, 256)
    high, rest = halve(vectors_ref[...])
    mid, rest = halve(rest)
    twice = jnp.concatenate([high, mid], axis=0)
    thrice = jnp.concatenate([high, mid, rest.astype(jnp.bfloat16)], axis=0)
    for top in range(0, total, block):
        down = slice(top, top + block)
        left = jnp.transpose(operands(rows_ref[:, down] * scale_ref[...])[0])
        for at in range(0, cols, step):
            here = slice(at, at + step)
            power = jnp.dot(left, right_ref[:, here], preferred_element_type=jnp.float32)
            high, rest = halve(jnp.exp2(power))
            low = rest.astype(jnp.bfloat16)
            tile_ref[down, here] = high
            tile_ref[total + top : total + top + block, here] = low
            large = jnp.dot(thrice[:, down], high, preferred_element_type=jnp.float32)
            small = jnp.dot(twice[:, down], low, preferred_element_type=jnp.float32)
            term = large[:probes] + (
                (large[probes : 2 * probes] + small[:probes]) + (large[2 * probes :] + small[probes:])
            )
            before = sum_ref if top == 0 else out_ref
            out_ref[:, here] = before[:, here] + term


def call(kernel, outs, *args, **cost):
    whole = pl.BlockSpec(memory_space=pltpu.VMEM)
    return pl.pallas_call(
        kernel,
        out_shape=outs,
        in_specs=[whole] * len(args),
        out_specs=jax.tree.map(lambda _: whole, outs),
        compiler_params=pltpu.CompilerParams(vmem_limit_bytes=VMEM_BYTES),
        cost_estimate=pl.CostEstimate(**cost),
    )(*args)


def build_piece(rows, vectors, scale, right, total):
    count, cols = rows.shape[1], right.shape[1]
    outs = (jax.ShapeDtypeStruct((2 * count, cols), jnp.bfloat16), jax.ShapeDtypeStruct(total.shape, jnp.float32))
    cost = dict(flops=2 * count * cols * 416, bytes_accessed=4 * count * cols, transcendentals=count * cols)
    return call(build_kernel, outs, rows, vectors, scale, right, total, **cost)


def parts_of(vectors):
    return jnp.concatenate(split(vectors, 3), axis=0)


def apply_piece(parts, piece):
    probes = parts.shape[0] // 3
    right = jnp.where(lax.broadcasted_iota(jnp.int32, parts.shape, 0) < 2 * probes, parts, 0)
    return jnp.dot(jnp.concatenate([parts, right], axis=1), piece, preferred_element_type=jnp.float32)


def apply_transposed(parts, piece):
    both = lax.dot_general(parts, piece, (((1,), (1,)), ((), ())), preferred_element_type=jnp.float32)
    half = both.shape[1] // 2
    return both[:, :half] + both[:, half:]


def collect(total):
    probes = total.shape[0] // 3
    return total[:probes] + (total[probes : 2 * probes] + total[2 * probes :])


def solution(mesh):
    n = mesh.shape["blk"]
    strides = [1 << k for k in reversed(range(n.bit_length() - 1))]

    def body(points, lengthscale, noise_var, targets):
        feats, width = points.shape
        team = min(n, 2)
        while team < n and (n * width) * (n * width) // team * 4 > TILE_BYTES:
            team *= 2
        outer, inner = [s for s in strides if s >= team], [s for s in strides if s < team]

        def others(own):
            if len(inner) == 1:
                return [swap(x, n, 1) for x in own]
            sent = list(own)
            pieces = [swap(x, n, 1) for x in own]
            for stride in inner[:-1]:
                came = swap(sent[0] if len(sent) == 1 else jnp.concatenate(sent, axis=1), n, stride)
                sent.append(came)
                pieces += [came, swap(came, n, 1)]
            return pieces

        scale = (POINT_SCALE / lengthscale)[:, None]
        mine = lax.optimization_barrier(jnp.concatenate([points, targets, noise_var[None, :]], axis=0))
        for stride in outer[:-1]:
            mine = jnp.concatenate([mine, swap(mine, n, stride)], axis=1)
        groups = [mine] + [swap(mine, n, stride) for stride in outer[-1:]]
        noise = [x[-1:] for x in groups]
        own = [x[:-1] for x in groups]
        rest = others(own)
        rights = [
            call(
                scaled_operand_kernel,
                jax.ShapeDtypeStruct((6 * feats + NORM_ROWS, x.shape[1]), jnp.bfloat16),
                x[:feats],
                scale,
                flops=feats * x.shape[1],
                bytes_accessed=feats * x.shape[1],
                transcendentals=0,
            )
            for x in own
        ]
        my_applied = [a * x[feats:] for a, x in zip(noise, own)]
        tile = {}

        def build(rows, name, j):
            tile[name, j], my_applied[j] = build_piece(rows[:feats], rows[feats:], scale, rights[j], my_applied[j])

        build(own[0], 0, 0)
        build(rest[0], 2, 0)
        if len(own) == 2:
            build(own[1], 1, 0)
            my_applied[1] += collect(apply_transposed(parts_of(own[0][feats:]), tile[1, 0]))
            build(own[1], 1, 1)
            build(rest[0], 2, 1)
        for k in range(1, len(rest)):
            for j in range(len(own)):
                build(rest[k], 2 + k, j)

        def operator(own, rest):
            left = [parts_of(x) for x in own]
            totals = [apply_piece(left[0], tile[0, 0])]
            if len(own) == 2:
                totals[0] += apply_piece(left[1], tile[1, 0])
                totals.append(apply_transposed(left[0], tile[1, 0]) + apply_piece(left[1], tile[1, 1]))
            totals, rest = lax.optimization_barrier((totals, rest))
            for k, x in enumerate(rest):
                totals = lax.optimization_barrier(totals) if k else totals
                left = parts_of(x)
                totals = [total + apply_piece(left, tile[2 + k, j]) for j, total in enumerate(totals)]
            return [collect(total) + a * x for total, a, x in zip(totals, noise, own)], rest

        def whole(own, rest):
            return jnp.concatenate([*own, *rest], axis=1)

        residual = direction = whole(own, rest)[feats:]
        cols = sum(x.shape[1] for x in own)
        my_solution = jnp.zeros_like(direction[:, :width])
        norm_now = jnp.sum(residual * residual, axis=1)
        my_image = my_applied
        for iteration in range(ITERS - 1):
            my_next, came = operator(my_applied, others(my_applied))
            applied = whole(my_applied, came)
            curve = jnp.sum(direction * applied, axis=1)
            step_size = (norm_now / curve)[:, None]
            my_solution = my_solution + step_size * direction[:, :width]
            residual = residual - step_size * applied
            norm_next = jnp.sum(residual * residual, axis=1)
            ratio = (norm_next / norm_now)[:, None]
            my_image = [x - step_size * y for x, y in zip(my_image, my_next)]
            my_applied = [x + ratio * y for x, y in zip(my_image, my_applied)]
            direction = residual + ratio * direction
            norm_now = norm_next
        curve = add_up(jnp.sum(direction[:, :cols] * jnp.concatenate(my_applied, axis=1), axis=1), n, inner)
        step_size = (norm_now / curve)[:, None]
        my_solution = my_solution + step_size * direction[:, :width]
        return my_solution, residual[:, :width] - step_size * my_applied[0][:, :width]

    in_specs = (P("groups", "blk"), P("groups"), P(("groups", "blk")), P("groups", "blk"))
    out_specs = (P("groups", "blk"), P("groups", "blk"))
    return jax.shard_map(body, mesh=mesh, in_specs=in_specs, out_specs=out_specs, check_vma=False)
```

```python
import math

import jax
import jax.numpy as jnp
from jax import lax
from jax.experimental import pallas as pl
from jax.experimental.pallas import tpu as pltpu
from jax.sharding import PartitionSpec as P

ITERS = 4
TILE_BYTES = 16 << 20
VMEM_BYTES = 16 << 20
NORM_ROWS = 64
BUILD_ROWS = 1024
POINT_SCALE = math.sqrt(math.log2(math.e))


def swap(x, n, stride):
    return lax.ppermute(x, "blk", [(i, i ^ stride) for i in range(n)])


def add_up(x, n, strides):
    for stride in strides:
        x = x + swap(x, n, stride)
    return x


def split(x, parts):
    out = []
    for _ in range(parts):
        high = lax.reduce_precision(x, 8, 7)
        out.append(high.astype(jnp.bfloat16))
        x = x - high
    return out


def halve(x):
    high = x.astype(jnp.bfloat16)
    return high, x - high.astype(jnp.float32)


def operands(pts):
    high, rest = halve(pts)
    mid, rest = halve(rest)
    low = rest.astype(jnp.bfloat16)
    norms = -0.5 * jnp.sum(pts * pts, axis=0, keepdims=True)
    row = lax.broadcasted_iota(jnp.int32, (NORM_ROWS, pts.shape[1]), 0)
    left = jnp.where((row >= 3) & (row < 6), 1.0, 0.0)
    right = jnp.where(row < 3, 1.0, 0.0)
    for k in range(3):
        part, norms = halve(norms)
        part = part.astype(jnp.float32)
        left = jnp.where(row == k, part, left)
        right = jnp.where(row == 3 + k, part, right)
    left = jnp.concatenate([high, high, mid, high, low, mid, left.astype(jnp.bfloat16)], axis=0)
    right = jnp.concatenate([high, mid, high, low, high, mid, right.astype(jnp.bfloat16)], axis=0)
    return left, right


def prepare_kernel(part_ref, scale_ref, right_ref, copy_ref):
    feats = scale_ref.shape[0]
    right_ref[...] = operands(part_ref[:feats] * scale_ref[...])[1]
    copy_ref[...] = part_ref[...]


def build_kernel(rows_ref, vectors_ref, scale_ref, right_ref, sum_ref, tile_ref, out_ref):
    total, cols = rows_ref.shape[1], right_ref.shape[1]
    probes = vectors_ref.shape[0]
    block, step = min(total, BUILD_ROWS), min(cols, 256)
    high, rest = halve(vectors_ref[...])
    mid, rest = halve(rest)
    twice = jnp.concatenate([high, mid], axis=0)
    thrice = jnp.concatenate([high, mid, rest.astype(jnp.bfloat16)], axis=0)
    for top in range(0, total, block):
        down = slice(top, top + block)
        left = jnp.transpose(operands(rows_ref[:, down] * scale_ref[...])[0])
        for at in range(0, cols, step):
            here = slice(at, at + step)
            power = jnp.dot(left, right_ref[:, here], preferred_element_type=jnp.float32)
            high, rest = halve(jnp.exp2(power))
            low = rest.astype(jnp.bfloat16)
            tile_ref[down, here] = high
            tile_ref[total + top : total + top + block, here] = low
            large = jnp.dot(thrice[:, down], high, preferred_element_type=jnp.float32)
            small = jnp.dot(twice[:, down], low, preferred_element_type=jnp.float32)
            term = large[:probes] + (
                (large[probes : 2 * probes] + small[:probes]) + (large[2 * probes :] + small[probes:])
            )
            before = sum_ref if top == 0 else out_ref
            out_ref[:, here] = before[:, here] + term


def call(kernel, outs, *args, **cost):
    whole = pl.BlockSpec(memory_space=pltpu.VMEM)
    return pl.pallas_call(
        kernel,
        out_shape=outs,
        in_specs=[whole] * len(args),
        out_specs=jax.tree.map(lambda _: whole, outs),
        compiler_params=pltpu.CompilerParams(vmem_limit_bytes=VMEM_BYTES),
        cost_estimate=pl.CostEstimate(**cost),
    )(*args)


def prepare(part, scale):
    feats, cols = scale.shape[0], part.shape[1]
    outs = (jax.ShapeDtypeStruct((6 * feats + NORM_ROWS, cols), jnp.bfloat16), jax.ShapeDtypeStruct(part.shape, part.dtype))
    return call(prepare_kernel, outs, part, scale, flops=10**9, bytes_accessed=feats * cols, transcendentals=0)


def join(*xs):
    return jnp.concatenate(xs, axis=1)


def build_piece(rows, vectors, scale, right, total):
    count, cols = rows.shape[1], right.shape[1]
    outs = (jax.ShapeDtypeStruct((2 * count, cols), jnp.bfloat16), jax.ShapeDtypeStruct(total.shape, jnp.float32))
    cost = dict(flops=2 * count * cols * 416, bytes_accessed=4 * count * cols, transcendentals=count * cols)
    return call(build_kernel, outs, rows, vectors, scale, right, total, **cost)


def apply_piece(vectors, piece):
    high, mid, low = split(vectors, 3)
    left = jnp.concatenate([high, mid, low], axis=0)
    right = jnp.concatenate([high, mid, jnp.zeros_like(low)], axis=0)
    return jnp.dot(jnp.concatenate([left, right], axis=1), piece, preferred_element_type=jnp.float32)


def solution(mesh):
    n = mesh.shape["blk"]
    strides = [1 << k for k in reversed(range(n.bit_length() - 1))]

    def body(points, lengthscale, noise_var, targets):
        feats, width = points.shape
        probes = targets.shape[0]
        team = min(n, 4)
        while team < n and (n * width) * (n * width) // team * 4 > TILE_BYTES:
            team *= 2
        outer, inner = [s for s in strides if s >= team], [s for s in strides if s < team]

        def arrivals(x):
            pieces, sent = [x, swap(x, n, 1)], [x]
            for stride in inner[:-1]:
                came = swap(sent[0] if len(sent) == 1 else jnp.concatenate(sent, axis=1), n, stride)
                sent.append(came)
                pieces += [came, swap(came, n, 1)]
            return pieces

        scale = (POINT_SCALE / lengthscale)[:, None]
        block = lax.optimization_barrier(jnp.concatenate([points, targets, noise_var[None, :]], axis=0))
        fence = lax.optimization_barrier
        tile = []

        def build(x, total):
            piece, total = build_piece(x[:feats], x[feats:], scale, right, total)
            tile.append(piece)
            return total

        if len(outer) == 2 and len(inner) == 2:
            far, near, side = outer[0], outer[1], inner[0]
            by_far = swap(block, n, far)
            right_own, copy = prepare(block, scale)
            by_near = swap(copy, n, near)
            side_own = swap(copy[:-1], n, side)
            by_both = swap(by_far, n, near)
            right_far = prepare(by_far, scale)[0]
            last, side_own = fence((join(by_far, by_near, by_both)[:-1], side_own))
            side_last = swap(last, n, side)
            right = join(right_own, right_far, prepare(join(by_near, by_both), scale)[0])
            mine = join(block, by_far, by_near, by_both)
            noise, mine = mine[-1:], mine[:-1]
            early = side_own
            across, early_across = swap(mine, n, 1), swap(early, n, 1)
            my_applied = build(mine, noise * mine[feats:])
            my_applied = build(across, my_applied)
            side_last, my_applied = fence((side_last, my_applied))
            last_across = swap(side_last, n, 1)
            beside = join(early, side_last)
            my_applied = build(beside, my_applied)
            beside_across = join(early_across, last_across)
            my_applied = build(beside_across, my_applied)
            first = [mine, across, beside, beside_across]
        else:
            mine = block
            for stride in outer:
                mine = join(mine, swap(mine, n, stride))
            right, noise, first = prepare(mine, scale)[0], mine[-1:], arrivals(mine[:-1])
            my_applied = noise * first[0][feats:]
            for x in first:
                my_applied = build(x, my_applied)
        cols = noise.shape[1]
        starts = [x[feats:] for x in first]

        def operator(pieces):
            total = apply_piece(pieces[0], tile[0])
            for x, piece in zip(pieces[1:], tile[1:]):
                total = lax.optimization_barrier(total + apply_piece(x, piece))
            return total[:probes] + (total[probes : 2 * probes] + total[2 * probes :]) + noise * pieces[0]

        residual = direction = jnp.concatenate(starts, axis=1)
        my_solution = jnp.zeros_like(direction[:, :width])
        norm_now = jnp.sum(residual * residual, axis=1)
        my_image = my_applied
        for iteration in range(ITERS - 1):
            pieces = arrivals(my_applied)
            my_next = operator(pieces)
            applied = jnp.concatenate(pieces, axis=1)
            curve = jnp.sum(direction * applied, axis=1)
            step_size = (norm_now / curve)[:, None]
            my_solution = my_solution + step_size * direction[:, :width]
            residual = residual - step_size * applied
            norm_next = jnp.sum(residual * residual, axis=1)
            ratio = (norm_next / norm_now)[:, None]
            my_image = my_image - step_size * my_next
            my_applied = my_image + ratio * my_applied
            direction = residual + ratio * direction
            norm_now = norm_next
        curve = add_up(jnp.sum(direction[:, :cols] * my_applied, axis=1), n, inner)
        step_size = (norm_now / curve)[:, None]
        my_solution = my_solution + step_size * direction[:, :width]
        return my_solution, residual[:, :width] - step_size * my_applied[:, :width]

    in_specs = (P("groups", "blk"), P("groups"), P(("groups", "blk")), P("groups", "blk"))
    out_specs = (P("groups", "blk"), P("groups", "blk"))
    return jax.shard_map(body, mesh=mesh, in_specs=in_specs, out_specs=out_specs, check_vma=False)
```

```python
import math

import jax
import jax.numpy as jnp
from jax import lax
from jax.experimental import pallas as pl
from jax.experimental.pallas import tpu as pltpu
from jax.sharding import PartitionSpec as P

ITERS = 4
TILE_BYTES = 16 << 20
VMEM_BYTES = 16 << 20
NORM_ROWS = 64
BUILD_ROWS = 1024
POINT_SCALE = math.sqrt(math.log2(math.e))


def swap(x, n, stride):
    return lax.ppermute(x, "blk", [(i, i ^ stride) for i in range(n)])


def add_up(x, n, strides):
    for stride in strides:
        x = x + swap(x, n, stride)
    return x


def split(x, parts):
    out = []
    for _ in range(parts):
        high = lax.reduce_precision(x, 8, 7)
        out.append(high.astype(jnp.bfloat16))
        x = x - high
    return out


def halve(x):
    high = x.astype(jnp.bfloat16)
    return high, x - high.astype(jnp.float32)


def operands(pts):
    high, rest = halve(pts)
    mid, rest = halve(rest)
    low = rest.astype(jnp.bfloat16)
    norms = -0.5 * jnp.sum(pts * pts, axis=0, keepdims=True)
    row = lax.broadcasted_iota(jnp.int32, (NORM_ROWS, pts.shape[1]), 0)
    left = jnp.where((row >= 3) & (row < 6), 1.0, 0.0)
    right = jnp.where(row < 3, 1.0, 0.0)
    for k in range(3):
        part, norms = halve(norms)
        part = part.astype(jnp.float32)
        left = jnp.where(row == k, part, left)
        right = jnp.where(row == 3 + k, part, right)
    left = jnp.concatenate([high, high, mid, high, low, mid, left.astype(jnp.bfloat16)], axis=0)
    right = jnp.concatenate([high, mid, high, low, high, mid, right.astype(jnp.bfloat16)], axis=0)
    return left, right


def scaled_operand_kernel(mine_ref, scale_ref, right_ref):
    right_ref[...] = operands(mine_ref[...] * scale_ref[...])[1]


def build_kernel(rows_ref, vectors_ref, scale_ref, right_ref, sum_ref, tile_ref, out_ref):
    total, cols = rows_ref.shape[1], right_ref.shape[1]
    probes = vectors_ref.shape[0]
    block, step = min(total, BUILD_ROWS), min(cols, 256)
    high, rest = halve(vectors_ref[...])
    mid, rest = halve(rest)
    twice = jnp.concatenate([high, mid], axis=0)
    thrice = jnp.concatenate([high, mid, rest.astype(jnp.bfloat16)], axis=0)
    steps = [(top, at) for top in range(0, total, block) for at in range(0, cols, step)]
    lefts, powers, parts = {}, {}, {}

    def contract(top, at):
        if top not in lefts:
            lefts[top] = jnp.transpose(operands(rows_ref[:, top : top + block] * scale_ref[...])[0])
        powers[top, at] = jnp.dot(lefts[top], right_ref[:, at : at + step], preferred_element_type=jnp.float32)

    def raise_power(top, at):
        high, rest = halve(jnp.exp2(powers.pop((top, at))))
        low = rest.astype(jnp.bfloat16)
        tile_ref[top : top + block, at : at + step] = high
        tile_ref[total + top : total + top + block, at : at + step] = low
        parts[top, at] = high, low

    def apply(top, at):
        down, here = slice(top, top + block), slice(at, at + step)
        high, low = parts.pop((top, at))
        large = jnp.dot(thrice[:, down], high, preferred_element_type=jnp.float32)
        small = jnp.dot(twice[:, down], low, preferred_element_type=jnp.float32)
        term = large[:probes] + ((large[probes : 2 * probes] + small[:probes]) + (large[2 * probes :] + small[probes:]))
        before = sum_ref if top == 0 else out_ref
        out_ref[:, here] = before[:, here] + term

    contract(*steps[0])
    for k, chunk in enumerate(steps):
        if k + 1 < len(steps):
            contract(*steps[k + 1])
        raise_power(*chunk)
        if k:
            apply(*steps[k - 1])
    apply(*steps[-1])


def call(kernel, outs, *args, **cost):
    whole = pl.BlockSpec(memory_space=pltpu.VMEM)
    return pl.pallas_call(
        kernel,
        out_shape=outs,
        in_specs=[whole] * len(args),
        out_specs=jax.tree.map(lambda _: whole, outs),
        compiler_params=pltpu.CompilerParams(vmem_limit_bytes=VMEM_BYTES),
        cost_estimate=pl.CostEstimate(**cost),
    )(*args)


def build_piece(rows, vectors, scale, right, total):
    count, cols = rows.shape[1], right.shape[1]
    outs = (jax.ShapeDtypeStruct((2 * count, cols), jnp.bfloat16), jax.ShapeDtypeStruct(total.shape, jnp.float32))
    cost = dict(flops=2 * count * cols * 416, bytes_accessed=4 * count * cols, transcendentals=count * cols)
    return call(build_kernel, outs, rows, vectors, scale, right, total, **cost)


def apply_piece(vectors, piece):
    high, mid, low = split(vectors, 3)
    left = jnp.concatenate([high, mid, low], axis=0)
    right = jnp.concatenate([high, mid, jnp.zeros_like(low)], axis=0)
    return jnp.dot(jnp.concatenate([left, right], axis=1), piece, preferred_element_type=jnp.float32)


def solution(mesh):
    n = mesh.shape["blk"]
    strides = [1 << k for k in reversed(range(n.bit_length() - 1))]

    def body(points, lengthscale, noise_var, targets):
        feats, width = points.shape
        probes = targets.shape[0]
        team = min(n, 4)
        while team < n and (n * width) * (n * width) // team * 4 > TILE_BYTES:
            team *= 2
        outer, inner = [s for s in strides if s >= team], [s for s in strides if s < team]

        def arrivals(x):
            pieces, sent = [x, swap(x, n, 1)], [x]
            for stride in inner[:-1]:
                came = swap(sent[0] if len(sent) == 1 else jnp.concatenate(sent, axis=1), n, stride)
                sent.append(came)
                pieces += [came, swap(came, n, 1)]
            return pieces

        mine = lax.optimization_barrier(jnp.concatenate([points, targets, noise_var[None, :]], axis=0))
        for stride in outer:
            mine = jnp.concatenate([mine, swap(mine, n, stride)], axis=1)
        noise = mine[-1:]
        scale = (POINT_SCALE / lengthscale)[:, None]
        first = arrivals(mine[:-1])
        cols = noise.shape[1]
        right = call(
            scaled_operand_kernel,
            jax.ShapeDtypeStruct((6 * feats + NORM_ROWS, cols), jnp.bfloat16),
            mine[:feats],
            scale,
            flops=feats * cols,
            bytes_accessed=feats * cols,
            transcendentals=0,
        )
        starts = [x[feats:] for x in first]
        tile = []
        my_applied = noise * starts[0]
        for x, start in zip(first, starts):
            piece, my_applied = build_piece(x[:feats], start, scale, right, my_applied)
            tile.append(piece)

        def operator(pieces):
            total = apply_piece(pieces[0], tile[0])
            for x, piece in zip(pieces[1:], tile[1:]):
                total = lax.optimization_barrier(total + apply_piece(x, piece))
            return total[:probes] + (total[probes : 2 * probes] + total[2 * probes :]) + noise * pieces[0]

        residual = direction = jnp.concatenate(starts, axis=1)
        my_solution = jnp.zeros_like(direction[:, :width])
        norm_now = jnp.sum(residual * residual, axis=1)
        my_image = my_applied
        for iteration in range(ITERS - 1):
            pieces = arrivals(my_applied)
            my_next = operator(pieces)
            applied = jnp.concatenate(pieces, axis=1)
            curve = jnp.sum(direction * applied, axis=1)
            step_size = (norm_now / curve)[:, None]
            my_solution = my_solution + step_size * direction[:, :width]
            residual = residual - step_size * applied
            norm_next = jnp.sum(residual * residual, axis=1)
            ratio = (norm_next / norm_now)[:, None]
            my_image = my_image - step_size * my_next
            my_applied = my_image + ratio * my_applied
            direction = residual + ratio * direction
            norm_now = norm_next
        curve = add_up(jnp.sum(direction[:, :cols] * my_applied, axis=1), n, inner)
        step_size = (norm_now / curve)[:, None]
        my_solution = my_solution + step_size * direction[:, :width]
        return my_solution, residual[:, :width] - step_size * my_applied[:, :width]

    in_specs = (P("groups", "blk"), P("groups"), P(("groups", "blk")), P("groups", "blk"))
    out_specs = (P("groups", "blk"), P("groups", "blk"))
    return jax.shard_map(body, mesh=mesh, in_specs=in_specs, out_specs=out_specs, check_vma=False)
```

```python
import functools
import math

import jax
import jax.numpy as jnp
from jax import lax
from jax.experimental import pallas as pl
from jax.experimental.pallas import tpu as pltpu
from jax.sharding import PartitionSpec as P

ITERS = 4
TILE_BYTES = 16 << 20
VMEM_BYTES = 16 << 20
NORM_ROWS = 64
BUILD_ROWS = 1024
POINT_SCALE = math.sqrt(math.log2(math.e))


def swap(x, n, stride):
    return lax.ppermute(x, "blk", [(i, i ^ stride) for i in range(n)])


def add_up(x, n, strides):
    for stride in strides:
        x = x + swap(x, n, stride)
    return x


def split(x, parts):
    out = []
    for _ in range(parts):
        high = lax.reduce_precision(x, 8, 7)
        out.append(high.astype(jnp.bfloat16))
        x = x - high
    return out


def halve(x):
    high = x.astype(jnp.bfloat16)
    return high, x - high.astype(jnp.float32)


def operands(pts):
    high, rest = halve(pts)
    mid, rest = halve(rest)
    low = rest.astype(jnp.bfloat16)
    norms = -0.5 * jnp.sum(pts * pts, axis=0, keepdims=True)
    row = lax.broadcasted_iota(jnp.int32, (NORM_ROWS, pts.shape[1]), 0)
    left = jnp.where((row >= 3) & (row < 6), 1.0, 0.0)
    right = jnp.where(row < 3, 1.0, 0.0)
    for k in range(3):
        part, norms = halve(norms)
        part = part.astype(jnp.float32)
        left = jnp.where(row == k, part, left)
        right = jnp.where(row == 3 + k, part, right)
    left = jnp.concatenate([high, high, mid, high, low, mid, left.astype(jnp.bfloat16)], axis=0)
    right = jnp.concatenate([high, mid, high, low, high, mid, right.astype(jnp.bfloat16)], axis=0)
    return left, right


def scaled_operand_kernel(mine_ref, scale_ref, right_ref):
    right_ref[...] = operands(mine_ref[...] * scale_ref[...])[1]


def build_kernel(rows_ref, vectors_ref, scale_ref, right_ref, sum_ref, tile_ref, out_ref):
    total, cols = rows_ref.shape[1], right_ref.shape[1]
    probes = vectors_ref.shape[0]
    block, step = min(total, BUILD_ROWS), min(cols, 256)
    high, rest = halve(vectors_ref[...])
    mid, rest = halve(rest)
    twice = jnp.concatenate([high, mid], axis=0)
    thrice = jnp.concatenate([high, mid, rest.astype(jnp.bfloat16)], axis=0)
    steps = [(top, at) for top in range(0, total, block) for at in range(0, cols, step)]
    lefts, powers, parts = {}, {}, {}

    def contract(top, at):
        if top not in lefts:
            lefts[top] = jnp.transpose(operands(rows_ref[:, top : top + block] * scale_ref[...])[0])
        powers[top, at] = jnp.dot(lefts[top], right_ref[:, at : at + step], preferred_element_type=jnp.float32)

    def raise_power(top, at):
        high, rest = halve(jnp.exp2(powers.pop((top, at))))
        low = rest.astype(jnp.bfloat16)
        tile_ref[top : top + block, at : at + step] = high
        tile_ref[total + top : total + top + block, at : at + step] = low
        parts[top, at] = high, low

    def apply(top, at):
        down, here = slice(top, top + block), slice(at, at + step)
        high, low = parts.pop((top, at))
        large = jnp.dot(thrice[:, down], high, preferred_element_type=jnp.float32)
        small = jnp.dot(twice[:, down], low, preferred_element_type=jnp.float32)
        term = large[:probes] + ((large[probes : 2 * probes] + small[:probes]) + (large[2 * probes :] + small[probes:]))
        before = sum_ref if top == 0 else out_ref
        out_ref[:, here] = before[:, here] + term

    contract(*steps[0])
    for k, chunk in enumerate(steps):
        if k + 1 < len(steps):
            contract(*steps[k + 1])
        raise_power(*chunk)
        if k:
            apply(*steps[k - 1])
    apply(*steps[-1])


def call(kernel, outs, *args, **cost):
    whole = pl.BlockSpec(memory_space=pltpu.VMEM)
    return pl.pallas_call(
        kernel,
        out_shape=outs,
        in_specs=[whole] * len(args),
        out_specs=jax.tree.map(lambda _: whole, outs),
        compiler_params=pltpu.CompilerParams(vmem_limit_bytes=VMEM_BYTES),
        cost_estimate=pl.CostEstimate(**cost),
    )(*args)


def build_piece(rows, vectors, scale, right, total):
    count, cols = rows.shape[1], right.shape[1]
    outs = (jax.ShapeDtypeStruct((2 * count, cols), jnp.bfloat16), jax.ShapeDtypeStruct(total.shape, jnp.float32))
    cost = dict(flops=2 * count * cols * 416, bytes_accessed=4 * count * cols, transcendentals=count * cols)
    return call(build_kernel, outs, rows, vectors, scale, right, total, **cost)


def finish_kernel(count, last, *refs):
    came = refs[:count]
    tile_ref, sum_ref, noise_ref, norm_ref, residual_ref, direction_ref, image_ref, solution_ref = refs[count : count + 8]
    new_norm, new_residual, new_direction, new_solution, new_applied, extra = refs[count + 8 :]
    probes, cols = image_ref.shape
    width, size, step = solution_ref.shape[1], came[-1].shape[1], min(cols, 256)

    high, rest = halve(came[-1][...])
    mid, rest = halve(rest)
    twice = jnp.concatenate([high, mid], axis=0)
    thrice = jnp.concatenate([high, mid, rest.astype(jnp.bfloat16)], axis=0)
    terms = []
    for at in range(0, cols, step):
        here = slice(at, at + step)
        large = sum_ref[:, here] + jnp.dot(thrice, tile_ref[:size, here], preferred_element_type=jnp.float32)
        small = jnp.dot(twice, tile_ref[size:, here], preferred_element_type=jnp.float32)
        terms.append(
            large[:probes] + ((large[probes : 2 * probes] + small[:probes]) + (large[2 * probes :] + small[probes:]))
        )

    def over(pieces):
        at = 0
        for ref in pieces:
            yield slice(at, at + ref.shape[1]), ref
            at += ref.shape[1]

    curve = sum(jnp.sum(direction_ref[:, here] * ref[...], axis=1, keepdims=True) for here, ref in over(came))
    norm = norm_ref[...]
    step_size = norm / curve
    for here, ref in over(came):
        new_residual[:, here] = residual_ref[:, here] - step_size * ref[...]
    norm_next = sum(jnp.sum(new_residual[:, here] * new_residual[:, here], axis=1, keepdims=True) for here, _ in over(came))
    new_norm[...] = norm_next
    ratio = norm_next / norm
    new_solution[...] = solution_ref[...] + step_size * direction_ref[:, :width]
    for here, _ in over(came):
        new_direction[:, here] = new_residual[:, here] + ratio * direction_ref[:, here]
    inner = jnp.zeros_like(norm)
    for at, term in zip(range(0, cols, step), terms):
        here = slice(at, at + step)
        mine = came[0][:, here]
        image = image_ref[:, here] - step_size * (term + noise_ref[:, here] * mine)
        applied = image + ratio * mine
        new_applied[:, here] = applied
        if last:
            inner += jnp.sum(new_direction[:, here] * applied, axis=1, keepdims=True)
        else:
            extra[:, here] = image
    if last:
        extra[...] = inner


def finish(last, came, tile, total, noise, norm, residual, direction, image, answer):
    outs = (norm, residual, direction, answer, image, norm if last else image)
    outs = tuple(jax.ShapeDtypeStruct(x.shape, jnp.float32) for x in outs)
    args = (*came, tile, total, noise, norm, residual, direction, image, answer)
    cost = dict(flops=2 * 96 * tile.size, bytes_accessed=2 * tile.size, transcendentals=0)
    return call(functools.partial(finish_kernel, len(came), last), outs, *args, **cost)


def apply_piece(vectors, piece):
    high, mid, low = split(vectors, 3)
    left = jnp.concatenate([high, mid, low], axis=0)
    right = jnp.concatenate([high, mid, jnp.zeros_like(low)], axis=0)
    return jnp.dot(jnp.concatenate([left, right], axis=1), piece, preferred_element_type=jnp.float32)


def solution(mesh):
    n = mesh.shape["blk"]
    strides = [1 << k for k in reversed(range(n.bit_length() - 1))]

    def body(points, lengthscale, noise_var, targets):
        feats, width = points.shape
        probes = targets.shape[0]
        team = min(n, 4)
        while team < n and (n * width) * (n * width) // team * 4 > TILE_BYTES:
            team *= 2
        outer, inner = [s for s in strides if s >= team], [s for s in strides if s < team]

        def arrivals(x):
            pieces, sent = [x, swap(x, n, 1)], [x]
            for stride in inner[:-1]:
                came = swap(sent[0] if len(sent) == 1 else jnp.concatenate(sent, axis=1), n, stride)
                sent.append(came)
                pieces += [came, swap(came, n, 1)]
            return pieces

        mine = lax.optimization_barrier(jnp.concatenate([points, targets, noise_var[None, :]], axis=0))
        for stride in outer:
            mine = jnp.concatenate([mine, swap(mine, n, stride)], axis=1)
        noise = mine[-1:]
        scale = (POINT_SCALE / lengthscale)[:, None]
        first = arrivals(mine[:-1])
        cols = noise.shape[1]
        right = call(
            scaled_operand_kernel,
            jax.ShapeDtypeStruct((6 * feats + NORM_ROWS, cols), jnp.bfloat16),
            mine[:feats],
            scale,
            flops=feats * cols,
            bytes_accessed=feats * cols,
            transcendentals=0,
        )
        starts = [x[feats:] for x in first]
        tile = []
        my_applied = noise * starts[0]
        for x, start in zip(first, starts):
            piece, my_applied = build_piece(x[:feats], start, scale, right, my_applied)
            tile.append(piece)

        def all_but_last(pieces):
            total = apply_piece(pieces[0], tile[0])
            for x, piece in zip(pieces[1:-1], tile[1:-1]):
                total = lax.optimization_barrier(total + apply_piece(x, piece))
            return total

        residual = direction = jnp.concatenate(starts, axis=1)
        my_solution = jnp.zeros_like(direction[:, :width])
        norm = jnp.sum(residual * residual, axis=1, keepdims=True)
        my_image = my_applied
        for iteration in range(ITERS - 1):
            came, last = arrivals(my_applied), iteration == ITERS - 2
            norm, residual, direction, my_solution, my_applied, extra = finish(
                last, came, tile[-1], all_but_last(came), noise, norm, residual, direction, my_image, my_solution
            )
            my_image = extra
        step_size = norm / add_up(extra, n, inner)
        my_solution = my_solution + step_size * direction[:, :width]
        return my_solution, residual[:, :width] - step_size * my_applied[:, :width]

    in_specs = (P("groups", "blk"), P("groups"), P(("groups", "blk")), P("groups", "blk"))
    out_specs = (P("groups", "blk"), P("groups", "blk"))
    return jax.shard_map(body, mesh=mesh, in_specs=in_specs, out_specs=out_specs, check_vma=False)
```

```python
import functools
import math

import jax
import jax.numpy as jnp
from jax import lax
from jax.experimental import pallas as pl
from jax.experimental.pallas import tpu as pltpu
from jax.sharding import PartitionSpec as P

ITERS = 4
TILE_BYTES = 16 << 20
VMEM_BYTES = 4 << 20
NORM_ROWS = 64
BUILD_ROWS = 1024
POINT_SCALE = math.sqrt(math.log2(math.e))


def swap(x, n, stride):
    return lax.ppermute(x, "blk", [(i, i ^ stride) for i in range(n)])


def add_up(x, n, strides):
    for stride in strides:
        x = x + swap(x, n, stride)
    return x


def split(x, parts):
    out = []
    for _ in range(parts):
        high = lax.reduce_precision(x, 8, 7)
        out.append(high.astype(jnp.bfloat16))
        x = x - high
    return out


def halve(x):
    high = x.astype(jnp.bfloat16)
    return high, x - high.astype(jnp.float32)


def operands(pts):
    high, rest = halve(pts)
    mid, rest = halve(rest)
    low = rest.astype(jnp.bfloat16)
    norms = -0.5 * jnp.sum(pts * pts, axis=0, keepdims=True)
    row = lax.broadcasted_iota(jnp.int32, (NORM_ROWS, pts.shape[1]), 0)
    left = jnp.where((row >= 3) & (row < 6), 1.0, 0.0)
    right = jnp.where(row < 3, 1.0, 0.0)
    for k in range(3):
        part, norms = halve(norms)
        part = part.astype(jnp.float32)
        left = jnp.where(row == k, part, left)
        right = jnp.where(row == 3 + k, part, right)
    left = jnp.concatenate([high, high, mid, high, low, mid, left.astype(jnp.bfloat16)], axis=0)
    right = jnp.concatenate([high, mid, high, low, high, mid, right.astype(jnp.bfloat16)], axis=0)
    return left, right


def scaled_operand_kernel(mine_ref, scale_ref, right_ref):
    right_ref[...] = operands(mine_ref[...] * scale_ref[...])[1]


def build_kernel(rows_ref, vectors_ref, scale_ref, right_ref, sum_ref, tile_ref, out_ref):
    total, cols = rows_ref.shape[1], right_ref.shape[1]
    probes = vectors_ref.shape[0]
    block, step = min(total, BUILD_ROWS), min(cols, 256)
    high, rest = halve(vectors_ref[...])
    mid, rest = halve(rest)
    twice = jnp.concatenate([high, mid], axis=0)
    thrice = jnp.concatenate([high, mid, rest.astype(jnp.bfloat16)], axis=0)
    steps = [(top, at) for top in range(0, total, block) for at in range(0, cols, step)]
    lefts, powers, parts = {}, {}, {}

    def contract(top, at):
        if top not in lefts:
            lefts[top] = jnp.transpose(operands(rows_ref[:, top : top + block] * scale_ref[...])[0])
        powers[top, at] = jnp.dot(lefts[top], right_ref[:, at : at + step], preferred_element_type=jnp.float32)

    def raise_power(top, at):
        high, rest = halve(jnp.exp2(powers.pop((top, at))))
        low = rest.astype(jnp.bfloat16)
        tile_ref[top : top + block, at : at + step] = high
        tile_ref[total + top : total + top + block, at : at + step] = low
        parts[top, at] = high, low

    def apply(top, at):
        down, here = slice(top, top + block), slice(at, at + step)
        high, low = parts.pop((top, at))
        large = jnp.dot(thrice[:, down], high, preferred_element_type=jnp.float32)
        small = jnp.dot(twice[:, down], low, preferred_element_type=jnp.float32)
        term = large[:probes] + ((large[probes : 2 * probes] + small[:probes]) + (large[2 * probes :] + small[probes:]))
        before = sum_ref if top == 0 else out_ref
        out_ref[:, here] = before[:, here] + term

    contract(*steps[0])
    for k, chunk in enumerate(steps):
        if k + 1 < len(steps):
            contract(*steps[k + 1])
        raise_power(*chunk)
        if k:
            apply(*steps[k - 1])
    apply(*steps[-1])


def call(kernel, outs, *args, **cost):
    whole = pl.BlockSpec(memory_space=pltpu.VMEM)
    return pl.pallas_call(
        kernel,
        out_shape=outs,
        in_specs=[whole] * len(args),
        out_specs=jax.tree.map(lambda _: whole, outs),
        compiler_params=pltpu.CompilerParams(vmem_limit_bytes=VMEM_BYTES),
        cost_estimate=pl.CostEstimate(**cost),
    )(*args)


def build_piece(rows, vectors, scale, right, total):
    count, cols = rows.shape[1], right.shape[1]
    outs = (jax.ShapeDtypeStruct((2 * count, cols), jnp.bfloat16), jax.ShapeDtypeStruct(total.shape, jnp.float32))
    cost = dict(flops=2 * count * cols * 416, bytes_accessed=4 * count * cols, transcendentals=count * cols)
    return call(build_kernel, outs, rows, vectors, scale, right, total, **cost)


def finish_kernel(count, last, *refs):
    came = refs[:count]
    tile_ref, sum_ref, noise_ref, norm_ref, residual_ref, direction_ref, image_ref, solution_ref = refs[count : count + 8]
    new_norm, new_residual, new_direction, new_solution, new_applied, extra = refs[count + 8 :]
    probes, cols = image_ref.shape
    width, size, step = solution_ref.shape[1], came[-1].shape[1], min(cols, 256)

    high, rest = halve(came[-1][...])
    mid, rest = halve(rest)
    twice = jnp.concatenate([high, mid], axis=0)
    thrice = jnp.concatenate([high, mid, rest.astype(jnp.bfloat16)], axis=0)
    terms = []
    for at in range(0, cols, step):
        here = slice(at, at + step)
        large = sum_ref[:, here] + jnp.dot(thrice, tile_ref[:size, here], preferred_element_type=jnp.float32)
        small = jnp.dot(twice, tile_ref[size:, here], preferred_element_type=jnp.float32)
        terms.append(
            large[:probes] + ((large[probes : 2 * probes] + small[:probes]) + (large[2 * probes :] + small[probes:]))
        )

    def over(pieces):
        at = 0
        for ref in pieces:
            yield slice(at, at + ref.shape[1]), ref
            at += ref.shape[1]

    curve = sum(jnp.sum(direction_ref[:, here] * ref[...], axis=1, keepdims=True) for here, ref in over(came))
    norm = norm_ref[...]
    step_size = norm / curve
    for here, ref in over(came):
        new_residual[:, here] = residual_ref[:, here] - step_size * ref[...]
    norm_next = sum(jnp.sum(new_residual[:, here] * new_residual[:, here], axis=1, keepdims=True) for here, _ in over(came))
    new_norm[...] = norm_next
    ratio = norm_next / norm
    new_solution[...] = solution_ref[...] + step_size * direction_ref[:, :width]
    for here, _ in over(came):
        new_direction[:, here] = new_residual[:, here] + ratio * direction_ref[:, here]
    inner = jnp.zeros_like(norm)
    for at, term in zip(range(0, cols, step), terms):
        here = slice(at, at + step)
        mine = came[0][:, here]
        image = image_ref[:, here] - step_size * (term + noise_ref[:, here] * mine)
        applied = image + ratio * mine
        new_applied[:, here] = applied
        if last:
            inner += jnp.sum(new_direction[:, here] * applied, axis=1, keepdims=True)
        else:
            extra[:, here] = image
    if last:
        extra[...] = inner


def finish(last, came, tile, total, noise, norm, residual, direction, image, answer):
    outs = (norm, residual, direction, answer, image, norm if last else image)
    outs = tuple(jax.ShapeDtypeStruct(x.shape, jnp.float32) for x in outs)
    args = (*came, tile, total, noise, norm, residual, direction, image, answer)
    cost = dict(flops=2 * 96 * tile.size, bytes_accessed=2 * tile.size, transcendentals=0)
    return call(functools.partial(finish_kernel, len(came), last), outs, *args, **cost)


def apply_piece(vectors, piece):
    high, mid, low = split(vectors, 3)
    left = jnp.concatenate([high, mid, low], axis=0)
    right = jnp.concatenate([high, mid, jnp.zeros_like(low)], axis=0)
    return jnp.dot(jnp.concatenate([left, right], axis=1), piece, preferred_element_type=jnp.float32)


def solution(mesh):
    n = mesh.shape["blk"]
    strides = [1 << k for k in reversed(range(n.bit_length() - 1))]

    def body(points, lengthscale, noise_var, targets):
        feats, width = points.shape
        probes = targets.shape[0]
        team = min(n, 4)
        while team < n and (n * width) * (n * width) // team * 4 > TILE_BYTES:
            team *= 2
        outer, inner = [s for s in strides if s >= team], [s for s in strides if s < team]

        def arrivals(x):
            pieces, sent = [x, swap(x, n, 1)], [x]
            for stride in inner[:-1]:
                came = swap(sent[0] if len(sent) == 1 else jnp.concatenate(sent, axis=1), n, stride)
                sent.append(came)
                pieces += [came, swap(came, n, 1)]
            return pieces

        mine = lax.optimization_barrier(jnp.concatenate([points, targets, noise_var[None, :]], axis=0))
        for stride in outer:
            mine = jnp.concatenate([mine, swap(mine, n, stride)], axis=1)
        noise = mine[-1:]
        scale = (POINT_SCALE / lengthscale)[:, None]
        first = arrivals(mine[:-1])
        cols = noise.shape[1]
        right = call(
            scaled_operand_kernel,
            jax.ShapeDtypeStruct((6 * feats + NORM_ROWS, cols), jnp.bfloat16),
            mine[:feats],
            scale,
            flops=feats * cols,
            bytes_accessed=feats * cols,
            transcendentals=0,
        )
        starts = [x[feats:] for x in first]
        tile = []
        my_applied = noise * starts[0]
        for x, start in zip(first, starts):
            piece, my_applied = build_piece(x[:feats], start, scale, right, my_applied)
            tile.append(piece)

        def all_but_last(pieces):
            total = apply_piece(pieces[0], tile[0])
            for x, piece in zip(pieces[1:-1], tile[1:-1]):
                total = lax.optimization_barrier(total + apply_piece(x, piece))
            return total

        residual = direction = jnp.concatenate(starts, axis=1)
        my_solution = jnp.zeros_like(direction[:, :width])
        norm = jnp.sum(residual * residual, axis=1, keepdims=True)
        my_image = my_applied
        for iteration in range(ITERS - 1):
            came, last = arrivals(my_applied), iteration == ITERS - 2
            norm, residual, direction, my_solution, my_applied, extra = finish(
                last, came, tile[-1], all_but_last(came), noise, norm, residual, direction, my_image, my_solution
            )
            my_image = extra
        step_size = norm / add_up(extra, n, inner)
        my_solution = my_solution + step_size * direction[:, :width]
        return my_solution, residual[:, :width] - step_size * my_applied[:, :width]

    in_specs = (P("groups", "blk"), P("groups"), P(("groups", "blk")), P("groups", "blk"))
    out_specs = (P("groups", "blk"), P("groups", "blk"))
    return jax.shard_map(body, mesh=mesh, in_specs=in_specs, out_specs=out_specs, check_vma=False)
```

```python
import math

import jax
import jax.numpy as jnp
from jax import lax
from jax.experimental import pallas as pl
from jax.experimental.pallas import tpu as pltpu
from jax.sharding import PartitionSpec as P

ITERS = 4
TILE_BYTES = 16 << 20
VMEM_BYTES = 16 << 20
NORM_ROWS = 64
BUILD_ROWS = 1024
POINT_SCALE = math.sqrt(math.log2(math.e))


def swap(x, n, stride):
    return lax.ppermute(x, "blk", [(i, i ^ stride) for i in range(n)])


def add_up(x, n, strides):
    for stride in strides:
        x = x + swap(x, n, stride)
    return x


def split(x, parts):
    out = []
    for _ in range(parts):
        high = lax.reduce_precision(x, 8, 7)
        out.append(high.astype(jnp.bfloat16))
        x = x - high
    return out


def halve(x):
    high = x.astype(jnp.bfloat16)
    return high, x - high.astype(jnp.float32)


def operands(pts):
    high, rest = halve(pts)
    mid, rest = halve(rest)
    low = rest.astype(jnp.bfloat16)
    norms = -0.5 * jnp.sum(pts * pts, axis=0, keepdims=True)
    row = lax.broadcasted_iota(jnp.int32, (NORM_ROWS, pts.shape[1]), 0)
    left = jnp.where((row >= 3) & (row < 6), 1.0, 0.0)
    right = jnp.where(row < 3, 1.0, 0.0)
    for k in range(3):
        part, norms = halve(norms)
        part = part.astype(jnp.float32)
        left = jnp.where(row == k, part, left)
        right = jnp.where(row == 3 + k, part, right)
    left = jnp.concatenate([high, high, mid, high, low, mid, left.astype(jnp.bfloat16)], axis=0)
    right = jnp.concatenate([high, mid, high, low, high, mid, right.astype(jnp.bfloat16)], axis=0)
    return left, right


def prepare_kernel(part_ref, scale_ref, right_ref, *copy_ref):
    feats = scale_ref.shape[0]
    right_ref[...] = operands(part_ref[:feats] * scale_ref[...])[1]
    for ref in copy_ref:
        ref[...] = part_ref[:-1]


def build_kernel(rows_ref, vectors_ref, scale_ref, right_ref, sum_ref, tile_ref, out_ref):
    total, cols = rows_ref.shape[1], right_ref.shape[1]
    probes = vectors_ref.shape[0]
    block, step = min(total, BUILD_ROWS), min(cols, 256)
    high, rest = halve(vectors_ref[...])
    mid, rest = halve(rest)
    twice = jnp.concatenate([high, mid], axis=0)
    thrice = jnp.concatenate([high, mid, rest.astype(jnp.bfloat16)], axis=0)
    steps = [(top, at) for top in range(0, total, block) for at in range(0, cols, step)]
    lefts, powers, parts = {}, {}, {}

    def contract(top, at):
        if top not in lefts:
            lefts[top] = jnp.transpose(operands(rows_ref[:, top : top + block] * scale_ref[...])[0])
        powers[top, at] = jnp.dot(lefts[top], right_ref[:, at : at + step], preferred_element_type=jnp.float32)

    def raise_power(top, at):
        high, rest = halve(jnp.exp2(powers.pop((top, at))))
        low = rest.astype(jnp.bfloat16)
        tile_ref[top : top + block, at : at + step] = high
        tile_ref[total + top : total + top + block, at : at + step] = low
        parts[top, at] = high, low

    def apply(top, at):
        down, here = slice(top, top + block), slice(at, at + step)
        high, low = parts.pop((top, at))
        large = jnp.dot(thrice[:, down], high, preferred_element_type=jnp.float32)
        small = jnp.dot(twice[:, down], low, preferred_element_type=jnp.float32)
        term = large[:probes] + ((large[probes : 2 * probes] + small[:probes]) + (large[2 * probes :] + small[probes:]))
        before = sum_ref if top == 0 else out_ref
        out_ref[:, here] = before[:, here] + term

    contract(*steps[0])
    for k, chunk in enumerate(steps):
        if k + 1 < len(steps):
            contract(*steps[k + 1])
        raise_power(*chunk)
        if k:
            apply(*steps[k - 1])
    apply(*steps[-1])


def call(kernel, outs, *args, **cost):
    whole = pl.BlockSpec(memory_space=pltpu.VMEM)
    return pl.pallas_call(
        kernel,
        out_shape=outs,
        in_specs=[whole] * len(args),
        out_specs=jax.tree.map(lambda _: whole, outs),
        compiler_params=pltpu.CompilerParams(vmem_limit_bytes=VMEM_BYTES),
        cost_estimate=pl.CostEstimate(**cost),
    )(*args)


def prepare(part, scale, copy=False):
    feats, cols = scale.shape[0], part.shape[1]
    outs = (jax.ShapeDtypeStruct((6 * feats + NORM_ROWS, cols), jnp.bfloat16),)
    if copy:
        outs += (jax.ShapeDtypeStruct((part.shape[0] - 1, cols), part.dtype),)
    return call(prepare_kernel, outs, part, scale, flops=10**9, bytes_accessed=feats * cols, transcendentals=0)


def join(*xs):
    return jnp.concatenate(xs, axis=1)


def build_piece(rows, vectors, scale, right, total):
    count, cols = rows.shape[1], right.shape[1]
    outs = (jax.ShapeDtypeStruct((2 * count, cols), jnp.bfloat16), jax.ShapeDtypeStruct(total.shape, jnp.float32))
    cost = dict(flops=2 * count * cols * 416, bytes_accessed=4 * count * cols, transcendentals=count * cols)
    return call(build_kernel, outs, rows, vectors, scale, right, total, **cost)


def apply_piece(vectors, piece):
    high, mid, low = split(vectors, 3)
    left = jnp.concatenate([high, mid, low], axis=0)
    right = jnp.concatenate([high, mid, jnp.zeros_like(low)], axis=0)
    return jnp.dot(jnp.concatenate([left, right], axis=1), piece, preferred_element_type=jnp.float32)


def solution(mesh):
    n = mesh.shape["blk"]
    strides = [1 << k for k in reversed(range(n.bit_length() - 1))]

    def body(points, lengthscale, noise_var, targets):
        feats, width = points.shape
        probes = targets.shape[0]
        team = min(n, 4)
        while team < n and (n * width) * (n * width) // team * 4 > TILE_BYTES:
            team *= 2
        outer, inner = [s for s in strides if s >= team], [s for s in strides if s < team]

        def arrivals(x):
            pieces, sent = [x, swap(x, n, 1)], [x]
            for stride in inner[:-1]:
                came = swap(sent[0] if len(sent) == 1 else jnp.concatenate(sent, axis=1), n, stride)
                sent.append(came)
                pieces += [came, swap(came, n, 1)]
            return pieces

        scale = (POINT_SCALE / lengthscale)[:, None]
        block = lax.optimization_barrier(jnp.concatenate([points, targets, noise_var[None, :]], axis=0))
        fence = lax.optimization_barrier
        tile = []

        def build(x, total):
            piece, total = build_piece(x[:feats], x[feats:], scale, right, total)
            tile.append(piece)
            return total

        if len(outer) == 2 and len(inner) == 2:
            far, near, side = outer[0], outer[1], inner[0]
            by_far = swap(block, n, far)
            right_own, copy = prepare(block, scale, True)
            side_own = swap(copy, n, side)
            by_near = swap(join(block, by_far), n, near)
            right_far, copy = prepare(by_far, scale, True)
            side_far = swap(copy, n, side)
            last, side_own, side_far = fence((by_near[:-1], side_own, side_far))
            side_last = swap(last, n, side)
            right = join(right_own, right_far, *prepare(by_near, scale))
            mine = join(block, by_far, by_near)
            noise, mine = mine[-1:], mine[:-1]
            across = swap(mine, n, 1)
            my_applied = build(mine, noise * mine[feats:])
            side_own, side_far, my_applied = fence((side_own, side_far, my_applied))
            early = join(side_own, side_far)
            early_across = swap(early, n, 1)
            my_applied = build(across, my_applied)
            side_last, my_applied = fence((side_last, my_applied))
            last_across = swap(side_last, n, 1)
            beside = join(early, side_last)
            my_applied = build(beside, my_applied)
            early_across, last_across, my_applied = fence((early_across, last_across, my_applied))
            beside_across = join(early_across, last_across)
            my_applied = build(beside_across, my_applied)
            first = [mine, across, beside, beside_across]
        else:
            mine = block
            for stride in outer:
                mine = join(mine, swap(mine, n, stride))
            (right,), noise, first = prepare(mine, scale), mine[-1:], arrivals(mine[:-1])
            my_applied = noise * first[0][feats:]
            for x in first:
                my_applied = build(x, my_applied)
        cols = noise.shape[1]
        starts = [x[feats:] for x in first]

        def operator(pieces):
            total = apply_piece(pieces[0], tile[0])
            for x, piece in zip(pieces[1:], tile[1:]):
                total = lax.optimization_barrier(total + apply_piece(x, piece))
            return total[:probes] + (total[probes : 2 * probes] + total[2 * probes :]) + noise * pieces[0]

        residual = direction = jnp.concatenate(starts, axis=1)
        my_solution = jnp.zeros_like(direction[:, :width])
        norm_now = jnp.sum(residual * residual, axis=1)
        my_image = my_applied
        for iteration in range(ITERS - 1):
            pieces = arrivals(my_applied)
            my_next = operator(pieces)
            applied = jnp.concatenate(pieces, axis=1)
            curve = jnp.sum(direction * applied, axis=1)
            step_size = (norm_now / curve)[:, None]
            my_solution = my_solution + step_size * direction[:, :width]
            residual = residual - step_size * applied
            norm_next = jnp.sum(residual * residual, axis=1)
            ratio = (norm_next / norm_now)[:, None]
            my_image = my_image - step_size * my_next
            my_applied = my_image + ratio * my_applied
            direction = residual + ratio * direction
            norm_now = norm_next
        curve = add_up(jnp.sum(direction[:, :cols] * my_applied, axis=1), n, inner)
        step_size = (norm_now / curve)[:, None]
        my_solution = my_solution + step_size * direction[:, :width]
        return my_solution, residual[:, :width] - step_size * my_applied[:, :width]

    in_specs = (P("groups", "blk"), P("groups"), P(("groups", "blk")), P("groups", "blk"))
    out_specs = (P("groups", "blk"), P("groups", "blk"))
    return jax.shard_map(body, mesh=mesh, in_specs=in_specs, out_specs=out_specs, check_vma=False)
```

```python
import math

import jax
import jax.numpy as jnp
from jax import lax
from jax.experimental import pallas as pl
from jax.experimental.pallas import tpu as pltpu
from jax.sharding import PartitionSpec as P

ITERS = 4
TILE_BYTES = 16 << 20
VMEM_BYTES = 16 << 20
NORM_ROWS = 64
BUILD_ROWS = 1024
POINT_SCALE = math.sqrt(math.log2(math.e))


def swap(x, n, stride):
    return lax.ppermute(x, "blk", [(i, i ^ stride) for i in range(n)])


def add_up(x, n, strides):
    for stride in strides:
        x = x + swap(x, n, stride)
    return x


def split(x, parts):
    out = []
    for _ in range(parts):
        high = lax.reduce_precision(x, 8, 7)
        out.append(high.astype(jnp.bfloat16))
        x = x - high
    return out


def halve(x):
    high = x.astype(jnp.bfloat16)
    return high, x - high.astype(jnp.float32)


def operands(pts):
    high, rest = halve(pts)
    mid, rest = halve(rest)
    low = rest.astype(jnp.bfloat16)
    norms = -0.5 * jnp.sum(pts * pts, axis=0, keepdims=True)
    row = lax.broadcasted_iota(jnp.int32, (NORM_ROWS, pts.shape[1]), 0)
    left = jnp.where((row >= 3) & (row < 6), 1.0, 0.0)
    right = jnp.where(row < 3, 1.0, 0.0)
    for k in range(3):
        part, norms = halve(norms)
        part = part.astype(jnp.float32)
        left = jnp.where(row == k, part, left)
        right = jnp.where(row == 3 + k, part, right)
    left = jnp.concatenate([high, high, mid, high, low, mid, left.astype(jnp.bfloat16)], axis=0)
    right = jnp.concatenate([high, mid, high, low, high, mid, right.astype(jnp.bfloat16)], axis=0)
    return left, right


def prepare_kernel(part_ref, scale_ref, right_ref, *copy_ref):
    feats = scale_ref.shape[0]
    right_ref[...] = operands(part_ref[:feats] * scale_ref[...])[1]
    for ref in copy_ref:
        ref[...] = part_ref[:-1]


def build_kernel(rows_ref, vectors_ref, scale_ref, right_ref, sum_ref, tile_ref, out_ref):
    total, cols = rows_ref.shape[1], right_ref.shape[1]
    probes = vectors_ref.shape[0]
    block, step = min(total, BUILD_ROWS), min(cols, 256)
    high, rest = halve(vectors_ref[...])
    mid, rest = halve(rest)
    twice = jnp.concatenate([high, mid], axis=0)
    thrice = jnp.concatenate([high, mid, rest.astype(jnp.bfloat16)], axis=0)
    steps = [(top, at) for top in range(0, total, block) for at in range(0, cols, step)]
    lefts, powers, parts = {}, {}, {}

    def contract(top, at):
        if top not in lefts:
            lefts[top] = jnp.transpose(operands(rows_ref[:, top : top + block] * scale_ref[...])[0])
        powers[top, at] = jnp.dot(lefts[top], right_ref[:, at : at + step], preferred_element_type=jnp.float32)

    def raise_power(top, at):
        high, rest = halve(jnp.exp2(powers.pop((top, at))))
        low = rest.astype(jnp.bfloat16)
        tile_ref[top : top + block, at : at + step] = high
        tile_ref[total + top : total + top + block, at : at + step] = low
        parts[top, at] = high, low

    def apply(top, at):
        down, here = slice(top, top + block), slice(at, at + step)
        high, low = parts.pop((top, at))
        large = jnp.dot(thrice[:, down], high, preferred_element_type=jnp.float32)
        small = jnp.dot(twice[:, down], low, preferred_element_type=jnp.float32)
        term = large[:probes] + ((large[probes : 2 * probes] + small[:probes]) + (large[2 * probes :] + small[probes:]))
        before = sum_ref if top == 0 else out_ref
        out_ref[:, here] = before[:, here] + term

    contract(*steps[0])
    for k, chunk in enumerate(steps):
        if k + 1 < len(steps):
            contract(*steps[k + 1])
        raise_power(*chunk)
        if k:
            apply(*steps[k - 1])
    apply(*steps[-1])


def call(kernel, outs, *args, **cost):
    whole = pl.BlockSpec(memory_space=pltpu.VMEM)
    return pl.pallas_call(
        kernel,
        out_shape=outs,
        in_specs=[whole] * len(args),
        out_specs=jax.tree.map(lambda _: whole, outs),
        compiler_params=pltpu.CompilerParams(vmem_limit_bytes=VMEM_BYTES),
        cost_estimate=pl.CostEstimate(**cost),
    )(*args)


def prepare(part, scale, copy=False):
    feats, cols = scale.shape[0], part.shape[1]
    outs = (jax.ShapeDtypeStruct((6 * feats + NORM_ROWS, cols), jnp.bfloat16),)
    if copy:
        outs += (jax.ShapeDtypeStruct((part.shape[0] - 1, cols), part.dtype),)
    return call(prepare_kernel, outs, part, scale, flops=10**10, bytes_accessed=feats * cols, transcendentals=0)


def join(*xs):
    return jnp.concatenate(xs, axis=1)


def build_piece(rows, vectors, scale, right, total):
    count, cols = rows.shape[1], right.shape[1]
    outs = (jax.ShapeDtypeStruct((2 * count, cols), jnp.bfloat16), jax.ShapeDtypeStruct(total.shape, jnp.float32))
    cost = dict(flops=2 * count * cols * 416, bytes_accessed=4 * count * cols, transcendentals=count * cols)
    return call(build_kernel, outs, rows, vectors, scale, right, total, **cost)


def apply_piece(vectors, piece):
    high, mid, low = split(vectors, 3)
    left = jnp.concatenate([high, mid, low], axis=0)
    right = jnp.concatenate([high, mid, jnp.zeros_like(low)], axis=0)
    return jnp.dot(jnp.concatenate([left, right], axis=1), piece, preferred_element_type=jnp.float32)


def solution(mesh):
    n = mesh.shape["blk"]
    strides = [1 << k for k in reversed(range(n.bit_length() - 1))]

    def body(points, lengthscale, noise_var, targets):
        feats, width = points.shape
        probes = targets.shape[0]
        team = min(n, 4)
        while team < n and (n * width) * (n * width) // team * 4 > TILE_BYTES:
            team *= 2
        outer, inner = [s for s in strides if s >= team], [s for s in strides if s < team]

        def arrivals(x):
            pieces, sent = [join(x, swap(x, n, 1))], [x]
            for stride in inner[:-1]:
                sent.append(swap(join(*sent), n, stride))
                pieces += [sent[-1], swap(sent[-1], n, 1)]
            return pieces

        scale = (POINT_SCALE / lengthscale)[:, None]
        block = lax.optimization_barrier(jnp.concatenate([points, targets, noise_var[None, :]], axis=0))
        fence = lax.optimization_barrier
        tile = []

        def build(x, total):
            piece, total = build_piece(x[:feats], x[feats:], scale, right, total)
            tile.append(piece)
            return total

        if len(outer) == 2 and len(inner) == 2:
            far, near, side = outer[0], outer[1], inner[0]
            by_far = swap(block, n, far)
            right_own, copy = prepare(block, scale, True)
            side_own = swap(copy, n, side)
            by_near = swap(join(block, by_far), n, near)
            right_far, copy = prepare(by_far, scale, True)
            side_far = swap(copy, n, side)
            last, side_own, side_far = fence((by_near[:-1], side_own, side_far))
            side_last = swap(last, n, side)
            right = join(right_own, right_far, *prepare(by_near, scale))
            mine = join(block, by_far, by_near)
            noise, mine = mine[-1:], mine[:-1]
            pair = join(mine, swap(mine, n, 1))
            my_applied = build(pair, noise * mine[feats:])
            side_last, my_applied = fence((side_last, my_applied))
            beside = join(side_own, side_far, side_last)
            beside_across = swap(beside, n, 1)
            my_applied = build(beside, my_applied)
            my_applied = build(beside_across, my_applied)
            first = [pair, beside, beside_across]
        else:
            mine = block
            for stride in outer:
                mine = join(mine, swap(mine, n, stride))
            (right,), noise, first = prepare(mine, scale), mine[-1:], arrivals(mine[:-1])
            my_applied = noise * mine[feats:-1]
            for x in first:
                my_applied = build(x, my_applied)
        cols = noise.shape[1]
        starts = [x[feats:] for x in first]

        def exchange(x, turn):
            raw, pieces, total = [x], [], None

            def add(k, piece):
                nonlocal total
                if k:
                    piece, total = fence((piece, total))
                pieces.append(turn(k, piece))
                term = apply_piece(pieces[-1], tile[k])
                total = term if total is None else total + term
                return piece

            came = [swap(x, n, stride) for stride in inner[:1] if stride > 1]
            beside = swap(x, n, 1)
            add(0, join(x, beside))
            for k, stride in enumerate(inner[:-1]):
                arrived, total = fence((came[0] if k == 0 else swap(join(*raw), n, stride), total))
                raw.append(arrived)
                beside = swap(arrived, n, 1)
                add(1 + 2 * k, arrived)
                add(2 + 2 * k, beside)
            return total[:probes] + (total[probes : 2 * probes] + total[2 * probes :]) + noise * pieces[0][:, :cols], pieces

        residual = direction = jnp.concatenate(starts, axis=1)
        my_solution = jnp.zeros_like(direction[:, :width])
        norm_now = jnp.sum(residual * residual, axis=1)
        my_next, applied = exchange(my_applied, lambda k, piece: piece)
        image = applied
        for iteration in range(ITERS - 1):
            last = iteration == ITERS - 2
            pieces, sent = (applied, my_next) if last else fence((applied, my_next))
            whole = jnp.concatenate(pieces, axis=1)
            curve = jnp.sum(direction * whole, axis=1)
            step_size = (norm_now / curve)[:, None]
            my_solution = my_solution + step_size * direction[:, :width]
            residual = residual - step_size * whole
            norm_next = jnp.sum(residual * residual, axis=1)
            ratio = (norm_next / norm_now)[:, None]
            direction = residual + ratio * direction
            norm_now = norm_next
            new_image = []

            def turn(k, piece):
                new_image.append(image[k] - step_size * piece)
                return new_image[k] + ratio * applied[k]

            if last:
                my_applied = image[0][:, :cols] - step_size * my_next + ratio * applied[0][:, :cols]
            else:
                my_next, applied = exchange(sent, turn)
                image = new_image
        curve = add_up(jnp.sum(direction[:, :cols] * my_applied, axis=1), n, inner)
        step_size = (norm_now / curve)[:, None]
        my_solution = my_solution + step_size * direction[:, :width]
        return my_solution, residual[:, :width] - step_size * my_applied[:, :width]

    in_specs = (P("groups", "blk"), P("groups"), P(("groups", "blk")), P("groups", "blk"))
    out_specs = (P("groups", "blk"), P("groups", "blk"))
    return jax.shard_map(body, mesh=mesh, in_specs=in_specs, out_specs=out_specs, check_vma=False)
```

```python
import math

import jax
import jax.numpy as jnp
from jax import lax
from jax.experimental import pallas as pl
from jax.experimental.pallas import tpu as pltpu
from jax.sharding import PartitionSpec as P

ITERS = 4
TILE_BYTES = 16 << 20
VMEM_BYTES = 16 << 20
NORM_ROWS = 64
BUILD_ROWS = 1024
POINT_SCALE = math.sqrt(math.log2(math.e))


def swap(x, n, stride):
    return lax.ppermute(x, "blk", [(i, i ^ stride) for i in range(n)])


def add_up(x, n, strides):
    for stride in strides:
        x = x + swap(x, n, stride)
    return x


def split(x, parts):
    out = []
    for _ in range(parts):
        high = lax.reduce_precision(x, 8, 7)
        out.append(high.astype(jnp.bfloat16))
        x = x - high
    return out


def halve(x):
    high = x.astype(jnp.bfloat16)
    return high, x - high.astype(jnp.float32)


def operands(pts):
    high, rest = halve(pts)
    mid, rest = halve(rest)
    low = rest.astype(jnp.bfloat16)
    norms = -0.5 * jnp.sum(pts * pts, axis=0, keepdims=True)
    row = lax.broadcasted_iota(jnp.int32, (NORM_ROWS, pts.shape[1]), 0)
    left = jnp.where((row >= 3) & (row < 6), 1.0, 0.0)
    right = jnp.where(row < 3, 1.0, 0.0)
    for k in range(3):
        part, norms = halve(norms)
        part = part.astype(jnp.float32)
        left = jnp.where(row == k, part, left)
        right = jnp.where(row == 3 + k, part, right)
    left = jnp.concatenate([high, high, mid, high, low, mid, left.astype(jnp.bfloat16)], axis=0)
    right = jnp.concatenate([high, mid, high, low, high, mid, right.astype(jnp.bfloat16)], axis=0)
    return left, right


def prepare_kernel(part_ref, scale_ref, right_ref, *copy_ref):
    feats = scale_ref.shape[0]
    right_ref[...] = operands(part_ref[:feats] * scale_ref[...])[1]
    for ref in copy_ref:
        ref[...] = part_ref[...]


def build_kernel(rows_ref, scale_ref, right_ref, *refs):
    applies = len(refs) > 1
    vectors_ref, sum_ref, tile_ref, out_ref = refs if applies else (None, None, *refs, None)
    total, cols = rows_ref.shape[1], right_ref.shape[1]
    block, step = min(total, BUILD_ROWS), min(cols, 256)
    if applies:
        probes = vectors_ref.shape[0]
        high, rest = halve(vectors_ref[...])
        mid, rest = halve(rest)
        twice = jnp.concatenate([high, mid], axis=0)
        thrice = jnp.concatenate([high, mid, rest.astype(jnp.bfloat16)], axis=0)
    steps = [(top, at) for top in range(0, total, block) for at in range(0, cols, step)]
    lefts, powers, parts = {}, {}, {}

    def contract(top, at):
        if top not in lefts:
            lefts[top] = jnp.transpose(operands(rows_ref[:, top : top + block] * scale_ref[...])[0])
        powers[top, at] = jnp.dot(lefts[top], right_ref[:, at : at + step], preferred_element_type=jnp.float32)

    def raise_power(top, at):
        high, rest = halve(jnp.exp2(powers.pop((top, at))))
        low = rest.astype(jnp.bfloat16)
        tile_ref[top : top + block, at : at + step] = high
        tile_ref[total + top : total + top + block, at : at + step] = low
        parts[top, at] = high, low

    def apply(top, at):
        down, here = slice(top, top + block), slice(at, at + step)
        high, low = parts.pop((top, at))
        large = jnp.dot(thrice[:, down], high, preferred_element_type=jnp.float32)
        small = jnp.dot(twice[:, down], low, preferred_element_type=jnp.float32)
        term = large[:probes] + ((large[probes : 2 * probes] + small[:probes]) + (large[2 * probes :] + small[probes:]))
        before = sum_ref if top == 0 else out_ref
        out_ref[:, here] = before[:, here] + term

    contract(*steps[0])
    for k, chunk in enumerate(steps):
        if k + 1 < len(steps):
            contract(*steps[k + 1])
        raise_power(*chunk)
        if k and applies:
            apply(*steps[k - 1])
    if applies:
        apply(*steps[-1])


def call(kernel, outs, *args, **cost):
    whole = pl.BlockSpec(memory_space=pltpu.VMEM)
    return pl.pallas_call(
        kernel,
        out_shape=outs,
        in_specs=[whole] * len(args),
        out_specs=jax.tree.map(lambda _: whole, outs),
        compiler_params=pltpu.CompilerParams(vmem_limit_bytes=VMEM_BYTES),
        cost_estimate=pl.CostEstimate(**cost),
    )(*args)


def prepare(part, scale, copy=False):
    feats, cols = scale.shape[0], part.shape[1]
    outs = (jax.ShapeDtypeStruct((6 * feats + NORM_ROWS, cols), jnp.bfloat16),)
    if copy:
        outs += (jax.ShapeDtypeStruct(part.shape, part.dtype),)
    return call(prepare_kernel, outs, part, scale, flops=10**9, bytes_accessed=feats * cols, transcendentals=0)


def join(*xs):
    return jnp.concatenate(xs, axis=1)


def build_piece(rows, scale, right, vectors=None, total=None):
    count, cols = rows.shape[1], right.shape[1]
    outs = (jax.ShapeDtypeStruct((2 * count, cols), jnp.bfloat16),)
    cost = dict(flops=2 * count * cols * 416, bytes_accessed=4 * count * cols, transcendentals=count * cols)
    args = (rows, scale, right)
    if vectors is not None:
        outs, args = (*outs, jax.ShapeDtypeStruct(total.shape, jnp.float32)), (*args, vectors, total)
    return call(build_kernel, outs, *args, **cost)


def parts_of(vectors):
    high, mid, low = split(vectors, 3)
    return jnp.concatenate([high, mid, low], axis=0)


def apply_parts(parts, piece):
    probes = parts.shape[0] // 3
    right = jnp.concatenate([parts[: 2 * probes], jnp.zeros_like(parts[2 * probes :])], axis=0)
    return jnp.dot(jnp.concatenate([parts, right], axis=1), piece, preferred_element_type=jnp.float32)


def apply_piece(vectors, piece):
    return apply_parts(parts_of(vectors), piece)


def collect(total):
    probes = total.shape[0] // 3
    return total[:probes] + (total[probes : 2 * probes] + total[2 * probes :])


def solution(mesh):
    n = mesh.shape["blk"]
    strides = [1 << k for k in reversed(range(n.bit_length() - 1))]

    def body(points, lengthscale, noise_var, targets):
        feats, width = points.shape
        probes = targets.shape[0]
        team = min(n, 4)
        while team < n and (n * width) * (n * width) // team * 4 > TILE_BYTES:
            team *= 2
        outer, inner = [s for s in strides if s >= team], [s for s in strides if s < team]

        def arrivals(x):
            pieces, sent = [x, swap(x, n, 1)], [x]
            for stride in inner[:-1]:
                came = swap(sent[0] if len(sent) == 1 else jnp.concatenate(sent, axis=1), n, stride)
                sent.append(came)
                pieces += [came, swap(came, n, 1)]
            return pieces

        scale = (POINT_SCALE / lengthscale)[:, None]
        block = lax.optimization_barrier(jnp.concatenate([points, targets, noise_var[None, :]], axis=0))
        fence = lax.optimization_barrier
        tile = []

        def build(x, total):
            piece, total = build_piece(x[:feats], scale, right, x[feats:], total)
            tile.append(piece)
            return total

        if len(outer) == 2 and len(inner) == 2:
            far, near, side = outer[0], outer[1], inner[0]
            by_far = swap(block, n, far)
            right_own, copy = prepare(block, scale, True)
            side_own = swap(copy, n, side)
            by_near = swap(join(block, by_far), n, near)
            right_far, copy = prepare(by_far, scale, True)
            side_far = swap(copy, n, side)
            last, side_own, side_far = fence((by_near, side_own, side_far))
            side_last = swap(last, n, side)
            right = join(right_own, right_far, *prepare(by_near, scale))
            mine = join(block, by_far, by_near)
            noise, mine = mine[-1:], mine[:-1]
            across = swap(mine, n, 1)
            my_applied = build(mine, noise * mine[feats:])
            side_own, side_far, my_applied = fence((side_own, side_far, my_applied))
            early = join(side_own, side_far)
            early_across = swap(early[:-1], n, 1)
            my_applied = build(across, my_applied)
            side_last, my_applied = fence((side_last, my_applied))
            last_across = swap(side_last[:-1], n, 1)
            beside = join(early, side_last)
            noise_beside, beside = beside[-1:], beside[:-1]
            my_far = build(beside, jnp.zeros_like(my_applied))
            early_across, last_across, my_far = fence((early_across, last_across, my_far))
            beside_across = join(early_across, last_across)
            my_far = build(beside_across, my_far)
            my_applied = my_applied + my_far
            first = [mine, across, beside, beside_across]
            far_rows = [beside[:feats], beside_across[:feats]]
        else:
            mine = block
            for stride in outer:
                mine = join(mine, swap(mine, n, stride))
            (right,), noise, first = prepare(mine, scale), mine[-1:], arrivals(mine[:-1])
            my_applied = noise * first[0][feats:]
            for x in first:
                my_applied = build(x, my_applied)
            my_far, far_rows = my_applied, []
        cols = noise.shape[1]
        starts = [x[feats:] for x in first]

        far_tile, right_far = [], None

        def exchange(x):
            nonlocal right_far
            parts, passed = fence((parts_of(x), x))
            pieces, sent = [x, swap(passed, n, 1)], [x]
            total = fence(apply_parts(parts, tile[0]))
            total = near = fence(total + apply_piece(pieces[1], tile[1]))
            for k, stride in enumerate(inner[:-1]):
                arrived = swap(join(*sent), n, stride)
                if len(far_tile) < len(far_rows):
                    rows, columns, total = fence((far_rows[len(far_tile)], far_rows[0], total))
                    if right_far is None:
                        (right_far,) = prepare(columns, scale)
                    (piece,) = build_piece(rows, scale, right_far)
                    arrived, piece, right_far, total = fence((arrived, piece, right_far, total))
                    far_tile.append(piece)
                sent.append(arrived)
                pieces += [arrived, swap(arrived, n, 1)]
                for at in (2 + 2 * k, 3 + 2 * k):
                    total = total + apply_piece(pieces[at], tile[at])
                    total = fence(total) if at < len(tile) - 1 else total
            return collect(total - near), collect(total) + noise * x, pieces

        residual = direction = join(*starts)
        my_solution = jnp.zeros_like(direction[:, :width])
        norm_now = jnp.sum(residual * residual, axis=1)
        my_image, far_image = my_applied, my_far
        for iteration in range(ITERS - 1):
            far_next, my_next, pieces = exchange(my_applied)
            applied = join(*pieces)
            curve = jnp.sum(direction * applied, axis=1)
            step_size = (norm_now / curve)[:, None]
            my_solution = my_solution + step_size * direction[:, :width]
            residual = residual - step_size * applied
            norm_next = jnp.sum(residual * residual, axis=1)
            ratio = (norm_next / norm_now)[:, None]
            my_image = my_image - step_size * my_next
            my_applied = my_image + ratio * my_applied
            far_image = far_image - step_size * far_next
            my_far = far_image + ratio * my_far
            direction = residual + ratio * direction
            norm_now = norm_next
        mine = direction[:, :cols]
        if far_rows:
            side, beside = direction[:, 2 * cols : 3 * cols], direction[:, 3 * cols :]
            image = collect(apply_piece(side, far_tile[0]) + apply_piece(beside, far_tile[1])) + noise_beside * side
            curve = add_up(jnp.sum(mine * (my_applied + my_far) + side * image, axis=1), n, [1])
        else:
            curve = add_up(jnp.sum(mine * my_applied, axis=1), n, inner)
        step_size = (norm_now / curve)[:, None]
        my_solution = my_solution + step_size * direction[:, :width]
        return my_solution, residual[:, :width] - step_size * my_applied[:, :width]

    in_specs = (P("groups", "blk"), P("groups"), P(("groups", "blk")), P("groups", "blk"))
    out_specs = (P("groups", "blk"), P("groups", "blk"))
    return jax.shard_map(body, mesh=mesh, in_specs=in_specs, out_specs=out_specs, check_vma=False)
```

```python
import math

import jax
import jax.numpy as jnp
from jax import lax
from jax.experimental import pallas as pl
from jax.experimental.pallas import tpu as pltpu
from jax.sharding import PartitionSpec as P

ITERS = 4
TILE_BYTES = 16 << 20
VMEM_BYTES = 16 << 20
NORM_ROWS = 64
BUILD_ROWS = 1024
POINT_SCALE = math.sqrt(math.log2(math.e))


def swap(x, n, stride):
    return lax.ppermute(x, "blk", [(i, i ^ stride) for i in range(n)])


def add_up(x, n, strides):
    for stride in strides:
        x = x + swap(x, n, stride)
    return x


def split(x, parts):
    out = []
    for _ in range(parts):
        high = lax.reduce_precision(x, 8, 7)
        out.append(high.astype(jnp.bfloat16))
        x = x - high
    return out


def halve(x):
    high = x.astype(jnp.bfloat16)
    return high, x - high.astype(jnp.float32)


def operands(pts):
    high, rest = halve(pts)
    mid, rest = halve(rest)
    low = rest.astype(jnp.bfloat16)
    norms = -0.5 * jnp.sum(pts * pts, axis=0, keepdims=True)
    row = lax.broadcasted_iota(jnp.int32, (NORM_ROWS, pts.shape[1]), 0)
    left = jnp.where((row >= 3) & (row < 6), 1.0, 0.0)
    right = jnp.where(row < 3, 1.0, 0.0)
    for k in range(3):
        part, norms = halve(norms)
        part = part.astype(jnp.float32)
        left = jnp.where(row == k, part, left)
        right = jnp.where(row == 3 + k, part, right)
    left = jnp.concatenate([high, high, mid, high, low, mid, left.astype(jnp.bfloat16)], axis=0)
    right = jnp.concatenate([high, mid, high, low, high, mid, right.astype(jnp.bfloat16)], axis=0)
    return left, right


def prepare_kernel(part_ref, scale_ref, right_ref, *copy_ref):
    feats = scale_ref.shape[0]
    right_ref[...] = operands(part_ref[:feats] * scale_ref[...])[1]
    for ref in copy_ref:
        ref[...] = part_ref[...]


def build_kernel(rows_ref, scale_ref, right_ref, *refs):
    applies = len(refs) > 1
    vectors_ref, sum_ref, tile_ref, out_ref = refs if applies else (None, None, *refs, None)
    total, cols = rows_ref.shape[1], right_ref.shape[1]
    block, step = min(total, BUILD_ROWS), min(cols, 256)
    if applies:
        probes = vectors_ref.shape[0]
        high, rest = halve(vectors_ref[...])
        mid, rest = halve(rest)
        twice = jnp.concatenate([high, mid], axis=0)
        thrice = jnp.concatenate([high, mid, rest.astype(jnp.bfloat16)], axis=0)
    steps = [(top, at) for top in range(0, total, block) for at in range(0, cols, step)]
    lefts, powers, parts = {}, {}, {}

    def contract(top, at):
        if top not in lefts:
            lefts[top] = jnp.transpose(operands(rows_ref[:, top : top + block] * scale_ref[...])[0])
        powers[top, at] = jnp.dot(lefts[top], right_ref[:, at : at + step], preferred_element_type=jnp.float32)

    def raise_power(top, at):
        high, rest = halve(jnp.exp2(powers.pop((top, at))))
        low = rest.astype(jnp.bfloat16)
        tile_ref[top : top + block, at : at + step] = high
        tile_ref[total + top : total + top + block, at : at + step] = low
        parts[top, at] = high, low

    def apply(top, at):
        down, here = slice(top, top + block), slice(at, at + step)
        high, low = parts.pop((top, at))
        large = jnp.dot(thrice[:, down], high, preferred_element_type=jnp.float32)
        small = jnp.dot(twice[:, down], low, preferred_element_type=jnp.float32)
        term = large[:probes] + ((large[probes : 2 * probes] + small[:probes]) + (large[2 * probes :] + small[probes:]))
        before = sum_ref if top == 0 else out_ref
        out_ref[:, here] = before[:, here] + term

    contract(*steps[0])
    for k, chunk in enumerate(steps):
        if k + 1 < len(steps):
            contract(*steps[k + 1])
        raise_power(*chunk)
        if k and applies:
            apply(*steps[k - 1])
    if applies:
        apply(*steps[-1])


def call(kernel, outs, *args, **cost):
    whole = pl.BlockSpec(memory_space=pltpu.VMEM)
    return pl.pallas_call(
        kernel,
        out_shape=outs,
        in_specs=[whole] * len(args),
        out_specs=jax.tree.map(lambda _: whole, outs),
        compiler_params=pltpu.CompilerParams(vmem_limit_bytes=VMEM_BYTES),
        cost_estimate=pl.CostEstimate(**cost),
    )(*args)


def prepare(part, scale, copy=False):
    feats, cols = scale.shape[0], part.shape[1]
    outs = (jax.ShapeDtypeStruct((6 * feats + NORM_ROWS, cols), jnp.bfloat16),)
    if copy:
        outs += (jax.ShapeDtypeStruct(part.shape, part.dtype),)
    return call(prepare_kernel, outs, part, scale, flops=10**9, bytes_accessed=feats * cols, transcendentals=0)


def join(*xs):
    return jnp.concatenate(xs, axis=1)


def build_piece(rows, scale, right, vectors=None, total=None):
    count, cols = rows.shape[1], right.shape[1]
    outs = (jax.ShapeDtypeStruct((2 * count, cols), jnp.bfloat16),)
    cost = dict(flops=2 * count * cols * 416, bytes_accessed=4 * count * cols, transcendentals=count * cols)
    args = (rows, scale, right)
    if vectors is not None:
        outs, args = (*outs, jax.ShapeDtypeStruct(total.shape, jnp.float32)), (*args, vectors, total)
    return call(build_kernel, outs, *args, **cost)


def parts_of(vectors):
    high, mid, low = split(vectors, 3)
    return jnp.concatenate([high, mid, low], axis=0)


def apply_parts(parts, piece):
    return jnp.dot(jnp.concatenate([parts, parts], axis=1), piece, preferred_element_type=jnp.float32)


def apply_piece(vectors, piece):
    return apply_parts(parts_of(vectors), piece)


def collect(total):
    probes = total.shape[0] // 3
    return total[:probes] + (total[probes : 2 * probes] + total[2 * probes :])


def solution(mesh):
    n = mesh.shape["blk"]
    strides = [1 << k for k in reversed(range(n.bit_length() - 1))]

    def body(points, lengthscale, noise_var, targets):
        feats, width = points.shape
        probes = targets.shape[0]
        team = min(n, 4)
        while team < n and (n * width) * (n * width) // team * 4 > TILE_BYTES:
            team *= 2
        outer, inner = [s for s in strides if s >= team], [s for s in strides if s < team]

        def arrivals(x):
            pieces, sent = [x, swap(x, n, 1)], [x]
            for stride in inner[:-1]:
                came = swap(sent[0] if len(sent) == 1 else jnp.concatenate(sent, axis=1), n, stride)
                sent.append(came)
                pieces += [came, swap(came, n, 1)]
            return pieces

        scale = (POINT_SCALE / lengthscale)[:, None]
        block = lax.optimization_barrier(jnp.concatenate([points, targets, noise_var[None, :]], axis=0))
        fence = lax.optimization_barrier
        tile = []

        def build(x, total):
            piece, total = build_piece(x[:feats], scale, right, x[feats:], total)
            tile.append(piece)
            return total

        if len(outer) == 2 and len(inner) == 2:
            far, near, side = outer[0], outer[1], inner[0]
            by_far = swap(block, n, far)
            right_own, copy = prepare(block, scale, True)
            side_own = swap(copy, n, side)
            by_near = swap(join(block, by_far), n, near)
            right_far, copy = prepare(by_far, scale, True)
            side_far = swap(copy, n, side)
            last, side_own, side_far = fence((by_near, side_own, side_far))
            side_last = swap(last, n, side)
            right = join(right_own, right_far, *prepare(by_near, scale))
            mine = join(block, by_far, by_near)
            noise, mine = mine[-1:], mine[:-1]
            across = swap(mine, n, 1)
            my_applied = build(mine, noise * mine[feats:])
            side_own, side_far, my_applied = fence((side_own, side_far, my_applied))
            early = join(side_own, side_far)
            early_across = swap(early[:-1], n, 1)
            my_applied = build(across, my_applied)
            side_last, my_applied = fence((side_last, my_applied))
            last_across = swap(side_last[:-1], n, 1)
            beside = join(early, side_last)
            noise_beside, beside = beside[-1:], beside[:-1]
            my_far = build(beside, jnp.zeros_like(my_applied))
            early_across, last_across, my_far = fence((early_across, last_across, my_far))
            beside_across = join(early_across, last_across)
            my_far = build(beside_across, my_far)
            my_applied = my_applied + my_far
            first = [mine, across, beside, beside_across]
            far_rows = [beside[:feats], beside_across[:feats]]
        else:
            mine = block
            for stride in outer:
                mine = join(mine, swap(mine, n, stride))
            (right,), noise, first = prepare(mine, scale), mine[-1:], arrivals(mine[:-1])
            my_applied = noise * first[0][feats:]
            for x in first:
                my_applied = build(x, my_applied)
            my_far, far_rows = my_applied, []
        cols = noise.shape[1]
        starts = [x[feats:] for x in first]

        far_tile, right_far = [], None

        def exchange(x, direction):
            nonlocal right_far
            parts, passed = fence((parts_of(x), x))
            pieces, sent = [x, swap(passed, n, 1)], [x]
            near = fence(apply_parts(parts, tile[0]))
            near = fence(near + apply_piece(pieces[1], tile[1]))
            far = jnp.zeros_like(near) if len(inner) == 1 else None
            for k, stride in enumerate(inner[:-1]):
                arrived = swap(join(*sent), n, stride)
                if len(far_tile) < len(far_rows):
                    rows, columns, near = fence((far_rows[len(far_tile)], far_rows[0], near))
                    if right_far is None:
                        (right_far,) = prepare(columns, scale)
                    (piece,) = build_piece(rows, scale, right_far)
                    piece, right_far, near = fence((piece, right_far, near))
                    far_tile.append(piece)
                arrived, near = fence((arrived, near))
                sent.append(arrived)
                pieces.append(arrived)
                term = apply_piece(arrived, tile[2 + 2 * k])
                far = fence(term if far is None else far + term)
                pieces.append(swap(arrived, n, 1))
                if k < len(inner) - 2:
                    far = fence(far + apply_piece(pieces[-1], tile[3 + 2 * k]))
            before = join(*pieces[:-1])
            curve = jnp.sum(direction[:, : before.shape[1]] * before, axis=1)
            curve, far = fence((curve, far))
            curve = curve + jnp.sum(direction[:, before.shape[1] :] * pieces[-1], axis=1)
            if len(inner) > 1:
                far = far + apply_piece(pieces[-1], tile[-1])
            return collect(far), collect(near) + collect(far) + noise * x, join(*pieces), curve

        residual = direction = join(*starts)
        my_solution = jnp.zeros_like(direction[:, :width])
        norm_now = jnp.sum(residual * residual, axis=1)
        my_image, far_image = my_applied, my_far
        for iteration in range(ITERS - 1):
            far_next, my_next, applied, curve = exchange(my_applied, direction)
            step_size = (norm_now / curve)[:, None]
            my_solution = my_solution + step_size * direction[:, :width]
            residual = residual - step_size * applied
            norm_next = jnp.sum(residual * residual, axis=1)
            ratio = (norm_next / norm_now)[:, None]
            my_image = my_image - step_size * my_next
            my_applied = my_image + ratio * my_applied
            far_image = far_image - step_size * far_next
            my_far = far_image + ratio * my_far
            direction = residual + ratio * direction
            norm_now = norm_next
        mine = direction[:, :cols]
        if far_rows:
            side, beside = direction[:, 2 * cols : 3 * cols], direction[:, 3 * cols :]
            image = collect(apply_piece(side, far_tile[0]) + apply_piece(beside, far_tile[1])) + noise_beside * side
            curve = add_up(jnp.sum(mine * (my_applied + my_far) + side * image, axis=1), n, [1])
        else:
            curve = add_up(jnp.sum(mine * my_applied, axis=1), n, inner)
        step_size = (norm_now / curve)[:, None]
        my_solution = my_solution + step_size * direction[:, :width]
        return my_solution, residual[:, :width] - step_size * my_applied[:, :width]

    in_specs = (P("groups", "blk"), P("groups"), P(("groups", "blk")), P("groups", "blk"))
    out_specs = (P("groups", "blk"), P("groups", "blk"))
    return jax.shard_map(body, mesh=mesh, in_specs=in_specs, out_specs=out_specs, check_vma=False)
```

```python
import math

import jax
import jax.numpy as jnp
from jax import lax
from jax.experimental import pallas as pl
from jax.experimental.pallas import tpu as pltpu
from jax.sharding import PartitionSpec as P

ITERS = 4
TILE_BYTES = 16 << 20
VMEM_BYTES = 16 << 20
NORM_ROWS = 64
BUILD_ROWS = 1024
POINT_SCALE = math.sqrt(math.log2(math.e))


def swap(x, n, stride):
    return lax.ppermute(x, "blk", [(i, i ^ stride) for i in range(n)])


def add_up(x, n, strides):
    for stride in strides:
        x = x + swap(x, n, stride)
    return x


def split(x, parts):
    out = []
    for _ in range(parts):
        high = lax.reduce_precision(x, 8, 7)
        out.append(high.astype(jnp.bfloat16))
        x = x - high
    return out


def halve(x):
    high = x.astype(jnp.bfloat16)
    return high, x - high.astype(jnp.float32)


def operands(pts):
    high, rest = halve(pts)
    mid, rest = halve(rest)
    low = rest.astype(jnp.bfloat16)
    norms = -0.5 * jnp.sum(pts * pts, axis=0, keepdims=True)
    row = lax.broadcasted_iota(jnp.int32, (NORM_ROWS, pts.shape[1]), 0)
    left = jnp.where((row >= 3) & (row < 6), 1.0, 0.0)
    right = jnp.where(row < 3, 1.0, 0.0)
    for k in range(3):
        part, norms = halve(norms)
        part = part.astype(jnp.float32)
        left = jnp.where(row == k, part, left)
        right = jnp.where(row == 3 + k, part, right)
    left = jnp.concatenate([high, high, mid, high, low, mid, left.astype(jnp.bfloat16)], axis=0)
    right = jnp.concatenate([high, mid, high, low, high, mid, right.astype(jnp.bfloat16)], axis=0)
    return left, right


def prepare_kernel(part_ref, scale_ref, right_ref, *copy_ref):
    feats = scale_ref.shape[0]
    right_ref[...] = operands(part_ref[:feats] * scale_ref[...])[1]
    for ref in copy_ref:
        ref[...] = part_ref[...]


def build_kernel(rows_ref, scale_ref, right_ref, *refs):
    applies = len(refs) > 1
    vectors_ref, sum_ref, tile_ref, out_ref = refs if applies else (None, None, *refs, None)
    total, cols = rows_ref.shape[1], right_ref.shape[1]
    block, step = min(total, BUILD_ROWS), min(cols, 256)
    if applies:
        probes = vectors_ref.shape[0]
        high, rest = halve(vectors_ref[...])
        mid, rest = halve(rest)
        twice = jnp.concatenate([high, mid], axis=0)
        thrice = jnp.concatenate([high, mid, rest.astype(jnp.bfloat16)], axis=0)
    steps = [(top, at) for top in range(0, total, block) for at in range(0, cols, step)]
    lefts, powers, parts = {}, {}, {}

    def contract(top, at):
        if top not in lefts:
            lefts[top] = jnp.transpose(operands(rows_ref[:, top : top + block] * scale_ref[...])[0])
        powers[top, at] = jnp.dot(lefts[top], right_ref[:, at : at + step], preferred_element_type=jnp.float32)

    def raise_power(top, at):
        high, rest = halve(jnp.exp2(powers.pop((top, at))))
        low = rest.astype(jnp.bfloat16)
        tile_ref[top : top + block, at : at + step] = high
        tile_ref[total + top : total + top + block, at : at + step] = low
        parts[top, at] = high, low

    def apply(top, at):
        down, here = slice(top, top + block), slice(at, at + step)
        high, low = parts.pop((top, at))
        large = jnp.dot(thrice[:, down], high, preferred_element_type=jnp.float32)
        small = jnp.dot(twice[:, down], low, preferred_element_type=jnp.float32)
        term = large[:probes] + ((large[probes : 2 * probes] + small[:probes]) + (large[2 * probes :] + small[probes:]))
        before = sum_ref if top == 0 else out_ref
        out_ref[:, here] = before[:, here] + term

    contract(*steps[0])
    for k, chunk in enumerate(steps):
        if k + 1 < len(steps):
            contract(*steps[k + 1])
        raise_power(*chunk)
        if k and applies:
            apply(*steps[k - 1])
    if applies:
        apply(*steps[-1])


def call(kernel, outs, *args, **cost):
    whole = pl.BlockSpec(memory_space=pltpu.VMEM)
    return pl.pallas_call(
        kernel,
        out_shape=outs,
        in_specs=[whole] * len(args),
        out_specs=jax.tree.map(lambda _: whole, outs),
        compiler_params=pltpu.CompilerParams(vmem_limit_bytes=VMEM_BYTES),
        cost_estimate=pl.CostEstimate(**cost),
    )(*args)


def prepare(part, scale, copy=False):
    feats, cols = scale.shape[0], part.shape[1]
    outs = (jax.ShapeDtypeStruct((6 * feats + NORM_ROWS, cols), jnp.bfloat16),)
    if copy:
        outs += (jax.ShapeDtypeStruct(part.shape, part.dtype),)
    return call(prepare_kernel, outs, part, scale, flops=10**9, bytes_accessed=feats * cols, transcendentals=0)


def join(*xs):
    return jnp.concatenate(xs, axis=1)


def build_piece(rows, scale, right, vectors=None, total=None):
    count, cols = rows.shape[1], right.shape[1]
    outs = (jax.ShapeDtypeStruct((2 * count, cols), jnp.bfloat16),)
    cost = dict(flops=2 * count * cols * 416, bytes_accessed=4 * count * cols, transcendentals=count * cols)
    args = (rows, scale, right)
    if vectors is not None:
        outs, args = (*outs, jax.ShapeDtypeStruct(total.shape, jnp.float32)), (*args, vectors, total)
    return call(build_kernel, outs, *args, **cost)


def parts_of(vectors):
    high, mid, low = split(vectors, 3)
    return jnp.concatenate([high, mid, low], axis=0)


def apply_parts(parts, piece):
    return jnp.dot(jnp.concatenate([parts, parts], axis=1), piece, preferred_element_type=jnp.float32)


def apply_piece(vectors, piece):
    return apply_parts(parts_of(vectors), piece)


def collect(total):
    probes = total.shape[0] // 3
    return total[:probes] + (total[probes : 2 * probes] + total[2 * probes :])


def solution(mesh):
    n = mesh.shape["blk"]
    strides = [1 << k for k in reversed(range(n.bit_length() - 1))]

    def body(points, lengthscale, noise_var, targets):
        feats, width = points.shape
        probes = targets.shape[0]
        team = min(n, 4)
        while team < n and (n * width) * (n * width) // team * 4 > TILE_BYTES:
            team *= 2
        outer, inner = [s for s in strides if s >= team], [s for s in strides if s < team]

        def arrivals(x):
            pieces, sent = [x, swap(x, n, 1)], [x]
            for stride in inner[:-1]:
                came = swap(sent[0] if len(sent) == 1 else jnp.concatenate(sent, axis=1), n, stride)
                sent.append(came)
                pieces += [came, swap(came, n, 1)]
            return pieces

        scale = (POINT_SCALE / lengthscale)[:, None]
        block = lax.optimization_barrier(jnp.concatenate([points, targets, noise_var[None, :]], axis=0))
        fence = lax.optimization_barrier
        tile = []

        def build(x, total):
            piece, total = build_piece(x[:feats], scale, right, x[feats:], total)
            tile.append(piece)
            return total

        if len(outer) == 2 and len(inner) == 2:
            far, near, side = outer[0], outer[1], inner[0]
            by_far = swap(block, n, far)
            right_own, copy = prepare(block, scale, True)
            side_own = swap(copy, n, side)
            by_near = swap(join(block, by_far), n, near)
            right_far, copy = prepare(by_far, scale, True)
            side_far = swap(copy, n, side)
            last, side_own, side_far = fence((by_near, side_own, side_far))
            side_last = swap(last, n, side)
            right = join(right_own, right_far, *prepare(by_near, scale))
            mine = join(block, by_far, by_near)
            noise, mine = mine[-1:], mine[:-1]
            across = swap(mine, n, 1)
            my_applied = build(mine, noise * mine[feats:])
            my_applied = build(across, my_applied)
            side_last, my_applied = fence((side_last, my_applied))
            beside = join(side_own, side_far, side_last)
            noise_beside, beside = beside[-1:], beside[:-1]
            beside_across = swap(beside, n, 1)
            my_far = build(beside, jnp.zeros_like(my_applied))
            my_far = build(beside_across, my_far)
            my_applied = my_applied + my_far
            first = [mine, across, beside, beside_across]
            far_rows = [beside[:feats], beside_across[:feats]]
        else:
            mine = block
            for stride in outer:
                mine = join(mine, swap(mine, n, stride))
            (right,), noise, first = prepare(mine, scale), mine[-1:], arrivals(mine[:-1])
            my_applied = noise * first[0][feats:]
            for x in first:
                my_applied = build(x, my_applied)
            my_far, far_rows = my_applied, []
        cols = noise.shape[1]
        starts = [x[feats:] for x in first]

        far_tile, right_far = [], None

        def exchange(x, direction):
            nonlocal right_far
            parts, passed = fence((parts_of(x), x))
            pieces, sent = [x, swap(passed, n, 1)], [x]
            near = fence(apply_parts(parts, tile[0]))
            near = fence(near + apply_piece(pieces[1], tile[1]))
            far = jnp.zeros_like(near) if len(inner) == 1 else None
            for k, stride in enumerate(inner[:-1]):
                arrived = swap(join(*sent), n, stride)
                if len(far_tile) < len(far_rows):
                    rows, columns, near = fence((far_rows[len(far_tile)], far_rows[0], near))
                    if right_far is None:
                        (right_far,) = prepare(columns, scale)
                    (piece,) = build_piece(rows, scale, right_far)
                    piece, right_far, near = fence((piece, right_far, near))
                    far_tile.append(piece)
                arrived, near = fence((arrived, near))
                sent.append(arrived)
                pieces.append(arrived)
                term = apply_piece(arrived, tile[2 + 2 * k])
                far = fence(term if far is None else far + term)
                pieces.append(swap(arrived, n, 1))
                if k < len(inner) - 2:
                    far = fence(far + apply_piece(pieces[-1], tile[3 + 2 * k]))
            before = join(*pieces[:-1])
            curve = jnp.sum(direction[:, : before.shape[1]] * before, axis=1)
            curve, far = fence((curve, far))
            curve = curve + jnp.sum(direction[:, before.shape[1] :] * pieces[-1], axis=1)
            if len(inner) > 1:
                far = far + apply_piece(pieces[-1], tile[-1])
            return collect(far), collect(near) + collect(far) + noise * x, join(*pieces), curve

        residual = direction = join(*starts)
        my_solution = jnp.zeros_like(direction[:, :width])
        norm_now = jnp.sum(residual * residual, axis=1)
        my_image, far_image = my_applied, my_far
        for iteration in range(ITERS - 1):
            far_next, my_next, applied, curve = exchange(my_applied, direction)
            step_size = (norm_now / curve)[:, None]
            my_solution = my_solution + step_size * direction[:, :width]
            residual = residual - step_size * applied
            norm_next = jnp.sum(residual * residual, axis=1)
            ratio = (norm_next / norm_now)[:, None]
            my_image = my_image - step_size * my_next
            my_applied = my_image + ratio * my_applied
            far_image = far_image - step_size * far_next
            my_far = far_image + ratio * my_far
            direction = residual + ratio * direction
            norm_now = norm_next
        mine = direction[:, :cols]
        if far_rows:
            side, beside = direction[:, 2 * cols : 3 * cols], direction[:, 3 * cols :]
            image = collect(apply_piece(side, far_tile[0]) + apply_piece(beside, far_tile[1])) + noise_beside * side
            curve = add_up(jnp.sum(mine * (my_applied + my_far) + side * image, axis=1), n, [1])
        else:
            curve = add_up(jnp.sum(mine * my_applied, axis=1), n, inner)
        step_size = (norm_now / curve)[:, None]
        my_solution = my_solution + step_size * direction[:, :width]
        return my_solution, residual[:, :width] - step_size * my_applied[:, :width]

    in_specs = (P("groups", "blk"), P("groups"), P(("groups", "blk")), P("groups", "blk"))
    out_specs = (P("groups", "blk"), P("groups", "blk"))
    return jax.shard_map(body, mesh=mesh, in_specs=in_specs, out_specs=out_specs, check_vma=False)
```

```python
import math

import jax
import jax.numpy as jnp
from jax import lax
from jax.experimental import pallas as pl
from jax.experimental.pallas import tpu as pltpu
from jax.sharding import PartitionSpec as P

ITERS = 4
TILE_BYTES = 16 << 20
VMEM_BYTES = 16 << 20
NORM_ROWS = 64
BUILD_ROWS = 1024
POINT_SCALE = math.sqrt(math.log2(math.e))


def swap(x, n, stride):
    return lax.ppermute(x, "blk", [(i, i ^ stride) for i in range(n)])


def add_up(x, n, strides):
    for stride in strides:
        x = x + swap(x, n, stride)
    return x


def split(x, parts):
    out = []
    for _ in range(parts):
        high = lax.reduce_precision(x, 8, 7)
        out.append(high.astype(jnp.bfloat16))
        x = x - high
    return out


def halve(x):
    high = x.astype(jnp.bfloat16)
    return high, x - high.astype(jnp.float32)


def operands(pts):
    high, rest = halve(pts)
    mid, rest = halve(rest)
    low = rest.astype(jnp.bfloat16)
    norms = -0.5 * jnp.sum(pts * pts, axis=0, keepdims=True)
    row = lax.broadcasted_iota(jnp.int32, (NORM_ROWS, pts.shape[1]), 0)
    left = jnp.where((row >= 3) & (row < 6), 1.0, 0.0)
    right = jnp.where(row < 3, 1.0, 0.0)
    for k in range(3):
        part, norms = halve(norms)
        part = part.astype(jnp.float32)
        left = jnp.where(row == k, part, left)
        right = jnp.where(row == 3 + k, part, right)
    left = jnp.concatenate([high, high, mid, high, low, mid, left.astype(jnp.bfloat16)], axis=0)
    right = jnp.concatenate([high, mid, high, low, high, mid, right.astype(jnp.bfloat16)], axis=0)
    return left, right


def prepare_kernel(part_ref, scale_ref, right_ref, *copy_ref):
    feats = scale_ref.shape[0]
    right_ref[...] = operands(part_ref[:feats] * scale_ref[...])[1]
    for ref in copy_ref:
        ref[...] = part_ref[: ref.shape[0]]


def build_kernel(rows_ref, scale_ref, right_ref, *refs):
    applies = len(refs) > 1
    vectors_ref, sum_ref, tile_ref, out_ref = refs if applies else (None, None, *refs, None)
    total, cols = rows_ref.shape[1], right_ref.shape[1]
    block, step = min(total, BUILD_ROWS), min(cols, 256)
    if applies:
        probes = vectors_ref.shape[0]
        high, rest = halve(vectors_ref[...])
        mid, rest = halve(rest)
        twice = jnp.concatenate([high, mid], axis=0)
        thrice = jnp.concatenate([high, mid, rest.astype(jnp.bfloat16)], axis=0)
    steps = [(top, at) for top in range(0, total, block) for at in range(0, cols, step)]
    lefts, powers, parts = {}, {}, {}

    def contract(top, at):
        if top not in lefts:
            lefts[top] = jnp.transpose(operands(rows_ref[:, top : top + block] * scale_ref[...])[0])
        powers[top, at] = jnp.dot(lefts[top], right_ref[:, at : at + step], preferred_element_type=jnp.float32)

    def raise_power(top, at):
        high, rest = halve(jnp.exp2(powers.pop((top, at))))
        low = rest.astype(jnp.bfloat16)
        tile_ref[top : top + block, at : at + step] = high
        tile_ref[total + top : total + top + block, at : at + step] = low
        parts[top, at] = high, low

    def apply(top, at):
        down, here = slice(top, top + block), slice(at, at + step)
        high, low = parts.pop((top, at))
        large = jnp.dot(thrice[:, down], high, preferred_element_type=jnp.float32)
        small = jnp.dot(twice[:, down], low, preferred_element_type=jnp.float32)
        term = large[:probes] + ((large[probes : 2 * probes] + small[:probes]) + (large[2 * probes :] + small[probes:]))
        before = sum_ref if top == 0 else out_ref
        out_ref[:, here] = before[:, here] + term

    contract(*steps[0])
    for k, chunk in enumerate(steps):
        if k + 1 < len(steps):
            contract(*steps[k + 1])
        raise_power(*chunk)
        if k and applies:
            apply(*steps[k - 1])
    if applies:
        apply(*steps[-1])


def call(kernel, outs, *args, **cost):
    whole = pl.BlockSpec(memory_space=pltpu.VMEM)
    return pl.pallas_call(
        kernel,
        out_shape=outs,
        in_specs=[whole] * len(args),
        out_specs=jax.tree.map(lambda _: whole, outs),
        compiler_params=pltpu.CompilerParams(vmem_limit_bytes=VMEM_BYTES),
        cost_estimate=pl.CostEstimate(**cost),
    )(*args)


def prepare(part, scale, copy=0):
    feats, cols = scale.shape[0], part.shape[1]
    outs = (jax.ShapeDtypeStruct((6 * feats + NORM_ROWS, cols), jnp.bfloat16),)
    if copy:
        outs += (jax.ShapeDtypeStruct((copy, cols), part.dtype),)
    return call(prepare_kernel, outs, part, scale, flops=10**0, bytes_accessed=feats * cols, transcendentals=0)


def join(*xs):
    return jnp.concatenate(xs, axis=1)


def build_piece(rows, scale, right, vectors=None, total=None):
    count, cols = rows.shape[1], right.shape[1]
    outs = (jax.ShapeDtypeStruct((2 * count, cols), jnp.bfloat16),)
    cost = dict(flops=2 * count * cols * 416, bytes_accessed=4 * count * cols, transcendentals=count * cols)
    args = (rows, scale, right)
    if vectors is not None:
        outs, args = (*outs, jax.ShapeDtypeStruct(total.shape, jnp.float32)), (*args, vectors, total)
    return call(build_kernel, outs, *args, **cost)


def parts_of(vectors):
    high, mid, low = split(vectors, 3)
    return jnp.concatenate([high, mid, low], axis=0)


def apply_parts(parts, piece):
    return jnp.dot(jnp.concatenate([parts, parts], axis=1), piece, preferred_element_type=jnp.float32)


def apply_piece(vectors, piece):
    return apply_parts(parts_of(vectors), piece)


def collect(total):
    probes = total.shape[0] // 3
    return total[:probes] + (total[probes : 2 * probes] + total[2 * probes :])


def solution(mesh):
    n = mesh.shape["blk"]
    strides = [1 << k for k in reversed(range(n.bit_length() - 1))]

    def body(points, lengthscale, noise_var, targets):
        feats, width = points.shape
        probes = targets.shape[0]
        team = min(n, 4)
        while team < n and (n * width) * (n * width) // team * 4 > TILE_BYTES:
            team *= 2
        outer, inner = [s for s in strides if s >= team], [s for s in strides if s < team]

        def arrivals(x):
            pieces, sent = [x, swap(x, n, 1)], [x]
            for stride in inner[:-1]:
                came = swap(sent[0] if len(sent) == 1 else jnp.concatenate(sent, axis=1), n, stride)
                sent.append(came)
                pieces += [came, swap(came, n, 1)]
            return pieces

        scale = (POINT_SCALE / lengthscale)[:, None]
        rows = [points, targets, noise_var[None, :]]
        used = sum(x.shape[0] for x in rows)
        block = lax.optimization_barrier(jnp.concatenate([*rows, jnp.zeros((-used % 8, width), jnp.float32)], axis=0))
        fence = lax.optimization_barrier
        tile = []

        def build(x, total):
            piece, total = build_piece(x[:feats], scale, right, x[feats:], total)
            tile.append(piece)
            return total

        if len(outer) == 2 and len(inner) == 2:
            far, near, side = outer[0], outer[1], inner[0]
            by_far = swap(block, n, far)
            right_own, copy = prepare(block, scale, used)
            near_own = swap(copy, n, near)
            side_own = swap(copy, n, side)
            near_far = swap(by_far, n, near)
            right_far, copy = prepare(by_far, scale, used)
            side_far = swap(copy, n, side)
            right_near, by_near = prepare(join(near_own, near_far[:used]), scale, used)
            last, side_own, side_far = fence((by_near, side_own, side_far))
            side_last = swap(last, n, side)
            right = join(right_own, right_far, right_near)
            mine = join(block[:used], by_far[:used], by_near)
            noise, mine = mine[-1:], mine[:-1]
            across = swap(mine, n, 1)
            my_applied = build(mine, noise * mine[feats:])
            my_applied = build(across, my_applied)
            side_last, my_applied = fence((side_last, my_applied))
            beside = join(side_own, side_far, side_last)
            noise_beside, beside = beside[-1:], beside[:-1]
            beside_across = swap(beside, n, 1)
            my_far = build(beside, jnp.zeros_like(my_applied))
            my_far = build(beside_across, my_far)
            my_applied = my_applied + my_far
            first = [mine, across, beside, beside_across]
            far_rows = [beside[:feats], beside_across[:feats]]
        else:
            mine = block
            for stride in outer:
                mine = join(mine, swap(mine, n, stride))
            mine = mine[:used]
            (right,), noise, first = prepare(mine, scale), mine[-1:], arrivals(mine[:-1])
            my_applied = noise * first[0][feats:]
            for x in first:
                my_applied = build(x, my_applied)
            my_far, far_rows = my_applied, []
        cols = noise.shape[1]
        starts = [x[feats:] for x in first]

        far_tile, right_far = [], None

        def exchange(x, direction):
            nonlocal right_far
            parts, passed = fence((parts_of(x), x))
            pieces, sent = [x, swap(passed, n, 1)], [x]
            near = fence(apply_parts(parts, tile[0]))
            near = fence(near + apply_piece(pieces[1], tile[1]))
            far = jnp.zeros_like(near) if len(inner) == 1 else None
            for k, stride in enumerate(inner[:-1]):
                arrived = swap(join(*sent), n, stride)
                if len(far_tile) < len(far_rows):
                    rows, columns, near = fence((far_rows[len(far_tile)], far_rows[0], near))
                    if right_far is None:
                        (right_far,) = prepare(columns, scale)
                    (piece,) = build_piece(rows, scale, right_far)
                    piece, right_far, near = fence((piece, right_far, near))
                    far_tile.append(piece)
                arrived, near = fence((arrived, near))
                sent.append(arrived)
                pieces.append(arrived)
                term = apply_piece(arrived, tile[2 + 2 * k])
                far = fence(term if far is None else far + term)
                pieces.append(swap(arrived, n, 1))
                if k < len(inner) - 2:
                    far = fence(far + apply_piece(pieces[-1], tile[3 + 2 * k]))
            before = join(*pieces[:-1])
            curve = jnp.sum(direction[:, : before.shape[1]] * before, axis=1)
            curve, far = fence((curve, far))
            curve = curve + jnp.sum(direction[:, before.shape[1] :] * pieces[-1], axis=1)
            if len(inner) > 1:
                far = far + apply_piece(pieces[-1], tile[-1])
            return collect(far), collect(near) + collect(far) + noise * x, join(*pieces), curve

        residual = direction = join(*starts)
        my_solution = jnp.zeros_like(direction[:, :width])
        norm_now = jnp.sum(residual * residual, axis=1)
        my_image, far_image = my_applied, my_far
        for iteration in range(ITERS - 1):
            far_next, my_next, applied, curve = exchange(my_applied, direction)
            step_size = (norm_now / curve)[:, None]
            my_solution = my_solution + step_size * direction[:, :width]
            residual = residual - step_size * applied
            norm_next = jnp.sum(residual * residual, axis=1)
            ratio = (norm_next / norm_now)[:, None]
            my_image = my_image - step_size * my_next
            my_applied = my_image + ratio * my_applied
            far_image = far_image - step_size * far_next
            my_far = far_image + ratio * my_far
            direction = residual + ratio * direction
            norm_now = norm_next
        mine = direction[:, :cols]
        if far_rows:
            side, beside = direction[:, 2 * cols : 3 * cols], direction[:, 3 * cols :]
            image = collect(apply_piece(side, far_tile[0]) + apply_piece(beside, far_tile[1])) + noise_beside * side
            curve = add_up(jnp.sum(mine * (my_applied + my_far) + side * image, axis=1), n, [1])
        else:
            curve = add_up(jnp.sum(mine * my_applied, axis=1), n, inner)
        step_size = (norm_now / curve)[:, None]
        my_solution = my_solution + step_size * direction[:, :width]
        return my_solution, residual[:, :width] - step_size * my_applied[:, :width]

    in_specs = (P("groups", "blk"), P("groups"), P(("groups", "blk")), P("groups", "blk"))
    out_specs = (P("groups", "blk"), P("groups", "blk"))
    return jax.shard_map(body, mesh=mesh, in_specs=in_specs, out_specs=out_specs, check_vma=False)
```

```python
import math

import jax
import jax.numpy as jnp
from jax import lax
from jax.experimental import pallas as pl
from jax.experimental.pallas import tpu as pltpu
from jax.sharding import PartitionSpec as P

ITERS = 4
TILE_BYTES = 16 << 20
VMEM_BYTES = 16 << 20
NORM_ROWS = 64
BUILD_ROWS = 1024
POINT_SCALE = math.sqrt(math.log2(math.e))


def swap(x, n, stride):
    return lax.ppermute(x, "blk", [(i, i ^ stride) for i in range(n)])


def add_up(x, n, strides):
    for stride in strides:
        x = x + swap(x, n, stride)
    return x


def split(x, parts):
    out = []
    for _ in range(parts):
        high = lax.reduce_precision(x, 8, 7)
        out.append(high.astype(jnp.bfloat16))
        x = x - high
    return out


def halve(x):
    high = x.astype(jnp.bfloat16)
    return high, x - high.astype(jnp.float32)


def operands(pts):
    high, rest = halve(pts)
    mid, rest = halve(rest)
    low = rest.astype(jnp.bfloat16)
    norms = -0.5 * jnp.sum(pts * pts, axis=0, keepdims=True)
    row = lax.broadcasted_iota(jnp.int32, (NORM_ROWS, pts.shape[1]), 0)
    left = jnp.where((row >= 3) & (row < 6), 1.0, 0.0)
    right = jnp.where(row < 3, 1.0, 0.0)
    for k in range(3):
        part, norms = halve(norms)
        part = part.astype(jnp.float32)
        left = jnp.where(row == k, part, left)
        right = jnp.where(row == 3 + k, part, right)
    left = jnp.concatenate([high, high, mid, high, low, mid, left.astype(jnp.bfloat16)], axis=0)
    right = jnp.concatenate([high, mid, high, low, high, mid, right.astype(jnp.bfloat16)], axis=0)
    return left, right


def prepare_kernel(part_ref, scale_ref, right_ref, *copy_ref):
    feats = scale_ref.shape[0]
    right_ref[...] = operands(part_ref[:feats] * scale_ref[...])[1]
    for ref in copy_ref:
        ref[...] = part_ref[: ref.shape[0]]


def build_kernel(rows_ref, scale_ref, right_ref, *refs):
    applies = len(refs) > 1
    vectors_ref, sum_ref, tile_ref, out_ref = refs if applies else (None, None, *refs, None)
    total, cols = rows_ref.shape[1], right_ref.shape[1]
    block, step = min(total, BUILD_ROWS), min(cols, 256)
    if applies:
        probes = vectors_ref.shape[0]
        high, rest = halve(vectors_ref[...])
        mid, rest = halve(rest)
        twice = jnp.concatenate([high, mid], axis=0)
        thrice = jnp.concatenate([high, mid, rest.astype(jnp.bfloat16)], axis=0)
    steps = [(top, at) for top in range(0, total, block) for at in range(0, cols, step)]
    lefts, powers, parts = {}, {}, {}

    def contract(top, at):
        if top not in lefts:
            lefts[top] = jnp.transpose(operands(rows_ref[:, top : top + block] * scale_ref[...])[0])
        powers[top, at] = jnp.dot(lefts[top], right_ref[:, at : at + step], preferred_element_type=jnp.float32)

    def raise_power(top, at):
        high, rest = halve(jnp.exp2(powers.pop((top, at))))
        low = rest.astype(jnp.bfloat16)
        tile_ref[top : top + block, at : at + step] = high
        tile_ref[total + top : total + top + block, at : at + step] = low
        parts[top, at] = high, low

    def apply(top, at):
        down, here = slice(top, top + block), slice(at, at + step)
        high, low = parts.pop((top, at))
        large = jnp.dot(thrice[:, down], high, preferred_element_type=jnp.float32)
        small = jnp.dot(twice[:, down], low, preferred_element_type=jnp.float32)
        term = large[:probes] + ((large[probes : 2 * probes] + small[:probes]) + (large[2 * probes :] + small[probes:]))
        before = sum_ref if top == 0 else out_ref
        out_ref[:, here] = before[:, here] + term

    contract(*steps[0])
    for k, chunk in enumerate(steps):
        if k + 1 < len(steps):
            contract(*steps[k + 1])
        raise_power(*chunk)
        if k and applies:
            apply(*steps[k - 1])
    if applies:
        apply(*steps[-1])


def call(kernel, outs, *args, **cost):
    whole = pl.BlockSpec(memory_space=pltpu.VMEM)
    return pl.pallas_call(
        kernel,
        out_shape=outs,
        in_specs=[whole] * len(args),
        out_specs=jax.tree.map(lambda _: whole, outs),
        compiler_params=pltpu.CompilerParams(vmem_limit_bytes=VMEM_BYTES),
        cost_estimate=pl.CostEstimate(**cost),
    )(*args)


def prepare(part, scale, copy=0):
    feats, cols = scale.shape[0], part.shape[1]
    outs = (jax.ShapeDtypeStruct((6 * feats + NORM_ROWS, cols), jnp.bfloat16),)
    if copy:
        outs += (jax.ShapeDtypeStruct((copy, cols), part.dtype),)
    return call(prepare_kernel, outs, part, scale, flops=10**0, bytes_accessed=feats * cols, transcendentals=0)


def join(*xs):
    return jnp.concatenate(xs, axis=1)


def build_piece(rows, scale, right, vectors=None, total=None):
    count, cols = rows.shape[1], right.shape[1]
    outs = (jax.ShapeDtypeStruct((2 * count, cols), jnp.bfloat16),)
    cost = dict(flops=2 * count * cols * 416, bytes_accessed=4 * count * cols, transcendentals=count * cols)
    args = (rows, scale, right)
    if vectors is not None:
        outs, args = (*outs, jax.ShapeDtypeStruct(total.shape, jnp.float32)), (*args, vectors, total)
    return call(build_kernel, outs, *args, **cost)


def parts_of(vectors):
    high, mid, low = split(vectors, 3)
    return jnp.concatenate([high, mid, low], axis=0)


def apply_parts(parts, piece):
    return jnp.dot(jnp.concatenate([parts, parts], axis=1), piece, preferred_element_type=jnp.float32)


def apply_piece(vectors, piece):
    return apply_parts(parts_of(vectors), piece)


def collect(total):
    probes = total.shape[0] // 3
    return total[:probes] + (total[probes : 2 * probes] + total[2 * probes :])


def solution(mesh):
    n = mesh.shape["blk"]
    strides = [1 << k for k in reversed(range(n.bit_length() - 1))]

    def body(points, lengthscale, noise_var, targets):
        feats, width = points.shape
        probes = targets.shape[0]
        team = min(n, 4)
        while team < n and (n * width) * (n * width) // team * 4 > TILE_BYTES:
            team *= 2
        outer, inner = [s for s in strides if s >= team], [s for s in strides if s < team]

        def arrivals(x):
            pieces, sent = [x, swap(x, n, 1)], [x]
            for stride in inner[:-1]:
                came = swap(sent[0] if len(sent) == 1 else jnp.concatenate(sent, axis=1), n, stride)
                sent.append(came)
                pieces += [came, swap(came, n, 1)]
            return pieces

        scale = (POINT_SCALE / lengthscale)[:, None]
        used = feats + probes + 1
        rest = jnp.broadcast_to(noise_var[None, :], (1 + -used % 8, width))
        block = lax.optimization_barrier(jnp.concatenate([points, targets, rest], axis=0))
        fence = lax.optimization_barrier
        tile = []

        def build(x, total):
            piece, total = build_piece(x[:feats], scale, right, x[feats:], total)
            tile.append(piece)
            return total

        if len(outer) == 2 and len(inner) == 2:
            far, near, side = outer[0], outer[1], inner[0]
            by_far = swap(block, n, far)
            right_own, copy = prepare(block, scale, used)
            near_own = swap(copy, n, near)
            side_own = swap(copy, n, side)
            near_far = swap(by_far, n, near)
            right_far, copy = prepare(by_far, scale, used)
            side_far = swap(copy, n, side)
            right_near, by_near = prepare(join(near_own, near_far[:used]), scale, used)
            last, side_own = fence((by_near, side_own))
            side_last = swap(last, n, side)
            right = join(right_own, right_far, right_near)
            mine = join(block[:used], by_far[:used], by_near)
            noise, mine = mine[-1:], mine[:-1]
            across = swap(mine, n, 1)
            my_applied = build(mine, noise * mine[feats:])
            my_applied = build(across, my_applied)
            side_last, side_far, my_applied = fence((side_last, side_far, my_applied))
            beside = join(side_own, side_far, side_last)
            noise_beside, beside = beside[-1:], beside[:-1]
            beside_across = swap(beside, n, 1)
            my_far = build(beside, jnp.zeros_like(my_applied))
            my_far = build(beside_across, my_far)
            my_applied = my_applied + my_far
            first = [mine, across, beside, beside_across]
            far_rows = [beside[:feats], beside_across[:feats]]
        else:
            mine = block
            for stride in outer:
                mine = join(mine, swap(mine, n, stride))
            mine = mine[:used]
            (right,), noise, first = prepare(mine, scale), mine[-1:], arrivals(mine[:-1])
            my_applied = noise * first[0][feats:]
            for x in first:
                my_applied = build(x, my_applied)
            my_far, far_rows = my_applied, []
        cols = noise.shape[1]
        starts = [x[feats:] for x in first]

        far_tile, right_far = [], None

        def exchange(x, direction):
            nonlocal right_far
            parts, passed = fence((parts_of(x), x))
            pieces, sent = [x, swap(passed, n, 1)], [x]
            near = fence(apply_parts(parts, tile[0]))
            near = fence(near + apply_piece(pieces[1], tile[1]))
            far = jnp.zeros_like(near) if len(inner) == 1 else None
            for k, stride in enumerate(inner[:-1]):
                arrived = swap(join(*sent), n, stride)
                if len(far_tile) < len(far_rows):
                    rows, columns, near = fence((far_rows[len(far_tile)], far_rows[0], near))
                    if right_far is None:
                        (right_far,) = prepare(columns, scale)
                    (piece,) = build_piece(rows, scale, right_far)
                    piece, right_far, near = fence((piece, right_far, near))
                    far_tile.append(piece)
                arrived, near = fence((arrived, near))
                sent.append(arrived)
                pieces.append(arrived)
                term = apply_piece(arrived, tile[2 + 2 * k])
                far = fence(term if far is None else far + term)
                pieces.append(swap(arrived, n, 1))
                if k < len(inner) - 2:
                    far = fence(far + apply_piece(pieces[-1], tile[3 + 2 * k]))
            before = join(*pieces[:-1])
            curve = jnp.sum(direction[:, : before.shape[1]] * before, axis=1)
            curve, far = fence((curve, far))
            curve = curve + jnp.sum(direction[:, before.shape[1] :] * pieces[-1], axis=1)
            if len(inner) > 1:
                far = far + apply_piece(pieces[-1], tile[-1])
            return collect(far), collect(near) + collect(far) + noise * x, join(*pieces), curve

        residual = direction = join(*starts)
        my_solution = jnp.zeros_like(direction[:, :width])
        norm_now = jnp.sum(residual * residual, axis=1)
        my_image, far_image = my_applied, my_far
        for iteration in range(ITERS - 1):
            far_next, my_next, applied, curve = exchange(my_applied, direction)
            step_size = (norm_now / curve)[:, None]
            my_solution = my_solution + step_size * direction[:, :width]
            residual = residual - step_size * applied
            norm_next = jnp.sum(residual * residual, axis=1)
            ratio = (norm_next / norm_now)[:, None]
            my_image = my_image - step_size * my_next
            my_applied = my_image + ratio * my_applied
            far_image = far_image - step_size * far_next
            my_far = far_image + ratio * my_far
            direction = residual + ratio * direction
            norm_now = norm_next
        mine = direction[:, :cols]
        if far_rows:
            side, beside = direction[:, 2 * cols : 3 * cols], direction[:, 3 * cols :]
            image = collect(apply_piece(side, far_tile[0]) + apply_piece(beside, far_tile[1])) + noise_beside * side
            curve = add_up(jnp.sum(mine * (my_applied + my_far) + side * image, axis=1), n, [1])
        else:
            curve = add_up(jnp.sum(mine * my_applied, axis=1), n, inner)
        step_size = (norm_now / curve)[:, None]
        my_solution = my_solution + step_size * direction[:, :width]
        return my_solution, residual[:, :width] - step_size * my_applied[:, :width]

    in_specs = (P("groups", "blk"), P("groups"), P(("groups", "blk")), P("groups", "blk"))
    out_specs = (P("groups", "blk"), P("groups", "blk"))
    return jax.shard_map(body, mesh=mesh, in_specs=in_specs, out_specs=out_specs, check_vma=False)
```

```python
import math

import jax
import jax.numpy as jnp
from jax import lax
from jax.experimental import pallas as pl
from jax.experimental.pallas import tpu as pltpu
from jax.sharding import PartitionSpec as P

ITERS = 4
TILE_BYTES = 16 << 20
VMEM_BYTES = 16 << 20
NORM_ROWS = 64
BUILD_ROWS = 1024
POINT_SCALE = math.sqrt(math.log2(math.e))


def swap(x, n, stride):
    return lax.ppermute(x, "blk", [(i, i ^ stride) for i in range(n)])


def add_up(x, n, strides):
    for stride in strides:
        x = x + swap(x, n, stride)
    return x


def split(x, parts):
    out = []
    for _ in range(parts):
        high = lax.reduce_precision(x, 8, 7)
        out.append(high.astype(jnp.bfloat16))
        x = x - high
    return out


def halve(x):
    high = x.astype(jnp.bfloat16)
    return high, x - high.astype(jnp.float32)


def operands(pts):
    high, rest = halve(pts)
    mid, rest = halve(rest)
    low = rest.astype(jnp.bfloat16)
    norms = -0.5 * jnp.sum(pts * pts, axis=0, keepdims=True)
    row = lax.broadcasted_iota(jnp.int32, (NORM_ROWS, pts.shape[1]), 0)
    left = jnp.where((row >= 3) & (row < 6), 1.0, 0.0)
    right = jnp.where(row < 3, 1.0, 0.0)
    for k in range(3):
        part, norms = halve(norms)
        part = part.astype(jnp.float32)
        left = jnp.where(row == k, part, left)
        right = jnp.where(row == 3 + k, part, right)
    left = jnp.concatenate([high, high, mid, high, low, mid, left.astype(jnp.bfloat16)], axis=0)
    right = jnp.concatenate([high, mid, high, low, high, mid, right.astype(jnp.bfloat16)], axis=0)
    return left, right


def prepare_kernel(part_ref, scale_ref, right_ref, *copy_ref):
    feats = scale_ref.shape[0]
    right_ref[...] = operands(part_ref[:feats] * scale_ref[...])[1]
    for ref in copy_ref:
        ref[...] = part_ref[: ref.shape[0]]


def build_kernel(rows_ref, scale_ref, right_ref, *refs):
    applies = len(refs) > 1
    vectors_ref, sum_ref, tile_ref, out_ref = refs if applies else (None, None, *refs, None)
    total, cols = rows_ref.shape[1], right_ref.shape[1]
    block, step = min(total, BUILD_ROWS), min(cols, 256)
    if applies:
        probes = vectors_ref.shape[0]
        high, rest = halve(vectors_ref[...])
        mid, rest = halve(rest)
        twice = jnp.concatenate([high, mid], axis=0)
        thrice = jnp.concatenate([high, mid, rest.astype(jnp.bfloat16)], axis=0)
    steps = [(top, at) for top in range(0, total, block) for at in range(0, cols, step)]
    lefts, powers, parts = {}, {}, {}

    def contract(top, at):
        if top not in lefts:
            lefts[top] = jnp.transpose(operands(rows_ref[:, top : top + block] * scale_ref[...])[0])
        powers[top, at] = jnp.dot(lefts[top], right_ref[:, at : at + step], preferred_element_type=jnp.float32)

    def raise_power(top, at):
        high, rest = halve(jnp.exp2(powers.pop((top, at))))
        low = rest.astype(jnp.bfloat16)
        tile_ref[top : top + block, at : at + step] = high
        tile_ref[total + top : total + top + block, at : at + step] = low
        parts[top, at] = high, low

    def apply(top, at):
        down, here = slice(top, top + block), slice(at, at + step)
        high, low = parts.pop((top, at))
        large = jnp.dot(thrice[:, down], high, preferred_element_type=jnp.float32)
        small = jnp.dot(twice[:, down], low, preferred_element_type=jnp.float32)
        term = large[:probes] + ((large[probes : 2 * probes] + small[:probes]) + (large[2 * probes :] + small[probes:]))
        before = sum_ref if top == 0 else out_ref
        out_ref[:, here] = before[:, here] + term

    contract(*steps[0])
    for k, chunk in enumerate(steps):
        if k + 1 < len(steps):
            contract(*steps[k + 1])
        raise_power(*chunk)
        if k and applies:
            apply(*steps[k - 1])
    if applies:
        apply(*steps[-1])


def call(kernel, outs, *args, **cost):
    whole = pl.BlockSpec(memory_space=pltpu.VMEM)
    return pl.pallas_call(
        kernel,
        out_shape=outs,
        in_specs=[whole] * len(args),
        out_specs=jax.tree.map(lambda _: whole, outs),
        compiler_params=pltpu.CompilerParams(vmem_limit_bytes=VMEM_BYTES),
        cost_estimate=pl.CostEstimate(**cost),
    )(*args)


def prepare(part, scale, copy=0):
    feats, cols = scale.shape[0], part.shape[1]
    outs = (jax.ShapeDtypeStruct((6 * feats + NORM_ROWS, cols), jnp.bfloat16),)
    if copy:
        outs += (jax.ShapeDtypeStruct((copy, cols), part.dtype),)
    return call(prepare_kernel, outs, part, scale, flops=10**0, bytes_accessed=feats * cols, transcendentals=0)


def join(*xs):
    return jnp.concatenate(xs, axis=1)


def build_piece(rows, scale, right, vectors=None, total=None):
    count, cols = rows.shape[1], right.shape[1]
    outs = (jax.ShapeDtypeStruct((2 * count, cols), jnp.bfloat16),)
    cost = dict(flops=2 * count * cols * 416, bytes_accessed=4 * count * cols, transcendentals=count * cols)
    args = (rows, scale, right)
    if vectors is not None:
        outs, args = (*outs, jax.ShapeDtypeStruct(total.shape, jnp.float32)), (*args, vectors, total)
    return call(build_kernel, outs, *args, **cost)


def parts_of(vectors):
    high, mid, low = split(vectors, 3)
    return jnp.concatenate([high, mid, low], axis=0)


def apply_parts(parts, piece):
    return jnp.dot(jnp.concatenate([parts, parts], axis=1), piece, preferred_element_type=jnp.float32)


def apply_piece(vectors, piece):
    return apply_parts(parts_of(vectors), piece)


def collect(total):
    probes = total.shape[0] // 3
    return total[:probes] + (total[probes : 2 * probes] + total[2 * probes :])


def solution(mesh):
    n = mesh.shape["blk"]
    strides = [1 << k for k in reversed(range(n.bit_length() - 1))]

    def body(points, lengthscale, noise_var, targets):
        feats, width = points.shape
        probes = targets.shape[0]
        team = min(n, 4)
        while team < n and (n * width) * (n * width) // team * 4 > TILE_BYTES:
            team *= 2
        outer, inner = [s for s in strides if s >= team], [s for s in strides if s < team]

        def arrivals(x):
            pieces, sent = [x, swap(x, n, 1)], [x]
            for stride in inner[:-1]:
                came = swap(sent[0] if len(sent) == 1 else jnp.concatenate(sent, axis=1), n, stride)
                sent.append(came)
                pieces += [came, swap(came, n, 1)]
            return pieces

        scale = (POINT_SCALE / lengthscale)[:, None]
        used = feats + probes + 1
        spare = points[: -used % 8]
        block = lax.optimization_barrier(jnp.concatenate([points, targets, noise_var[None, :], spare], axis=0))
        fence = lax.optimization_barrier
        tile = []

        def build(x, total):
            piece, total = build_piece(x[:feats], scale, right, x[feats:], total)
            tile.append(piece)
            return total

        if len(outer) == 2 and len(inner) == 2:
            far, near, side = outer[0], outer[1], inner[0]
            by_far = swap(block, n, far)
            right_own, copy = prepare(block, scale, used)
            near_own = swap(copy, n, near)
            side_own = swap(copy, n, side)
            near_far = swap(by_far, n, near)
            right_far, copy = prepare(by_far, scale, used)
            side_far = swap(copy, n, side)
            right_near, by_near = prepare(join(near_own, near_far[:used]), scale, used)
            last, side_own = fence((by_near, side_own))
            side_last = swap(last, n, side)
            right = join(right_own, right_far, right_near)
            mine = join(block[:used], by_far[:used], by_near)
            noise, mine = mine[-1:], mine[:-1]
            across = swap(mine, n, 1)
            my_applied = build(mine, noise * mine[feats:])
            my_applied = build(across, my_applied)
            side_last, side_far, my_applied = fence((side_last, side_far, my_applied))
            beside = join(side_own, side_far, side_last)
            noise_beside, beside = beside[-1:], beside[:-1]
            beside_across = swap(beside, n, 1)
            my_far = build(beside, jnp.zeros_like(my_applied))
            my_far = build(beside_across, my_far)
            my_applied = my_applied + my_far
            first = [mine, across, beside, beside_across]
            far_rows = [beside[:feats], beside_across[:feats]]
        else:
            mine = block
            for stride in outer:
                mine = join(mine, swap(mine, n, stride))
            mine = mine[:used]
            (right,), noise, first = prepare(mine, scale), mine[-1:], arrivals(mine[:-1])
            my_applied = noise * first[0][feats:]
            for x in first:
                my_applied = build(x, my_applied)
            my_far, far_rows = my_applied, []
        cols = noise.shape[1]
        starts = [x[feats:] for x in first]

        far_tile, right_far = [], None

        def exchange(x, direction):
            nonlocal right_far
            parts, passed = fence((parts_of(x), x))
            pieces, sent = [x, swap(passed, n, 1)], [x]
            near = fence(apply_parts(parts, tile[0]))
            near = fence(near + apply_piece(pieces[1], tile[1]))
            far = jnp.zeros_like(near) if len(inner) == 1 else None
            for k, stride in enumerate(inner[:-1]):
                arrived = swap(join(*sent), n, stride)
                if len(far_tile) < len(far_rows):
                    rows, columns, near = fence((far_rows[len(far_tile)], far_rows[0], near))
                    if right_far is None:
                        (right_far,) = prepare(columns, scale)
                    (piece,) = build_piece(rows, scale, right_far)
                    piece, right_far, near = fence((piece, right_far, near))
                    far_tile.append(piece)
                arrived, near = fence((arrived, near))
                sent.append(arrived)
                pieces.append(arrived)
                term = apply_piece(arrived, tile[2 + 2 * k])
                far = fence(term if far is None else far + term)
                pieces.append(swap(arrived, n, 1))
                if k < len(inner) - 2:
                    far = fence(far + apply_piece(pieces[-1], tile[3 + 2 * k]))
            before = join(*pieces[:-1])
            curve = jnp.sum(direction[:, : before.shape[1]] * before, axis=1)
            curve, far = fence((curve, far))
            curve = curve + jnp.sum(direction[:, before.shape[1] :] * pieces[-1], axis=1)
            if len(inner) > 1:
                far = far + apply_piece(pieces[-1], tile[-1])
            return collect(far), collect(near) + collect(far) + noise * x, join(*pieces), curve

        residual = direction = join(*starts)
        my_solution = jnp.zeros_like(direction[:, :width])
        norm_now = jnp.sum(residual * residual, axis=1)
        my_image, far_image = my_applied, my_far
        for iteration in range(ITERS - 1):
            far_next, my_next, applied, curve = exchange(my_applied, direction)
            step_size = (norm_now / curve)[:, None]
            my_solution = my_solution + step_size * direction[:, :width]
            residual = residual - step_size * applied
            norm_next = jnp.sum(residual * residual, axis=1)
            ratio = (norm_next / norm_now)[:, None]
            my_image = my_image - step_size * my_next
            my_applied = my_image + ratio * my_applied
            far_image = far_image - step_size * far_next
            my_far = far_image + ratio * my_far
            direction = residual + ratio * direction
            norm_now = norm_next
        mine = direction[:, :cols]
        if far_rows:
            side, beside = direction[:, 2 * cols : 3 * cols], direction[:, 3 * cols :]
            image = collect(apply_piece(side, far_tile[0]) + apply_piece(beside, far_tile[1])) + noise_beside * side
            curve = add_up(jnp.sum(mine * (my_applied + my_far) + side * image, axis=1), n, [1])
        else:
            curve = add_up(jnp.sum(mine * my_applied, axis=1), n, inner)
        step_size = (norm_now / curve)[:, None]
        my_solution = my_solution + step_size * direction[:, :width]
        return my_solution, residual[:, :width] - step_size * my_applied[:, :width]

    in_specs = (P("groups", "blk"), P("groups"), P(("groups", "blk")), P("groups", "blk"))
    out_specs = (P("groups", "blk"), P("groups", "blk"))
    return jax.shard_map(body, mesh=mesh, in_specs=in_specs, out_specs=out_specs, check_vma=False)
```

```python
import math

import jax
import jax.numpy as jnp
from jax import lax
from jax.experimental import pallas as pl
from jax.experimental.pallas import tpu as pltpu
from jax.sharding import PartitionSpec as P

ITERS = 4
TILE_BYTES = 16 << 20
VMEM_BYTES = 16 << 20
NORM_ROWS = 64
BUILD_ROWS = 1024
POINT_SCALE = math.sqrt(math.log2(math.e))


def swap(x, n, stride):
    return lax.ppermute(x, "blk", [(i, i ^ stride) for i in range(n)])


def add_up(x, n, strides):
    for stride in strides:
        x = x + swap(x, n, stride)
    return x


def split(x, parts):
    out = []
    for _ in range(parts):
        high = lax.reduce_precision(x, 8, 7)
        out.append(high.astype(jnp.bfloat16))
        x = x - high
    return out


def halve(x):
    high = x.astype(jnp.bfloat16)
    return high, x - high.astype(jnp.float32)


def operands(pts):
    high, rest = halve(pts)
    mid, rest = halve(rest)
    low = rest.astype(jnp.bfloat16)
    norms = -0.5 * jnp.sum(pts * pts, axis=0, keepdims=True)
    row = lax.broadcasted_iota(jnp.int32, (NORM_ROWS, pts.shape[1]), 0)
    left = jnp.where((row >= 3) & (row < 6), 1.0, 0.0)
    right = jnp.where(row < 3, 1.0, 0.0)
    for k in range(3):
        part, norms = halve(norms)
        part = part.astype(jnp.float32)
        left = jnp.where(row == k, part, left)
        right = jnp.where(row == 3 + k, part, right)
    left = jnp.concatenate([high, high, mid, high, low, mid, left.astype(jnp.bfloat16)], axis=0)
    right = jnp.concatenate([high, mid, high, low, high, mid, right.astype(jnp.bfloat16)], axis=0)
    return left, right


def prepare_kernel(part_ref, scale_ref, right_ref, *copy_ref):
    feats = scale_ref.shape[0]
    right_ref[...] = operands(part_ref[:feats] * scale_ref[...])[1]
    for ref in copy_ref:
        ref[...] = part_ref[: ref.shape[0]]


def build_kernel(rows_ref, scale_ref, right_ref, *refs):
    applies = len(refs) > 1
    vectors_ref, sum_ref, tile_ref, out_ref = refs if applies else (None, None, *refs, None)
    total, cols = rows_ref.shape[1], right_ref.shape[1]
    block, step = min(total, BUILD_ROWS), min(cols, 256)
    if applies:
        probes = vectors_ref.shape[0]
        high, rest = halve(vectors_ref[...])
        mid, rest = halve(rest)
        twice = jnp.concatenate([high, mid], axis=0)
        thrice = jnp.concatenate([high, mid, rest.astype(jnp.bfloat16)], axis=0)
    steps = [(top, at) for top in range(0, total, block) for at in range(0, cols, step)]
    lefts, powers, parts = {}, {}, {}

    def contract(top, at):
        if top not in lefts:
            lefts[top] = jnp.transpose(operands(rows_ref[:, top : top + block] * scale_ref[...])[0])
        powers[top, at] = jnp.dot(lefts[top], right_ref[:, at : at + step], preferred_element_type=jnp.float32)

    def raise_power(top, at):
        high, rest = halve(jnp.exp2(powers.pop((top, at))))
        low = rest.astype(jnp.bfloat16)
        tile_ref[top : top + block, at : at + step] = high
        tile_ref[total + top : total + top + block, at : at + step] = low
        parts[top, at] = high, low

    def apply(top, at):
        down, here = slice(top, top + block), slice(at, at + step)
        high, low = parts.pop((top, at))
        large = jnp.dot(thrice[:, down], high, preferred_element_type=jnp.float32)
        small = jnp.dot(twice[:, down], low, preferred_element_type=jnp.float32)
        term = large[:probes] + ((large[probes : 2 * probes] + small[:probes]) + (large[2 * probes :] + small[probes:]))
        before = sum_ref if top == 0 else out_ref
        out_ref[:, here] = before[:, here] + term

    contract(*steps[0])
    for k, chunk in enumerate(steps):
        if k + 1 < len(steps):
            contract(*steps[k + 1])
        raise_power(*chunk)
        if k and applies:
            apply(*steps[k - 1])
    if applies:
        apply(*steps[-1])


def call(kernel, outs, *args, **cost):
    whole = pl.BlockSpec(memory_space=pltpu.VMEM)
    return pl.pallas_call(
        kernel,
        out_shape=outs,
        in_specs=[whole] * len(args),
        out_specs=jax.tree.map(lambda _: whole, outs),
        compiler_params=pltpu.CompilerParams(vmem_limit_bytes=VMEM_BYTES),
        cost_estimate=pl.CostEstimate(**cost),
    )(*args)


def prepare(part, scale, copy=0):
    feats, cols = scale.shape[0], part.shape[1]
    outs = (jax.ShapeDtypeStruct((6 * feats + NORM_ROWS, cols), jnp.bfloat16),)
    if copy:
        outs += (jax.ShapeDtypeStruct((copy, cols), part.dtype),)
    return call(prepare_kernel, outs, part, scale, flops=10**0, bytes_accessed=feats * cols, transcendentals=0)


def join(*xs):
    return jnp.concatenate(xs, axis=1)


def build_piece(rows, scale, right, vectors=None, total=None):
    count, cols = rows.shape[1], right.shape[1]
    outs = (jax.ShapeDtypeStruct((2 * count, cols), jnp.bfloat16),)
    cost = dict(flops=2 * count * cols * 416, bytes_accessed=4 * count * cols, transcendentals=count * cols)
    args = (rows, scale, right)
    if vectors is not None:
        outs, args = (*outs, jax.ShapeDtypeStruct(total.shape, jnp.float32)), (*args, vectors, total)
    return call(build_kernel, outs, *args, **cost)


def parts_of(vectors):
    high, mid, low = split(vectors, 3)
    return jnp.concatenate([high, mid, low], axis=0)


def apply_parts(parts, piece):
    return jnp.dot(jnp.concatenate([parts, parts], axis=1), piece, preferred_element_type=jnp.float32)


def apply_piece(vectors, piece):
    return apply_parts(parts_of(vectors), piece)


def collect(total):
    probes = total.shape[0] // 3
    return total[:probes] + (total[probes : 2 * probes] + total[2 * probes :])


def solution(mesh):
    n = mesh.shape["blk"]
    strides = [1 << k for k in reversed(range(n.bit_length() - 1))]

    def body(points, lengthscale, noise_var, targets):
        feats, width = points.shape
        probes = targets.shape[0]
        team = min(n, 4)
        while team < n and (n * width) * (n * width) // team * 4 > TILE_BYTES:
            team *= 2
        outer, inner = [s for s in strides if s >= team], [s for s in strides if s < team]

        def arrivals(x):
            pieces, sent = [x, swap(x, n, 1)], [x]
            for stride in inner[:-1]:
                came = swap(sent[0] if len(sent) == 1 else jnp.concatenate(sent, axis=1), n, stride)
                sent.append(came)
                pieces += [came, swap(came, n, 1)]
            return pieces

        scale = (POINT_SCALE / lengthscale)[:, None]
        used = feats + probes + 1
        spare = jnp.zeros((-used % 8, width), jnp.float32)
        block = lax.optimization_barrier(jnp.concatenate([points, targets, jnp.pad(noise_var[None, :], ((0, -used % 8), (0, 0)))], axis=0))
        fence = lax.optimization_barrier
        tile = []

        def build(x, total):
            piece, total = build_piece(x[:feats], scale, right, x[feats:], total)
            tile.append(piece)
            return total

        if len(outer) == 2 and len(inner) == 2:
            far, near, side = outer[0], outer[1], inner[0]
            by_far = swap(block, n, far)
            right_own, copy = prepare(block, scale, used)
            near_own = swap(copy, n, near)
            side_own = swap(copy, n, side)
            near_far = swap(by_far, n, near)
            right_far, copy = prepare(by_far, scale, used)
            side_far = swap(copy, n, side)
            right_near, by_near = prepare(join(near_own, near_far[:used]), scale, used)
            last, side_own = fence((by_near, side_own))
            side_last = swap(last, n, side)
            right = join(right_own, right_far, right_near)
            mine = join(block[:used], by_far[:used], by_near)
            noise, mine = mine[-1:], mine[:-1]
            across = swap(mine, n, 1)
            my_applied = build(mine, noise * mine[feats:])
            my_applied = build(across, my_applied)
            side_last, side_far, my_applied = fence((side_last, side_far, my_applied))
            beside = join(side_own, side_far, side_last)
            noise_beside, beside = beside[-1:], beside[:-1]
            beside_across = swap(beside, n, 1)
            my_far = build(beside, jnp.zeros_like(my_applied))
            my_far = build(beside_across, my_far)
            my_applied = my_applied + my_far
            first = [mine, across, beside, beside_across]
            far_rows = [beside[:feats], beside_across[:feats]]
        else:
            mine = block
            for stride in outer:
                mine = join(mine, swap(mine, n, stride))
            mine = mine[:used]
            (right,), noise, first = prepare(mine, scale), mine[-1:], arrivals(mine[:-1])
            my_applied = noise * first[0][feats:]
            for x in first:
                my_applied = build(x, my_applied)
            my_far, far_rows = my_applied, []
        cols = noise.shape[1]
        starts = [x[feats:] for x in first]

        far_tile, right_far = [], None

        def exchange(x, direction):
            nonlocal right_far
            parts, passed = fence((parts_of(x), x))
            pieces, sent = [x, swap(passed, n, 1)], [x]
            near = fence(apply_parts(parts, tile[0]))
            near = fence(near + apply_piece(pieces[1], tile[1]))
            far = jnp.zeros_like(near) if len(inner) == 1 else None
            for k, stride in enumerate(inner[:-1]):
                arrived = swap(join(*sent), n, stride)
                if len(far_tile) < len(far_rows):
                    rows, columns, near = fence((far_rows[len(far_tile)], far_rows[0], near))
                    if right_far is None:
                        (right_far,) = prepare(columns, scale)
                    (piece,) = build_piece(rows, scale, right_far)
                    piece, right_far, near = fence((piece, right_far, near))
                    far_tile.append(piece)
                arrived, near = fence((arrived, near))
                sent.append(arrived)
                pieces.append(arrived)
                term = apply_piece(arrived, tile[2 + 2 * k])
                far = fence(term if far is None else far + term)
                pieces.append(swap(arrived, n, 1))
                if k < len(inner) - 2:
                    far = fence(far + apply_piece(pieces[-1], tile[3 + 2 * k]))
            before = join(*pieces[:-1])
            curve = jnp.sum(direction[:, : before.shape[1]] * before, axis=1)
            curve, far = fence((curve, far))
            curve = curve + jnp.sum(direction[:, before.shape[1] :] * pieces[-1], axis=1)
            if len(inner) > 1:
                far = far + apply_piece(pieces[-1], tile[-1])
            return collect(far), collect(near) + collect(far) + noise * x, join(*pieces), curve

        residual = direction = join(*starts)
        my_solution = jnp.zeros_like(direction[:, :width])
        norm_now = jnp.sum(residual * residual, axis=1)
        my_image, far_image = my_applied, my_far
        for iteration in range(ITERS - 1):
            far_next, my_next, applied, curve = exchange(my_applied, direction)
            step_size = (norm_now / curve)[:, None]
            my_solution = my_solution + step_size * direction[:, :width]
            residual = residual - step_size * applied
            norm_next = jnp.sum(residual * residual, axis=1)
            ratio = (norm_next / norm_now)[:, None]
            my_image = my_image - step_size * my_next
            my_applied = my_image + ratio * my_applied
            far_image = far_image - step_size * far_next
            my_far = far_image + ratio * my_far
            direction = residual + ratio * direction
            norm_now = norm_next
        mine = direction[:, :cols]
        if far_rows:
            side, beside = direction[:, 2 * cols : 3 * cols], direction[:, 3 * cols :]
            image = collect(apply_piece(side, far_tile[0]) + apply_piece(beside, far_tile[1])) + noise_beside * side
            curve = add_up(jnp.sum(mine * (my_applied + my_far) + side * image, axis=1), n, [1])
        else:
            curve = add_up(jnp.sum(mine * my_applied, axis=1), n, inner)
        step_size = (norm_now / curve)[:, None]
        my_solution = my_solution + step_size * direction[:, :width]
        return my_solution, residual[:, :width] - step_size * my_applied[:, :width]

    in_specs = (P("groups", "blk"), P("groups"), P(("groups", "blk")), P("groups", "blk"))
    out_specs = (P("groups", "blk"), P("groups", "blk"))
    return jax.shard_map(body, mesh=mesh, in_specs=in_specs, out_specs=out_specs, check_vma=False)
```

```python
import math

import jax
import jax.numpy as jnp
from jax import lax
from jax.experimental import pallas as pl
from jax.experimental.pallas import tpu as pltpu
from jax.sharding import PartitionSpec as P

ITERS = 4
TILE_BYTES = 16 << 20
VMEM_BYTES = 16 << 20
NORM_ROWS = 64
BUILD_ROWS = 1024
POINT_SCALE = math.sqrt(math.log2(math.e))


def swap(x, n, stride):
    return lax.ppermute(x, "blk", [(i, i ^ stride) for i in range(n)])


def add_up(x, n, strides):
    for stride in strides:
        x = x + swap(x, n, stride)
    return x


def split(x, parts):
    out = []
    for _ in range(parts):
        high = lax.reduce_precision(x, 8, 7)
        out.append(high.astype(jnp.bfloat16))
        x = x - high
    return out


def halve(x):
    high = x.astype(jnp.bfloat16)
    return high, x - high.astype(jnp.float32)


def operands(pts):
    high, rest = halve(pts)
    mid, rest = halve(rest)
    low = rest.astype(jnp.bfloat16)
    norms = -0.5 * jnp.sum(pts * pts, axis=0, keepdims=True)
    row = lax.broadcasted_iota(jnp.int32, (NORM_ROWS, pts.shape[1]), 0)
    left = jnp.where((row >= 3) & (row < 6), 1.0, 0.0)
    right = jnp.where(row < 3, 1.0, 0.0)
    for k in range(3):
        part, norms = halve(norms)
        part = part.astype(jnp.float32)
        left = jnp.where(row == k, part, left)
        right = jnp.where(row == 3 + k, part, right)
    left = jnp.concatenate([high, high, mid, high, low, mid, left.astype(jnp.bfloat16)], axis=0)
    right = jnp.concatenate([high, mid, high, low, high, mid, right.astype(jnp.bfloat16)], axis=0)
    return left, right


def prepare_kernel(part_ref, scale_ref, right_ref, *copy_ref):
    feats = scale_ref.shape[0]
    right_ref[...] = operands(part_ref[:feats] * scale_ref[...])[1]
    for ref in copy_ref:
        ref[...] = part_ref[: ref.shape[0]]


def build_kernel(rows_ref, scale_ref, right_ref, *refs):
    applies = len(refs) > 1
    vectors_ref, sum_ref, tile_ref, out_ref = refs if applies else (None, None, *refs, None)
    total, cols = rows_ref.shape[1], right_ref.shape[1]
    block, step = min(total, BUILD_ROWS), min(cols, 256)
    if applies:
        probes = vectors_ref.shape[0]
        high, rest = halve(vectors_ref[...])
        mid, rest = halve(rest)
        twice = jnp.concatenate([high, mid], axis=0)
        thrice = jnp.concatenate([high, mid, rest.astype(jnp.bfloat16)], axis=0)
    steps = [(top, at) for top in range(0, total, block) for at in range(0, cols, step)]
    lefts, powers, parts = {}, {}, {}

    def contract(top, at):
        if top not in lefts:
            lefts[top] = jnp.transpose(operands(rows_ref[:, top : top + block] * scale_ref[...])[0])
        powers[top, at] = jnp.dot(lefts[top], right_ref[:, at : at + step], preferred_element_type=jnp.float32)

    def raise_power(top, at):
        high, rest = halve(jnp.exp2(powers.pop((top, at))))
        low = rest.astype(jnp.bfloat16)
        tile_ref[top : top + block, at : at + step] = high
        tile_ref[total + top : total + top + block, at : at + step] = low
        parts[top, at] = high, low

    def apply(top, at):
        down, here = slice(top, top + block), slice(at, at + step)
        high, low = parts.pop((top, at))
        large = jnp.dot(thrice[:, down], high, preferred_element_type=jnp.float32)
        small = jnp.dot(twice[:, down], low, preferred_element_type=jnp.float32)
        term = large[:probes] + ((large[probes : 2 * probes] + small[:probes]) + (large[2 * probes :] + small[probes:]))
        before = sum_ref if top == 0 else out_ref
        out_ref[:, here] = before[:, here] + term

    contract(*steps[0])
    for k, chunk in enumerate(steps):
        if k + 1 < len(steps):
            contract(*steps[k + 1])
        raise_power(*chunk)
        if k and applies:
            apply(*steps[k - 1])
    if applies:
        apply(*steps[-1])


def call(kernel, outs, *args, **cost):
    whole = pl.BlockSpec(memory_space=pltpu.VMEM)
    return pl.pallas_call(
        kernel,
        out_shape=outs,
        in_specs=[whole] * len(args),
        out_specs=jax.tree.map(lambda _: whole, outs),
        compiler_params=pltpu.CompilerParams(vmem_limit_bytes=VMEM_BYTES),
        cost_estimate=pl.CostEstimate(**cost),
    )(*args)


def prepare(part, scale, copy=0):
    feats, cols = scale.shape[0], part.shape[1]
    outs = (jax.ShapeDtypeStruct((6 * feats + NORM_ROWS, cols), jnp.bfloat16),)
    if copy:
        outs += (jax.ShapeDtypeStruct((copy, cols), part.dtype),)
    return call(prepare_kernel, outs, part, scale, flops=10**0, bytes_accessed=feats * cols, transcendentals=0)


def join(*xs):
    return jnp.concatenate(xs, axis=1)


def build_piece(rows, scale, right, vectors=None, total=None):
    count, cols = rows.shape[1], right.shape[1]
    outs = (jax.ShapeDtypeStruct((2 * count, cols), jnp.bfloat16),)
    cost = dict(flops=2 * count * cols * 416, bytes_accessed=4 * count * cols, transcendentals=count * cols)
    args = (rows, scale, right)
    if vectors is not None:
        outs, args = (*outs, jax.ShapeDtypeStruct(total.shape, jnp.float32)), (*args, vectors, total)
    return call(build_kernel, outs, *args, **cost)


def parts_of(vectors):
    high, mid, low = split(vectors, 3)
    return jnp.concatenate([high, mid, low], axis=0)


def apply_parts(parts, piece):
    return jnp.dot(jnp.concatenate([parts, parts], axis=1), piece, preferred_element_type=jnp.float32)


def apply_piece(vectors, piece):
    return apply_parts(parts_of(vectors), piece)


def collect(total):
    probes = total.shape[0] // 3
    return total[:probes] + (total[probes : 2 * probes] + total[2 * probes :])


def solution(mesh):
    n = mesh.shape["blk"]
    strides = [1 << k for k in reversed(range(n.bit_length() - 1))]

    def body(points, lengthscale, noise_var, targets):
        feats, width = points.shape
        probes = targets.shape[0]
        team = min(n, 4)
        while team < n and (n * width) * (n * width) // team * 4 > TILE_BYTES:
            team *= 2
        outer, inner = [s for s in strides if s >= team], [s for s in strides if s < team]

        def arrivals(x):
            pieces, sent = [x, swap(x, n, 1)], [x]
            for stride in inner[:-1]:
                came = swap(sent[0] if len(sent) == 1 else jnp.concatenate(sent, axis=1), n, stride)
                sent.append(came)
                pieces += [came, swap(came, n, 1)]
            return pieces

        scale = (POINT_SCALE / lengthscale)[:, None]
        used = feats + probes + 1
        spare = jnp.zeros((-used % 8, width), jnp.float32)
        block = lax.optimization_barrier(jnp.concatenate([points, targets, jnp.pad(noise_var[None, :], ((0, -used % 8), (0, 0)))], axis=0))
        fence = lax.optimization_barrier
        tile = []

        def build(x, total, right):
            piece, total = build_piece(x[:feats], scale, right, x[feats:], total)
            tile.append(piece)
            return total

        if len(outer) == 2 and len(inner) == 2:
            far, near, side = outer[0], outer[1], inner[0]
            by_far = swap(block, n, far)
            right_own, copy = prepare(block, scale, used)
            near_own = swap(copy, n, near)
            side_own = swap(copy, n, side)
            near_far = swap(by_far, n, near)
            right_far, copy = prepare(by_far, scale, used)
            side_far = swap(copy, n, side)
            right_near, by_near = prepare(join(near_own, near_far[:used]), scale, used)
            last, side_own = fence((by_near, side_own))
            side_last = swap(last, n, side)
            right = join(right_own, right_far, right_near)
            mine = join(block[:used], by_far[:used], by_near)
            noise, mine = mine[-1:], mine[:-1]
            across = swap(mine, n, 1)
            zeros = jnp.zeros((probes, mine.shape[1]), jnp.float32)
            near_own = build(mine, noise * mine[feats:], right)
            across, near_own = fence((across, near_own))
            (right_across,) = prepare(across, scale)
            near_other = build(mine, zeros, right_across)
            near_came = swap(near_other, n, 1)
            side_last, side_far, near_other = fence((side_last, side_far, near_other))
            beside = join(side_own, side_far, side_last)
            noise_beside, beside = beside[-1:], beside[:-1]
            beside_across = swap(beside, n, 1)
            far_other = build(beside, zeros, right_across)
            far_came = swap(far_other, n, 1)
            far_own = build(beside, zeros, right)
            far_came, near_came, far_own = fence((far_came, near_came, far_own))
            my_far = far_own + far_came
            my_applied = near_own + near_came + my_far
            first = [mine, across, beside, beside_across]
            far_rows = [beside[:feats], beside_across[:feats]]
        else:
            mine = block
            for stride in outer:
                mine = join(mine, swap(mine, n, stride))
            mine = mine[:used]
            (right,), noise, first = prepare(mine, scale), mine[-1:], arrivals(mine[:-1])
            my_applied = noise * first[0][feats:]
            for x in first:
                my_applied = build(x, my_applied, right)
            my_far, far_rows = my_applied, []
        cols = noise.shape[1]
        starts = [x[feats:] for x in first]

        far_tile, right_far = [], None

        def exchange(x, direction):
            nonlocal right_far
            parts, passed = fence((parts_of(x), x))
            pieces, sent = [x, swap(passed, n, 1)], [x]
            near = fence(apply_parts(parts, tile[0]))
            near = fence(near + apply_piece(pieces[1], tile[1]))
            far = jnp.zeros_like(near) if len(inner) == 1 else None
            for k, stride in enumerate(inner[:-1]):
                arrived = swap(join(*sent), n, stride)
                if len(far_tile) < len(far_rows):
                    rows, columns, near = fence((far_rows[len(far_tile)], far_rows[0], near))
                    if right_far is None:
                        (right_far,) = prepare(columns, scale)
                    (piece,) = build_piece(rows, scale, right_far)
                    piece, right_far, near = fence((piece, right_far, near))
                    far_tile.append(piece)
                arrived, near = fence((arrived, near))
                sent.append(arrived)
                pieces.append(arrived)
                term = apply_piece(arrived, tile[2 + 2 * k])
                far = fence(term if far is None else far + term)
                pieces.append(swap(arrived, n, 1))
                if k < len(inner) - 2:
                    far = fence(far + apply_piece(pieces[-1], tile[3 + 2 * k]))
            before = join(*pieces[:-1])
            curve = jnp.sum(direction[:, : before.shape[1]] * before, axis=1)
            curve, far = fence((curve, far))
            curve = curve + jnp.sum(direction[:, before.shape[1] :] * pieces[-1], axis=1)
            if len(inner) > 1:
                far = far + apply_piece(pieces[-1], tile[-1])
            return collect(far), collect(near) + collect(far) + noise * x, join(*pieces), curve

        def exchange_sums(x, direction):
            nonlocal right_far
            arrived = swap(x, n, inner[0])
            parts, passed = fence((parts_of(x), x))
            across = swap(passed, n, 1)
            near_other = collect(apply_parts(parts, tile[1]))
            near_came = swap(near_other, n, 1)
            parts, near_other = fence((parts, near_other))
            near_own = apply_parts(parts, tile[0])
            if len(far_tile) < len(far_rows):
                rows, columns, near_own = fence((far_rows[len(far_tile)], far_rows[0], near_own))
                if right_far is None:
                    (right_far,) = prepare(columns, scale)
                (piece,) = build_piece(rows, scale, right_far)
                piece, right_far, near_own = fence((piece, right_far, near_own))
                far_tile.append(piece)
            arrived, near_own = fence((arrived, near_own))
            arrived_across = swap(arrived, n, 1)
            parts = parts_of(arrived)
            far_other = collect(apply_parts(parts, tile[2]))
            far_came = swap(far_other, n, 1)
            parts, far_other = fence((parts, far_other))
            far_own = apply_parts(parts, tile[3])
            before = join(x, across, arrived)
            curve = jnp.sum(direction[:, : before.shape[1]] * before, axis=1)
            curve, far_own, arrived_across = fence((curve, far_own, arrived_across))
            curve = curve + jnp.sum(direction[:, before.shape[1] :] * arrived_across, axis=1)
            far = collect(far_own) + far_came
            return far, collect(near_own) + near_came + far + noise * x, join(before, arrived_across), curve

        residual = direction = join(*starts)
        my_solution = jnp.zeros_like(direction[:, :width])
        norm_now = jnp.sum(residual * residual, axis=1)
        my_image, far_image = my_applied, my_far
        for iteration in range(ITERS - 1):
            far_next, my_next, applied, curve = (exchange_sums if far_rows else exchange)(my_applied, direction)
            step_size = (norm_now / curve)[:, None]
            my_solution = my_solution + step_size * direction[:, :width]
            residual = residual - step_size * applied
            norm_next = jnp.sum(residual * residual, axis=1)
            ratio = (norm_next / norm_now)[:, None]
            my_image = my_image - step_size * my_next
            my_applied = my_image + ratio * my_applied
            far_image = far_image - step_size * far_next
            my_far = far_image + ratio * my_far
            direction = residual + ratio * direction
            norm_now = norm_next
        mine = direction[:, :cols]
        if far_rows:
            side, beside = direction[:, 2 * cols : 3 * cols], direction[:, 3 * cols :]
            image = collect(apply_piece(side, far_tile[0]) + apply_piece(beside, far_tile[1])) + noise_beside * side
            curve = add_up(jnp.sum(mine * (my_applied + my_far) + side * image, axis=1), n, [1])
        else:
            curve = add_up(jnp.sum(mine * my_applied, axis=1), n, inner)
        step_size = (norm_now / curve)[:, None]
        my_solution = my_solution + step_size * direction[:, :width]
        return my_solution, residual[:, :width] - step_size * my_applied[:, :width]

    in_specs = (P("groups", "blk"), P("groups"), P(("groups", "blk")), P("groups", "blk"))
    out_specs = (P("groups", "blk"), P("groups", "blk"))
    return jax.shard_map(body, mesh=mesh, in_specs=in_specs, out_specs=out_specs, check_vma=False)
```

```python
import math

import jax
import jax.numpy as jnp
from jax import lax
from jax.experimental import pallas as pl
from jax.experimental.pallas import tpu as pltpu
from jax.sharding import PartitionSpec as P

ITERS = 4
TILE_BYTES = 16 << 20
VMEM_BYTES = 16 << 20
NORM_ROWS = 64
BUILD_ROWS = 1024
POINT_SCALE = math.sqrt(math.log2(math.e))


def swap(x, n, stride):
    return lax.ppermute(x, "blk", [(i, i ^ stride) for i in range(n)])


def add_up(x, n, strides):
    for stride in strides:
        x = x + swap(x, n, stride)
    return x


def split(x, parts):
    out = []
    for _ in range(parts):
        high = lax.reduce_precision(x, 8, 7)
        out.append(high.astype(jnp.bfloat16))
        x = x - high
    return out


def halve(x):
    high = x.astype(jnp.bfloat16)
    return high, x - high.astype(jnp.float32)


def operands(pts):
    high, rest = halve(pts)
    mid, rest = halve(rest)
    low = rest.astype(jnp.bfloat16)
    norms = -0.5 * jnp.sum(pts * pts, axis=0, keepdims=True)
    row = lax.broadcasted_iota(jnp.int32, (NORM_ROWS, pts.shape[1]), 0)
    left = jnp.where((row >= 3) & (row < 6), 1.0, 0.0)
    right = jnp.where(row < 3, 1.0, 0.0)
    for k in range(3):
        part, norms = halve(norms)
        part = part.astype(jnp.float32)
        left = jnp.where(row == k, part, left)
        right = jnp.where(row == 3 + k, part, right)
    left = jnp.concatenate([high, high, mid, high, low, mid, left.astype(jnp.bfloat16)], axis=0)
    right = jnp.concatenate([high, mid, high, low, high, mid, right.astype(jnp.bfloat16)], axis=0)
    return left, right


def prepare_kernel(part_ref, scale_ref, right_ref, *copy_ref):
    feats = scale_ref.shape[0]
    right_ref[...] = operands(part_ref[:feats] * scale_ref[...])[1]
    for ref in copy_ref:
        ref[...] = part_ref[: ref.shape[0]]


def build_kernel(rows_ref, scale_ref, right_ref, *refs):
    applies = len(refs) > 1
    vectors_ref, sum_ref, tile_ref, out_ref = refs if applies else (None, None, *refs, None)
    total, cols = rows_ref.shape[1], right_ref.shape[1]
    block, step = min(total, BUILD_ROWS), min(cols, 256)
    if applies:
        probes = vectors_ref.shape[0]
        high, rest = halve(vectors_ref[...])
        mid, rest = halve(rest)
        twice = jnp.concatenate([high, mid], axis=0)
        thrice = jnp.concatenate([high, mid, rest.astype(jnp.bfloat16)], axis=0)
    steps = [(top, at) for top in range(0, total, block) for at in range(0, cols, step)]
    lefts, powers, parts = {}, {}, {}

    def contract(top, at):
        if top not in lefts:
            lefts[top] = jnp.transpose(operands(rows_ref[:, top : top + block] * scale_ref[...])[0])
        powers[top, at] = jnp.dot(lefts[top], right_ref[:, at : at + step], preferred_element_type=jnp.float32)

    def raise_power(top, at):
        high, rest = halve(jnp.exp2(powers.pop((top, at))))
        low = rest.astype(jnp.bfloat16)
        tile_ref[top : top + block, at : at + step] = high
        tile_ref[total + top : total + top + block, at : at + step] = low
        parts[top, at] = high, low

    def apply(top, at):
        down, here = slice(top, top + block), slice(at, at + step)
        high, low = parts.pop((top, at))
        large = jnp.dot(thrice[:, down], high, preferred_element_type=jnp.float32)
        small = jnp.dot(twice[:, down], low, preferred_element_type=jnp.float32)
        term = large[:probes] + ((large[probes : 2 * probes] + small[:probes]) + (large[2 * probes :] + small[probes:]))
        before = sum_ref if top == 0 else out_ref
        out_ref[:, here] = before[:, here] + term

    contract(*steps[0])
    for k, chunk in enumerate(steps):
        if k + 1 < len(steps):
            contract(*steps[k + 1])
        raise_power(*chunk)
        if k and applies:
            apply(*steps[k - 1])
    if applies:
        apply(*steps[-1])


def call(kernel, outs, *args, **cost):
    whole = pl.BlockSpec(memory_space=pltpu.VMEM)
    return pl.pallas_call(
        kernel,
        out_shape=outs,
        in_specs=[whole] * len(args),
        out_specs=jax.tree.map(lambda _: whole, outs),
        compiler_params=pltpu.CompilerParams(vmem_limit_bytes=VMEM_BYTES),
        cost_estimate=pl.CostEstimate(**cost),
    )(*args)


def prepare(part, scale, copy=0):
    feats, cols = scale.shape[0], part.shape[1]
    outs = (jax.ShapeDtypeStruct((6 * feats + NORM_ROWS, cols), jnp.bfloat16),)
    if copy:
        outs += (jax.ShapeDtypeStruct((copy, cols), part.dtype),)
    return call(prepare_kernel, outs, part, scale, flops=10**0, bytes_accessed=feats * cols, transcendentals=0)


def join(*xs):
    return jnp.concatenate(xs, axis=1)


def build_piece(rows, scale, right, vectors=None, total=None):
    count, cols = rows.shape[1], right.shape[1]
    outs = (jax.ShapeDtypeStruct((2 * count, cols), jnp.bfloat16),)
    cost = dict(flops=2 * count * cols * 416, bytes_accessed=4 * count * cols, transcendentals=count * cols)
    args = (rows, scale, right)
    if vectors is not None:
        outs, args = (*outs, jax.ShapeDtypeStruct(total.shape, jnp.float32)), (*args, vectors, total)
    return call(build_kernel, outs, *args, **cost)


def stack(vectors):
    return jnp.concatenate([parts_of(x) for x in vectors], axis=0)


def parts_of(vectors):
    high, mid, low = split(vectors, 3)
    return jnp.concatenate([high, mid, low], axis=0)


def apply_parts(parts, piece):
    return jnp.dot(jnp.concatenate([parts, parts], axis=1), piece, preferred_element_type=jnp.float32)


def apply_piece(vectors, piece):
    return apply_parts(parts_of(vectors), piece)


def cut(x):
    middle = x.shape[1] // 2
    return x[:, :middle], x[:, middle:]


def collect(total):
    probes = total.shape[0] // 3
    return total[:probes] + (total[probes : 2 * probes] + total[2 * probes :])


def solution(mesh):
    n = mesh.shape["blk"]
    strides = [1 << k for k in reversed(range(n.bit_length() - 1))]

    def body(points, lengthscale, noise_var, targets):
        feats, width = points.shape
        probes = targets.shape[0]
        team = min(n, 4)
        while team < n and (n * width) * (n * width) // team * 4 > TILE_BYTES:
            team *= 2
        outer, inner = [s for s in strides if s >= team], [s for s in strides if s < team]

        def arrivals(x):
            pieces, sent = [x, swap(x, n, 1)], [x]
            for stride in inner[:-1]:
                came = swap(sent[0] if len(sent) == 1 else jnp.concatenate(sent, axis=1), n, stride)
                sent.append(came)
                pieces += [came, swap(came, n, 1)]
            return pieces

        scale = (POINT_SCALE / lengthscale)[:, None]
        used = feats + probes + 1
        spare = jnp.pad(noise_var[None, :], ((0, -used % 8), (0, 0)))
        block = lax.optimization_barrier(jnp.concatenate([points, targets, spare], axis=0))
        fence = lax.optimization_barrier
        tile = []

        def build(x, total):
            piece, total = build_piece(x[:feats], scale, right, x[feats:], total)
            tile.append(piece)
            return total

        if len(outer) == 2 and len(inner) == 2:
            far, near, side = outer[0], outer[1], inner[0]
            by_far = swap(block, n, far)
            right_own, copy = prepare(block, scale, used)
            near_own = swap(copy, n, near)
            side_own = swap(copy, n, side)
            near_far = swap(by_far, n, near)
            right_far, copy = prepare(by_far, scale, used)
            side_far = swap(copy, n, side)
            right_near, by_near = prepare(join(near_own, near_far[:used]), scale, used)
            last, side_own = fence((by_near, side_own))
            side_last = swap(last, n, side)
            right = join(right_own, right_far, right_near)
            mine = join(block[:used], by_far[:used], by_near)
            noise, mine = mine[-1:], mine[:-1]
            across = swap(mine, n, 1)
            my_applied = build(mine, noise * mine[feats:])
            my_applied = build(across, my_applied)
            side_last, side_far, my_applied = fence((side_last, side_far, my_applied))
            beside = join(side_own, side_far, side_last)
            noise_beside, beside = beside[-1:], beside[:-1]
            beside_across = swap(beside, n, 1)
            my_far = build(beside, jnp.zeros_like(my_applied))
            my_far = build(beside_across, my_far)
            my_applied = my_applied + my_far
            first = [mine, across, beside, beside_across]
            far_rows = [beside[:feats], beside_across[:feats]]
        else:
            mine = block
            for stride in outer:
                mine = join(mine, swap(mine, n, stride))
            mine = mine[:used]
            (right,), noise, first = prepare(mine, scale), mine[-1:], arrivals(mine[:-1])
            my_applied = noise * first[0][feats:]
            for x in first:
                my_applied = build(x, my_applied)
            my_far, far_rows = my_applied, []
        cols = noise.shape[1]
        starts = [x[feats:] for x in first]

        far_tile, right_far = [], None
        first_core = lax.axis_index("blk") % 2 == 0

        def paired(x):
            low, high = cut(x)
            return jnp.where(first_core, low, high), jnp.where(first_core, high, low)

        def far_own_product(vectors):
            return [collect(x) for x in jnp.split(apply_parts(stack(vectors), far_tile[0]), len(vectors))]

        def far_cross_product(vectors):
            low, high = zip(*[cut(x) for x in vectors])
            terms = [apply_parts(stack(x), piece) for x, piece in zip((low, high), far_tile[1])]
            return [join(*[collect(x) for x in pair]) for pair in zip(*[jnp.split(x, len(vectors)) for x in terms])]

        def far_build():
            nonlocal right_far
            if right_far is None:
                (right_far,) = prepare(far_rows[0], scale)
                return build_piece(far_rows[0], scale, right_far)[0]
            return [build_piece(x, scale, y)[0] for x, y in zip(cut(far_rows[1]), paired(right_far))]

        def exchange(x, residual, direction, last):
            nonlocal far_rows
            parts, passed = fence((parts_of(x), x))
            pieces, sent, known = [x, swap(passed, n, 1)], [x], []
            near = fence(apply_parts(parts, tile[0]))
            near = fence(near + apply_piece(pieces[1], tile[1]))
            far = jnp.zeros_like(near) if len(inner) == 1 else None
            for k, stride in enumerate(inner[:-1]):
                arrived = swap(join(*sent), n, stride)
                if far_rows and not last:
                    far_rows, near = fence((far_rows, near))
                    piece, near = fence((far_build(), near))
                    far_tile.append(piece)
                elif far_rows:
                    state, near = fence(([residual, direction], near))
                    known = [far_own_product([v[:, 2 * cols : 3 * cols] for v in state])]
                    known.append(far_cross_product([v[:, 3 * cols :] for v in state]))
                    known, near = fence((known, near))
                arrived, near = fence((arrived, near))
                sent.append(arrived)
                pieces.append(arrived)
                term = apply_piece(arrived, tile[2 + 2 * k])
                far = fence(term if far is None else far + term)
                pieces.append(swap(arrived, n, 1))
                if k < len(inner) - 2:
                    far = fence(far + apply_piece(pieces[-1], tile[3 + 2 * k]))
            if known:
                own_term, far = fence((far_own_product([arrived])[0], far))
            before = join(*pieces[:-1])
            curve = jnp.sum(direction[:, : before.shape[1]] * before, axis=1)
            curve, far = fence((curve, far))
            curve = curve + jnp.sum(direction[:, before.shape[1] :] * pieces[-1], axis=1)
            if len(inner) > 1:
                far = far + apply_piece(pieces[-1], tile[-1])
            if known:
                known = [[*known[0], own_term], [*known[1], *far_cross_product(pieces[-1:])]]
            return collect(far), collect(near) + collect(far) + noise * x, join(*pieces), curve, known

        residual = direction = join(*starts)
        my_solution = jnp.zeros_like(direction[:, :width])
        norm_now = jnp.sum(residual * residual, axis=1)
        my_image, far_image = my_applied, my_far
        for iteration in range(ITERS - 1):
            far_next, my_next, applied, curve, known = exchange(my_applied, residual, direction, iteration == ITERS - 2)
            step_size = (norm_now / curve)[:, None]
            my_solution = my_solution + step_size * direction[:, :width]
            residual = residual - step_size * applied
            norm_next = jnp.sum(residual * residual, axis=1)
            ratio = (norm_next / norm_now)[:, None]
            my_image = my_image - step_size * my_next
            my_applied = my_image + ratio * my_applied
            far_image = far_image - step_size * far_next
            my_far = far_image + ratio * my_far
            direction = residual + ratio * direction
            norm_now = norm_next
        mine = direction[:, :cols]
        if far_rows:
            own_part, cross = [of_res + ratio * of_dir - step_size * of_app for of_res, of_dir, of_app in known]
            side = direction[:, 2 * cols : 3 * cols]
            far_terms = side * (own_part + noise_beside * side) + 2.0 * join(*paired(side)) * cross
            curve = add_up(jnp.sum(mine * (my_applied + my_far) + far_terms, axis=1), n, [1])
        else:
            curve = add_up(jnp.sum(mine * my_applied, axis=1), n, inner)
        step_size = (norm_now / curve)[:, None]
        my_solution = my_solution + step_size * direction[:, :width]
        return my_solution, residual[:, :width] - step_size * my_applied[:, :width]

    in_specs = (P("groups", "blk"), P("groups"), P(("groups", "blk")), P("groups", "blk"))
    out_specs = (P("groups", "blk"), P("groups", "blk"))
    return jax.shard_map(body, mesh=mesh, in_specs=in_specs, out_specs=out_specs, check_vma=False)
```

```python
import math

import jax
import jax.numpy as jnp
from jax import lax
from jax.experimental import pallas as pl
from jax.experimental.pallas import tpu as pltpu
from jax.sharding import PartitionSpec as P

ITERS = 4
TILE_BYTES = 16 << 20
VMEM_BYTES = 16 << 20
NORM_ROWS = 64
BUILD_ROWS = 1024
POINT_SCALE = math.sqrt(math.log2(math.e))


def swap(x, n, stride):
    return lax.ppermute(x, "blk", [(i, i ^ stride) for i in range(n)])


def add_up(x, n, strides):
    for stride in strides:
        x = x + swap(x, n, stride)
    return x


def split(x, parts):
    out = []
    for _ in range(parts):
        high = lax.reduce_precision(x, 8, 7)
        out.append(high.astype(jnp.bfloat16))
        x = x - high
    return out


def halve(x):
    high = x.astype(jnp.bfloat16)
    return high, x - high.astype(jnp.float32)


def operands(pts):
    high, rest = halve(pts)
    mid, rest = halve(rest)
    low = rest.astype(jnp.bfloat16)
    norms = -0.5 * jnp.sum(pts * pts, axis=0, keepdims=True)
    row = lax.broadcasted_iota(jnp.int32, (NORM_ROWS, pts.shape[1]), 0)
    left = jnp.where((row >= 3) & (row < 6), 1.0, 0.0)
    right = jnp.where(row < 3, 1.0, 0.0)
    for k in range(3):
        part, norms = halve(norms)
        part = part.astype(jnp.float32)
        left = jnp.where(row == k, part, left)
        right = jnp.where(row == 3 + k, part, right)
    left = jnp.concatenate([high, high, mid, high, low, mid, left.astype(jnp.bfloat16)], axis=0)
    right = jnp.concatenate([high, mid, high, low, high, mid, right.astype(jnp.bfloat16)], axis=0)
    return left, right


def prepare_kernel(part_ref, scale_ref, right_ref, *copy_ref):
    feats = scale_ref.shape[0]
    right_ref[...] = operands(part_ref[:feats] * scale_ref[...])[1]
    for ref in copy_ref:
        ref[...] = part_ref[: ref.shape[0]]


def build_kernel(rows_ref, scale_ref, right_ref, *refs):
    applies = len(refs) > 1
    vectors_ref, sum_ref, tile_ref, out_ref = refs if applies else (None, None, *refs, None)
    total, cols = rows_ref.shape[1], right_ref.shape[1]
    block, step = min(total, BUILD_ROWS), min(cols, 256)
    if applies:
        probes = vectors_ref.shape[0]
        high, rest = halve(vectors_ref[...])
        mid, rest = halve(rest)
        thrice = jnp.concatenate([high, mid, rest.astype(jnp.bfloat16)], axis=0)
    steps = [(top, at) for top in range(0, total, block) for at in range(0, cols, step)]
    lefts, powers, parts = {}, {}, {}

    def contract(top, at):
        if top not in lefts:
            lefts[top] = jnp.transpose(operands(rows_ref[:, top : top + block] * scale_ref[...])[0])
        powers[top, at] = jnp.dot(lefts[top], right_ref[:, at : at + step], preferred_element_type=jnp.float32)

    def raise_power(top, at):
        high, rest = halve(jnp.exp2(powers.pop((top, at))))
        low = rest.astype(jnp.bfloat16)
        tile_ref[top : top + block, at : at + step] = high
        tile_ref[total + top : total + top + block, at : at + step] = low
        parts[top, at] = high, low

    def apply(top, at):
        down, here = slice(top, top + block), slice(at, at + step)
        vectors = jnp.concatenate([thrice[:, down]] * 2, axis=1)
        both = jnp.concatenate(parts.pop((top, at)), axis=0)
        term = jnp.dot(vectors, both, preferred_element_type=jnp.float32)
        term = term[:probes] + (term[probes : 2 * probes] + term[2 * probes :])
        before = sum_ref if top == 0 else out_ref
        out_ref[:, here] = before[:, here] + term

    contract(*steps[0])
    for k, chunk in enumerate(steps):
        if k + 1 < len(steps):
            contract(*steps[k + 1])
        raise_power(*chunk)
        if k and applies:
            apply(*steps[k - 1])
    if applies:
        apply(*steps[-1])


def call(kernel, outs, *args, **cost):
    whole = pl.BlockSpec(memory_space=pltpu.VMEM)
    return pl.pallas_call(
        kernel,
        out_shape=outs,
        in_specs=[whole] * len(args),
        out_specs=jax.tree.map(lambda _: whole, outs),
        compiler_params=pltpu.CompilerParams(vmem_limit_bytes=VMEM_BYTES),
        cost_estimate=pl.CostEstimate(**cost),
    )(*args)


def prepare(part, scale, copy=0):
    feats, cols = scale.shape[0], part.shape[1]
    outs = (jax.ShapeDtypeStruct((6 * feats + NORM_ROWS, cols), jnp.bfloat16),)
    if copy:
        outs += (jax.ShapeDtypeStruct((copy, cols), part.dtype),)
    return call(prepare_kernel, outs, part, scale, flops=10**0, bytes_accessed=feats * cols, transcendentals=0)


def join(*xs):
    return jnp.concatenate(xs, axis=1)


def build_piece(rows, scale, right, vectors=None, total=None):
    count, cols = rows.shape[1], right.shape[1]
    outs = (jax.ShapeDtypeStruct((2 * count, cols), jnp.bfloat16),)
    cost = dict(flops=2 * count * cols * 416, bytes_accessed=4 * count * cols, transcendentals=count * cols)
    args = (rows, scale, right)
    if vectors is not None:
        outs, args = (*outs, jax.ShapeDtypeStruct(total.shape, jnp.float32)), (*args, vectors, total)
    return call(build_kernel, outs, *args, **cost)


def parts_of(vectors):
    high, mid, low = split(vectors, 3)
    return jnp.concatenate([high, mid, low], axis=0)


def apply_parts(parts, piece):
    return jnp.dot(jnp.concatenate([parts, parts], axis=1), piece, preferred_element_type=jnp.float32)


def apply_piece(vectors, piece):
    return apply_parts(parts_of(vectors), piece)


def collect(total):
    probes = total.shape[0] // 3
    return total[:probes] + (total[probes : 2 * probes] + total[2 * probes :])


def solution(mesh):
    n = mesh.shape["blk"]
    strides = [1 << k for k in reversed(range(n.bit_length() - 1))]

    def body(points, lengthscale, noise_var, targets):
        feats, width = points.shape
        probes = targets.shape[0]
        team = min(n, 4)
        while team < n and (n * width) * (n * width) // team * 4 > TILE_BYTES:
            team *= 2
        outer, inner = [s for s in strides if s >= team], [s for s in strides if s < team]

        def arrivals(x):
            pieces, sent = [x, swap(x, n, 1)], [x]
            for stride in inner[:-1]:
                came = swap(sent[0] if len(sent) == 1 else jnp.concatenate(sent, axis=1), n, stride)
                sent.append(came)
                pieces += [came, swap(came, n, 1)]
            return pieces

        scale = (POINT_SCALE / lengthscale)[:, None]
        used = feats + probes + 1
        spare = jnp.pad(noise_var[None, :], ((0, -used % 8), (0, 0)))
        block = lax.optimization_barrier(jnp.concatenate([points, targets, spare], axis=0))
        fence = lax.optimization_barrier
        tile = []

        def build(x, total):
            piece, total = build_piece(x[:feats], scale, right, x[feats:], total)
            tile.append(piece)
            return total

        if len(outer) == 2 and len(inner) == 2:
            far, near, side = outer[0], outer[1], inner[0]
            by_far = swap(block, n, far)
            right_own, copy = prepare(block, scale, used)
            near_own = swap(copy, n, near)
            side_own = swap(copy, n, side)
            near_far = swap(by_far, n, near)
            right_far, copy = prepare(by_far, scale, used)
            side_far = swap(copy, n, side)
            right_near, by_near = prepare(join(near_own, near_far[:used]), scale, used)
            last, side_own = fence((by_near, side_own))
            side_last = swap(last, n, side)
            right = join(right_own, right_far, right_near)
            mine = join(block[:used], by_far[:used], by_near)
            noise, mine = mine[-1:], mine[:-1]
            across = swap(mine, n, 1)
            my_applied = build(mine, noise * mine[feats:])
            my_applied = build(across, my_applied)
            side_last, side_far, my_applied = fence((side_last, side_far, my_applied))
            beside = join(side_own, side_far, side_last)
            noise_beside, beside = beside[-1:], beside[:-1]
            beside_across = swap(beside, n, 1)
            my_far = build(beside, jnp.zeros_like(my_applied))
            my_far = build(beside_across, my_far)
            my_applied = my_applied + my_far
            first = [mine, across, beside, beside_across]
            far_rows = [beside[:feats], beside_across[:feats]]
        else:
            mine = block
            for stride in outer:
                mine = join(mine, swap(mine, n, stride))
            mine = mine[:used]
            (right,), noise, first = prepare(mine, scale), mine[-1:], arrivals(mine[:-1])
            my_applied = noise * first[0][feats:]
            for x in first:
                my_applied = build(x, my_applied)
            my_far, far_rows = my_applied, []
        cols = noise.shape[1]
        starts = [x[feats:] for x in first]

        far_tile, right_far = [], None

        def exchange(x, direction):
            nonlocal right_far
            parts, passed = fence((parts_of(x), x))
            pieces, sent = [x, swap(passed, n, 1)], [x]
            near = fence(apply_parts(parts, tile[0]))
            near = fence(near + apply_piece(pieces[1], tile[1]))
            far = jnp.zeros_like(near) if len(inner) == 1 else None
            for k, stride in enumerate(inner[:-1]):
                arrived = swap(join(*sent), n, stride)
                if len(far_tile) < len(far_rows):
                    rows, columns, near = fence((far_rows[len(far_tile)], far_rows[0], near))
                    if right_far is None:
                        (right_far,) = prepare(columns, scale)
                    (piece,) = build_piece(rows, scale, right_far)
                    piece, right_far, near = fence((piece, right_far, near))
                    far_tile.append(piece)
                arrived, near = fence((arrived, near))
                sent.append(arrived)
                pieces.append(arrived)
                term = apply_piece(arrived, tile[2 + 2 * k])
                far = fence(term if far is None else far + term)
                pieces.append(swap(arrived, n, 1))
                if k < len(inner) - 2:
                    far = fence(far + apply_piece(pieces[-1], tile[3 + 2 * k]))
            before = join(*pieces[:-1])
            curve = jnp.sum(direction[:, : before.shape[1]] * before, axis=1)
            curve, far = fence((curve, far))
            curve = curve + jnp.sum(direction[:, before.shape[1] :] * pieces[-1], axis=1)
            if len(inner) > 1:
                far = far + apply_piece(pieces[-1], tile[-1])
            return collect(far), collect(near) + collect(far) + noise * x, join(*pieces), curve

        residual = direction = join(*starts)
        my_solution = jnp.zeros_like(direction[:, :width])
        norm_now = jnp.sum(residual * residual, axis=1)
        my_image, far_image = my_applied, my_far
        for iteration in range(ITERS - 1):
            far_next, my_next, applied, curve = exchange(my_applied, direction)
            step_size = (norm_now / curve)[:, None]
            my_solution = my_solution + step_size * direction[:, :width]
            residual = residual - step_size * applied
            norm_next = jnp.sum(residual * residual, axis=1)
            ratio = (norm_next / norm_now)[:, None]
            my_image = my_image - step_size * my_next
            my_applied = my_image + ratio * my_applied
            far_image = far_image - step_size * far_next
            my_far = far_image + ratio * my_far
            direction = residual + ratio * direction
            norm_now = norm_next
        mine = direction[:, :cols]
        if far_rows:
            side, beside = direction[:, 2 * cols : 3 * cols], direction[:, 3 * cols :]
            image = collect(apply_piece(side, far_tile[0]) + apply_piece(beside, far_tile[1])) + noise_beside * side
            curve = add_up(jnp.sum(mine * (my_applied + my_far) + side * image, axis=1), n, [1])
        else:
            curve = add_up(jnp.sum(mine * my_applied, axis=1), n, inner)
        step_size = (norm_now / curve)[:, None]
        my_solution = my_solution + step_size * direction[:, :width]
        return my_solution, residual[:, :width] - step_size * my_applied[:, :width]

    in_specs = (P("groups", "blk"), P("groups"), P(("groups", "blk")), P("groups", "blk"))
    out_specs = (P("groups", "blk"), P("groups", "blk"))
    return jax.shard_map(body, mesh=mesh, in_specs=in_specs, out_specs=out_specs, check_vma=False)
```

```python
import math

import jax
import jax.numpy as jnp
from jax import lax
from jax.experimental import pallas as pl
from jax.experimental.pallas import tpu as pltpu
from jax.sharding import PartitionSpec as P

ITERS = 4
TILE_BYTES = 16 << 20
VMEM_BYTES = 16 << 20
NORM_ROWS = 64
BUILD_ROWS = 1024
POINT_SCALE = math.sqrt(math.log2(math.e))


def swap(x, n, stride):
    return lax.ppermute(x, "blk", [(i, i ^ stride) for i in range(n)])


def add_up(x, n, strides):
    for stride in strides:
        x = x + swap(x, n, stride)
    return x


def split(x, parts):
    out = []
    for _ in range(parts):
        high = lax.reduce_precision(x, 8, 7)
        out.append(high.astype(jnp.bfloat16))
        x = x - high
    return out


def halve(x):
    high = x.astype(jnp.bfloat16)
    return high, x - high.astype(jnp.float32)


def operands(pts):
    high, rest = halve(pts)
    mid, rest = halve(rest)
    low = rest.astype(jnp.bfloat16)
    norms = -0.5 * jnp.sum(pts * pts, axis=0, keepdims=True)
    row = lax.broadcasted_iota(jnp.int32, (NORM_ROWS, pts.shape[1]), 0)
    left = jnp.where((row >= 3) & (row < 6), 1.0, 0.0)
    right = jnp.where(row < 3, 1.0, 0.0)
    for k in range(3):
        part, norms = halve(norms)
        part = part.astype(jnp.float32)
        left = jnp.where(row == k, part, left)
        right = jnp.where(row == 3 + k, part, right)
    left = jnp.concatenate([high, high, mid, high, low, mid, left.astype(jnp.bfloat16)], axis=0)
    right = jnp.concatenate([high, mid, high, low, high, mid, right.astype(jnp.bfloat16)], axis=0)
    return left, right


def prepare_kernel(part_ref, scale_ref, right_ref, *copy_ref):
    feats = scale_ref.shape[0]
    right_ref[...] = operands(part_ref[:feats] * scale_ref[...])[1]
    for ref in copy_ref:
        ref[...] = part_ref[: ref.shape[0]]


def build_kernel(rows_ref, scale_ref, right_ref, *refs):
    applies = len(refs) > 1
    vectors_ref, sum_ref, tile_ref, out_ref = refs if applies else (None, None, *refs, None)
    total, cols = rows_ref.shape[1], right_ref.shape[1]
    block, step = min(total, BUILD_ROWS), min(cols, 256)
    if applies:
        probes = vectors_ref.shape[0]
        high, rest = halve(vectors_ref[...])
        mid, rest = halve(rest)
        thrice = jnp.concatenate([high, mid, rest.astype(jnp.bfloat16)], axis=0)
    steps = [(top, at) for top in range(0, total, block) for at in range(0, cols, step)]
    lefts, powers, parts = {}, {}, {}

    def contract(top, at):
        if top not in lefts:
            lefts[top] = jnp.transpose(operands(rows_ref[:, top : top + block] * scale_ref[...])[0])
        powers[top, at] = jnp.dot(lefts[top], right_ref[:, at : at + step], preferred_element_type=jnp.float32)

    def raise_power(top, at):
        high, rest = halve(jnp.exp2(powers.pop((top, at))))
        low = rest.astype(jnp.bfloat16)
        tile_ref[top : top + block, at : at + step] = high
        tile_ref[total + top : total + top + block, at : at + step] = low
        parts[top, at] = high, low

    def apply(top, at):
        down, here = slice(top, top + block), slice(at, at + step)
        vectors = jnp.concatenate([thrice[:, down]] * 2, axis=1)
        both = jnp.concatenate(parts.pop((top, at)), axis=0)
        term = jnp.dot(vectors, both, preferred_element_type=jnp.float32)
        term = term[:probes] + (term[probes : 2 * probes] + term[2 * probes :])
        before = sum_ref if top == 0 else out_ref
        out_ref[:, here] = before[:, here] + term

    contract(*steps[0])
    for k, chunk in enumerate(steps):
        if k and applies:
            apply(*steps[k - 1])
        if k + 1 < len(steps):
            contract(*steps[k + 1])
        raise_power(*chunk)
    if applies:
        apply(*steps[-1])


def call(kernel, outs, *args, **cost):
    whole = pl.BlockSpec(memory_space=pltpu.VMEM)
    return pl.pallas_call(
        kernel,
        out_shape=outs,
        in_specs=[whole] * len(args),
        out_specs=jax.tree.map(lambda _: whole, outs),
        compiler_params=pltpu.CompilerParams(vmem_limit_bytes=VMEM_BYTES),
        cost_estimate=pl.CostEstimate(**cost),
    )(*args)


def prepare(part, scale, copy=0):
    feats, cols = scale.shape[0], part.shape[1]
    outs = (jax.ShapeDtypeStruct((6 * feats + NORM_ROWS, cols), jnp.bfloat16),)
    if copy:
        outs += (jax.ShapeDtypeStruct((copy, cols), part.dtype),)
    return call(prepare_kernel, outs, part, scale, flops=10**0, bytes_accessed=feats * cols, transcendentals=0)


def join(*xs):
    return jnp.concatenate(xs, axis=1)


def build_piece(rows, scale, right, vectors=None, total=None):
    count, cols = rows.shape[1], right.shape[1]
    outs = (jax.ShapeDtypeStruct((2 * count, cols), jnp.bfloat16),)
    cost = dict(flops=2 * count * cols * 416, bytes_accessed=4 * count * cols, transcendentals=count * cols)
    args = (rows, scale, right)
    if vectors is not None:
        outs, args = (*outs, jax.ShapeDtypeStruct(total.shape, jnp.float32)), (*args, vectors, total)
    return call(build_kernel, outs, *args, **cost)


def parts_of(vectors):
    high, mid, low = split(vectors, 3)
    return jnp.concatenate([high, mid, low], axis=0)


def apply_parts(parts, piece):
    return jnp.dot(jnp.concatenate([parts, parts], axis=1), piece, preferred_element_type=jnp.float32)


def apply_piece(vectors, piece):
    return apply_parts(parts_of(vectors), piece)


def collect(total):
    probes = total.shape[0] // 3
    return total[:probes] + (total[probes : 2 * probes] + total[2 * probes :])


def solution(mesh):
    n = mesh.shape["blk"]
    strides = [1 << k for k in reversed(range(n.bit_length() - 1))]

    def body(points, lengthscale, noise_var, targets):
        feats, width = points.shape
        probes = targets.shape[0]
        team = min(n, 4)
        while team < n and (n * width) * (n * width) // team * 4 > TILE_BYTES:
            team *= 2
        outer, inner = [s for s in strides if s >= team], [s for s in strides if s < team]

        def arrivals(x):
            pieces, sent = [x, swap(x, n, 1)], [x]
            for stride in inner[:-1]:
                came = swap(sent[0] if len(sent) == 1 else jnp.concatenate(sent, axis=1), n, stride)
                sent.append(came)
                pieces += [came, swap(came, n, 1)]
            return pieces

        scale = (POINT_SCALE / lengthscale)[:, None]
        used = feats + probes + 1
        spare = jnp.pad(noise_var[None, :], ((0, -used % 8), (0, 0)))
        block = lax.optimization_barrier(jnp.concatenate([points, targets, spare], axis=0))
        fence = lax.optimization_barrier
        tile = []

        def build(x, total):
            piece, total = build_piece(x[:feats], scale, right, x[feats:], total)
            tile.append(piece)
            return total

        if len(outer) == 2 and len(inner) == 2:
            far, near, side = outer[0], outer[1], inner[0]
            by_far = swap(block, n, far)
            right_own, copy = prepare(block, scale, used)
            near_own = swap(copy, n, near)
            side_own = swap(copy, n, side)
            near_far = swap(by_far, n, near)
            right_far, copy = prepare(by_far, scale, used)
            side_far = swap(copy, n, side)
            right_near, by_near = prepare(join(near_own, near_far[:used]), scale, used)
            last, side_own = fence((by_near, side_own))
            side_last = swap(last, n, side)
            right = join(right_own, right_far, right_near)
            mine = join(block[:used], by_far[:used], by_near)
            noise, mine = mine[-1:], mine[:-1]
            across = swap(mine, n, 1)
            my_applied = build(mine, noise * mine[feats:])
            my_applied = build(across, my_applied)
            side_last, side_far, my_applied = fence((side_last, side_far, my_applied))
            beside = join(side_own, side_far, side_last)
            noise_beside, beside = beside[-1:], beside[:-1]
            beside_across = swap(beside, n, 1)
            my_far = build(beside, jnp.zeros_like(my_applied))
            my_far = build(beside_across, my_far)
            my_applied = my_applied + my_far
            first = [mine, across, beside, beside_across]
            far_rows = [beside[:feats], beside_across[:feats]]
        else:
            mine = block
            for stride in outer:
                mine = join(mine, swap(mine, n, stride))
            mine = mine[:used]
            (right,), noise, first = prepare(mine, scale), mine[-1:], arrivals(mine[:-1])
            my_applied = noise * first[0][feats:]
            for x in first:
                my_applied = build(x, my_applied)
            my_far, far_rows = my_applied, []
        cols = noise.shape[1]
        starts = [x[feats:] for x in first]

        far_tile, right_far = [], None

        def exchange(x, direction):
            nonlocal right_far
            parts, passed = fence((parts_of(x), x))
            pieces, sent = [x, swap(passed, n, 1)], [x]
            near = fence(apply_parts(parts, tile[0]))
            near = fence(near + apply_piece(pieces[1], tile[1]))
            far = jnp.zeros_like(near) if len(inner) == 1 else None
            for k, stride in enumerate(inner[:-1]):
                arrived = swap(join(*sent), n, stride)
                if len(far_tile) < len(far_rows):
                    rows, columns, near = fence((far_rows[len(far_tile)], far_rows[0], near))
                    if right_far is None:
                        (right_far,) = prepare(columns, scale)
                    (piece,) = build_piece(rows, scale, right_far)
                    piece, right_far, near = fence((piece, right_far, near))
                    far_tile.append(piece)
                arrived, near = fence((arrived, near))
                sent.append(arrived)
                pieces.append(arrived)
                term = apply_piece(arrived, tile[2 + 2 * k])
                far = fence(term if far is None else far + term)
                pieces.append(swap(arrived, n, 1))
                if k < len(inner) - 2:
                    far = fence(far + apply_piece(pieces[-1], tile[3 + 2 * k]))
            before = join(*pieces[:-1])
            curve = jnp.sum(direction[:, : before.shape[1]] * before, axis=1)
            curve, far = fence((curve, far))
            curve = curve + jnp.sum(direction[:, before.shape[1] :] * pieces[-1], axis=1)
            if len(inner) > 1:
                far = far + apply_piece(pieces[-1], tile[-1])
            return collect(far), collect(near) + collect(far) + noise * x, join(*pieces), curve

        residual = direction = join(*starts)
        my_solution = jnp.zeros_like(direction[:, :width])
        norm_now = jnp.sum(residual * residual, axis=1)
        my_image, far_image = my_applied, my_far
        for iteration in range(ITERS - 1):
            far_next, my_next, applied, curve = exchange(my_applied, direction)
            step_size = (norm_now / curve)[:, None]
            my_solution = my_solution + step_size * direction[:, :width]
            residual = residual - step_size * applied
            norm_next = jnp.sum(residual * residual, axis=1)
            ratio = (norm_next / norm_now)[:, None]
            my_image = my_image - step_size * my_next
            my_applied = my_image + ratio * my_applied
            far_image = far_image - step_size * far_next
            my_far = far_image + ratio * my_far
            direction = residual + ratio * direction
            norm_now = norm_next
        mine = direction[:, :cols]
        if far_rows:
            side, beside = direction[:, 2 * cols : 3 * cols], direction[:, 3 * cols :]
            image = collect(apply_piece(side, far_tile[0]) + apply_piece(beside, far_tile[1])) + noise_beside * side
            curve = add_up(jnp.sum(mine * (my_applied + my_far) + side * image, axis=1), n, [1])
        else:
            curve = add_up(jnp.sum(mine * my_applied, axis=1), n, inner)
        step_size = (norm_now / curve)[:, None]
        my_solution = my_solution + step_size * direction[:, :width]
        return my_solution, residual[:, :width] - step_size * my_applied[:, :width]

    in_specs = (P("groups", "blk"), P("groups"), P(("groups", "blk")), P("groups", "blk"))
    out_specs = (P("groups", "blk"), P("groups", "blk"))
    return jax.shard_map(body, mesh=mesh, in_specs=in_specs, out_specs=out_specs, check_vma=False)
```

```python
import math

import jax
import jax.numpy as jnp
from jax import lax
from jax.experimental import pallas as pl
from jax.experimental.pallas import tpu as pltpu
from jax.sharding import PartitionSpec as P

ITERS = 4
TILE_BYTES = 16 << 20
VMEM_BYTES = 16 << 20
NORM_ROWS = 64
BUILD_ROWS = 512
POINT_SCALE = math.sqrt(math.log2(math.e))


def swap(x, n, stride):
    return lax.ppermute(x, "blk", [(i, i ^ stride) for i in range(n)])


def add_up(x, n, strides):
    for stride in strides:
        x = x + swap(x, n, stride)
    return x


def split(x, parts):
    out = []
    for _ in range(parts):
        high = lax.reduce_precision(x, 8, 7)
        out.append(high.astype(jnp.bfloat16))
        x = x - high
    return out


def halve(x):
    high = x.astype(jnp.bfloat16)
    return high, x - high.astype(jnp.float32)


def operands(pts):
    high, rest = halve(pts)
    mid, rest = halve(rest)
    low = rest.astype(jnp.bfloat16)
    norms = -0.5 * jnp.sum(pts * pts, axis=0, keepdims=True)
    row = lax.broadcasted_iota(jnp.int32, (NORM_ROWS, pts.shape[1]), 0)
    left = jnp.where((row >= 3) & (row < 6), 1.0, 0.0)
    right = jnp.where(row < 3, 1.0, 0.0)
    for k in range(3):
        part, norms = halve(norms)
        part = part.astype(jnp.float32)
        left = jnp.where(row == k, part, left)
        right = jnp.where(row == 3 + k, part, right)
    left = jnp.concatenate([high, high, mid, high, low, mid, left.astype(jnp.bfloat16)], axis=0)
    right = jnp.concatenate([high, mid, high, low, high, mid, right.astype(jnp.bfloat16)], axis=0)
    return left, right


def prepare_kernel(part_ref, scale_ref, right_ref, *copy_ref):
    feats = scale_ref.shape[0]
    right_ref[...] = operands(part_ref[:feats] * scale_ref[...])[1]
    for ref in copy_ref:
        ref[...] = part_ref[: ref.shape[0]]


def build_kernel(rows_ref, scale_ref, right_ref, *refs):
    applies = len(refs) > 1
    vectors_ref, sum_ref, tile_ref, out_ref = refs if applies else (None, None, *refs, None)
    total, cols = rows_ref.shape[1], right_ref.shape[1]
    block, step = min(total, BUILD_ROWS), min(cols, 256)
    if applies:
        probes = vectors_ref.shape[0]
        high, rest = halve(vectors_ref[...])
        mid, rest = halve(rest)
        thrice = jnp.concatenate([high, mid, rest.astype(jnp.bfloat16)], axis=0)
    steps = [(top, at) for top in range(0, total, block) for at in range(0, cols, step)]
    lefts, powers, parts = {}, {}, {}

    def contract(top, at):
        if top not in lefts:
            lefts[top] = jnp.transpose(operands(rows_ref[:, top : top + block] * scale_ref[...])[0])
        powers[top, at] = jnp.dot(lefts[top], right_ref[:, at : at + step], preferred_element_type=jnp.float32)

    def raise_power(top, at):
        high, rest = halve(jnp.exp2(powers.pop((top, at))))
        low = rest.astype(jnp.bfloat16)
        tile_ref[top : top + block, at : at + step] = high
        tile_ref[total + top : total + top + block, at : at + step] = low
        parts[top, at] = high, low

    def apply(top, at):
        down, here = slice(top, top + block), slice(at, at + step)
        vectors = jnp.concatenate([thrice[:, down]] * 2, axis=1)
        both = jnp.concatenate(parts.pop((top, at)), axis=0)
        term = jnp.dot(vectors, both, preferred_element_type=jnp.float32)
        term = term[:probes] + (term[probes : 2 * probes] + term[2 * probes :])
        before = sum_ref if top == 0 else out_ref
        out_ref[:, here] = before[:, here] + term

    contract(*steps[0])
    for k, chunk in enumerate(steps):
        if k + 1 < len(steps):
            contract(*steps[k + 1])
        raise_power(*chunk)
        if k and applies:
            apply(*steps[k - 1])
    if applies:
        apply(*steps[-1])


def call(kernel, outs, *args, **cost):
    whole = pl.BlockSpec(memory_space=pltpu.VMEM)
    return pl.pallas_call(
        kernel,
        out_shape=outs,
        in_specs=[whole] * len(args),
        out_specs=jax.tree.map(lambda _: whole, outs),
        compiler_params=pltpu.CompilerParams(vmem_limit_bytes=VMEM_BYTES),
        cost_estimate=pl.CostEstimate(**cost),
    )(*args)


def prepare(part, scale, copy=0):
    feats, cols = scale.shape[0], part.shape[1]
    outs = (jax.ShapeDtypeStruct((6 * feats + NORM_ROWS, cols), jnp.bfloat16),)
    if copy:
        outs += (jax.ShapeDtypeStruct((copy, cols), part.dtype),)
    return call(prepare_kernel, outs, part, scale, flops=10**0, bytes_accessed=feats * cols, transcendentals=0)


def join(*xs):
    return jnp.concatenate(xs, axis=1)


def build_piece(rows, scale, right, vectors=None, total=None):
    count, cols = rows.shape[1], right.shape[1]
    outs = (jax.ShapeDtypeStruct((2 * count, cols), jnp.bfloat16),)
    cost = dict(flops=2 * count * cols * 416, bytes_accessed=4 * count * cols, transcendentals=count * cols)
    args = (rows, scale, right)
    if vectors is not None:
        outs, args = (*outs, jax.ShapeDtypeStruct(total.shape, jnp.float32)), (*args, vectors, total)
    return call(build_kernel, outs, *args, **cost)


def parts_of(vectors):
    high, mid, low = split(vectors, 3)
    return jnp.concatenate([high, mid, low], axis=0)


def apply_parts(parts, piece):
    return jnp.dot(jnp.concatenate([parts, parts], axis=1), piece, preferred_element_type=jnp.float32)


def apply_piece(vectors, piece):
    return apply_parts(parts_of(vectors), piece)


def collect(total):
    probes = total.shape[0] // 3
    return total[:probes] + (total[probes : 2 * probes] + total[2 * probes :])


def solution(mesh):
    n = mesh.shape["blk"]
    strides = [1 << k for k in reversed(range(n.bit_length() - 1))]

    def body(points, lengthscale, noise_var, targets):
        feats, width = points.shape
        probes = targets.shape[0]
        team = min(n, 4)
        while team < n and (n * width) * (n * width) // team * 4 > TILE_BYTES:
            team *= 2
        outer, inner = [s for s in strides if s >= team], [s for s in strides if s < team]

        def arrivals(x):
            pieces, sent = [x, swap(x, n, 1)], [x]
            for stride in inner[:-1]:
                came = swap(sent[0] if len(sent) == 1 else jnp.concatenate(sent, axis=1), n, stride)
                sent.append(came)
                pieces += [came, swap(came, n, 1)]
            return pieces

        scale = (POINT_SCALE / lengthscale)[:, None]
        used = feats + probes + 1
        spare = jnp.pad(noise_var[None, :], ((0, -used % 8), (0, 0)))
        block = lax.optimization_barrier(jnp.concatenate([points, targets, spare], axis=0))
        fence = lax.optimization_barrier
        tile = []

        def build(x, total):
            piece, total = build_piece(x[:feats], scale, right, x[feats:], total)
            tile.append(piece)
            return total

        if len(outer) == 2 and len(inner) == 2:
            far, near, side = outer[0], outer[1], inner[0]
            by_far = swap(block, n, far)
            right_own, copy = prepare(block, scale, used)
            near_own = swap(copy, n, near)
            side_own = swap(copy, n, side)
            near_far = swap(by_far, n, near)
            right_far, copy = prepare(by_far, scale, used)
            side_far = swap(copy, n, side)
            right_near, by_near = prepare(join(near_own, near_far[:used]), scale, used)
            last, side_own = fence((by_near, side_own))
            side_last = swap(last, n, side)
            right = join(right_own, right_far, right_near)
            mine = join(block[:used], by_far[:used], by_near)
            noise, mine = mine[-1:], mine[:-1]
            across = swap(mine, n, 1)
            my_applied = build(mine, noise * mine[feats:])
            my_applied = build(across, my_applied)
            side_last, side_far, my_applied = fence((side_last, side_far, my_applied))
            beside = join(side_own, side_far, side_last)
            noise_beside, beside = beside[-1:], beside[:-1]
            beside_across = swap(beside, n, 1)
            my_far = build(beside, jnp.zeros_like(my_applied))
            my_far = build(beside_across, my_far)
            my_applied = my_applied + my_far
            first = [mine, across, beside, beside_across]
            far_rows = [beside[:feats], beside_across[:feats]]
        else:
            mine = block
            for stride in outer:
                mine = join(mine, swap(mine, n, stride))
            mine = mine[:used]
            (right,), noise, first = prepare(mine, scale), mine[-1:], arrivals(mine[:-1])
            my_applied = noise * first[0][feats:]
            for x in first:
                my_applied = build(x, my_applied)
            my_far, far_rows = my_applied, []
        cols = noise.shape[1]
        starts = [x[feats:] for x in first]

        far_tile, right_far = [], None

        def exchange(x, direction):
            nonlocal right_far
            parts, passed = fence((parts_of(x), x))
            pieces, sent = [x, swap(passed, n, 1)], [x]
            near = fence(apply_parts(parts, tile[0]))
            near = fence(near + apply_piece(pieces[1], tile[1]))
            far = jnp.zeros_like(near) if len(inner) == 1 else None
            for k, stride in enumerate(inner[:-1]):
                arrived = swap(join(*sent), n, stride)
                if len(far_tile) < len(far_rows):
                    rows, columns, near = fence((far_rows[len(far_tile)], far_rows[0], near))
                    if right_far is None:
                        (right_far,) = prepare(columns, scale)
                    (piece,) = build_piece(rows, scale, right_far)
                    piece, right_far, near = fence((piece, right_far, near))
                    far_tile.append(piece)
                arrived, near = fence((arrived, near))
                sent.append(arrived)
                pieces.append(arrived)
                term = apply_piece(arrived, tile[2 + 2 * k])
                far = fence(term if far is None else far + term)
                pieces.append(swap(arrived, n, 1))
                if k < len(inner) - 2:
                    far = fence(far + apply_piece(pieces[-1], tile[3 + 2 * k]))
            before = join(*pieces[:-1])
            curve = jnp.sum(direction[:, : before.shape[1]] * before, axis=1)
            curve, far = fence((curve, far))
            curve = curve + jnp.sum(direction[:, before.shape[1] :] * pieces[-1], axis=1)
            if len(inner) > 1:
                far = far + apply_piece(pieces[-1], tile[-1])
            return collect(far), collect(near) + collect(far) + noise * x, join(*pieces), curve

        residual = direction = join(*starts)
        my_solution = jnp.zeros_like(direction[:, :width])
        norm_now = jnp.sum(residual * residual, axis=1)
        my_image, far_image = my_applied, my_far
        for iteration in range(ITERS - 1):
            far_next, my_next, applied, curve = exchange(my_applied, direction)
            step_size = (norm_now / curve)[:, None]
            my_solution = my_solution + step_size * direction[:, :width]
            residual = residual - step_size * applied
            norm_next = jnp.sum(residual * residual, axis=1)
            ratio = (norm_next / norm_now)[:, None]
            my_image = my_image - step_size * my_next
            my_applied = my_image + ratio * my_applied
            far_image = far_image - step_size * far_next
            my_far = far_image + ratio * my_far
            direction = residual + ratio * direction
            norm_now = norm_next
        mine = direction[:, :cols]
        if far_rows:
            side, beside = direction[:, 2 * cols : 3 * cols], direction[:, 3 * cols :]
            image = collect(apply_piece(side, far_tile[0]) + apply_piece(beside, far_tile[1])) + noise_beside * side
            curve = add_up(jnp.sum(mine * (my_applied + my_far) + side * image, axis=1), n, [1])
        else:
            curve = add_up(jnp.sum(mine * my_applied, axis=1), n, inner)
        step_size = (norm_now / curve)[:, None]
        my_solution = my_solution + step_size * direction[:, :width]
        return my_solution, residual[:, :width] - step_size * my_applied[:, :width]

    in_specs = (P("groups", "blk"), P("groups"), P(("groups", "blk")), P("groups", "blk"))
    out_specs = (P("groups", "blk"), P("groups", "blk"))
    return jax.shard_map(body, mesh=mesh, in_specs=in_specs, out_specs=out_specs, check_vma=False)
```

```python
import math

import jax
import jax.numpy as jnp
from jax import lax
from jax.experimental import pallas as pl
from jax.experimental.pallas import tpu as pltpu
from jax.sharding import PartitionSpec as P

ITERS = 4
TILE_BYTES = 16 << 20
VMEM_BYTES = 16 << 20
NORM_ROWS = 64
BUILD_ROWS = 1024
POINT_SCALE = math.sqrt(math.log2(math.e))


def swap(x, n, stride):
    return lax.ppermute(x, "blk", [(i, i ^ stride) for i in range(n)])


def add_up(x, n, strides):
    for stride in strides:
        x = x + swap(x, n, stride)
    return x


def split(x, parts):
    out = []
    for _ in range(parts):
        high = lax.reduce_precision(x, 8, 7)
        out.append(high.astype(jnp.bfloat16))
        x = x - high
    return out


def halve(x):
    high = x.astype(jnp.bfloat16)
    return high, x - high.astype(jnp.float32)


def operands(pts):
    high, rest = halve(pts)
    mid, rest = halve(rest)
    low = rest.astype(jnp.bfloat16)
    norms = -0.5 * jnp.sum(pts * pts, axis=0, keepdims=True)
    row = lax.broadcasted_iota(jnp.int32, (NORM_ROWS, pts.shape[1]), 0)
    left = jnp.where((row >= 3) & (row < 6), 1.0, 0.0)
    right = jnp.where(row < 3, 1.0, 0.0)
    for k in range(3):
        part, norms = halve(norms)
        part = part.astype(jnp.float32)
        left = jnp.where(row == k, part, left)
        right = jnp.where(row == 3 + k, part, right)
    left = jnp.concatenate([high, high, mid, high, low, mid, left.astype(jnp.bfloat16)], axis=0)
    right = jnp.concatenate([high, mid, high, low, high, mid, right.astype(jnp.bfloat16)], axis=0)
    return left, right


def prepare_kernel(part_ref, scale_ref, right_ref, *copy_ref):
    feats = scale_ref.shape[0]
    right_ref[...] = operands(part_ref[:feats] * scale_ref[...])[1]
    for ref in copy_ref:
        ref[...] = part_ref[: ref.shape[0]]


def build_kernel(rows_ref, scale_ref, right_ref, *refs):
    applies = len(refs) > 1
    vectors_ref, sum_ref, tile_ref, out_ref = refs if applies else (None, None, *refs, None)
    total, cols = rows_ref.shape[1], right_ref.shape[1]
    block, step = min(total, BUILD_ROWS), min(cols, 256)
    if applies:
        probes = vectors_ref.shape[0]
        high, rest = halve(vectors_ref[...])
        mid, rest = halve(rest)
        thrice = jnp.concatenate([high, mid, rest.astype(jnp.bfloat16)], axis=0)
    steps = [(top, at) for top in range(0, total, block) for at in range(0, cols, step)]
    lefts, powers, parts = {}, {}, {}

    def contract(top, at):
        if top not in lefts:
            lefts[top] = jnp.transpose(operands(rows_ref[:, top : top + block] * scale_ref[...])[0])
        powers[top, at] = jnp.dot(lefts[top], right_ref[:, at : at + step], preferred_element_type=jnp.float32)

    def raise_power(top, at):
        high, rest = halve(jnp.exp2(powers.pop((top, at))))
        low = rest.astype(jnp.bfloat16)
        tile_ref[top : top + block, at : at + step] = high
        tile_ref[total + top : total + top + block, at : at + step] = low
        parts[top, at] = high, low

    def apply(top, at):
        down, here = slice(top, top + block), slice(at, at + step)
        vectors = jnp.concatenate([thrice[:, down]] * 2, axis=1)
        both = jnp.concatenate(parts.pop((top, at)), axis=0)
        term = jnp.dot(vectors, both, preferred_element_type=jnp.float32)
        term = term[:probes] + (term[probes : 2 * probes] + term[2 * probes :])
        before = sum_ref if top == 0 else out_ref
        out_ref[:, here] = before[:, here] + term

    contract(*steps[0])
    for k, chunk in enumerate(steps):
        if k + 1 < len(steps):
            contract(*steps[k + 1])
        raise_power(*chunk)
        if k and applies:
            apply(*steps[k - 1])
    if applies:
        apply(*steps[-1])


def call(kernel, outs, *args, **cost):
    whole = pl.BlockSpec(memory_space=pltpu.VMEM)
    return pl.pallas_call(
        kernel,
        out_shape=outs,
        in_specs=[whole] * len(args),
        out_specs=jax.tree.map(lambda _: whole, outs),
        compiler_params=pltpu.CompilerParams(vmem_limit_bytes=VMEM_BYTES),
        cost_estimate=pl.CostEstimate(**cost),
    )(*args)


def prepare(part, scale, copy=0):
    feats, cols = scale.shape[0], part.shape[1]
    outs = (jax.ShapeDtypeStruct((6 * feats + NORM_ROWS, cols), jnp.bfloat16),)
    if copy:
        outs += (jax.ShapeDtypeStruct((copy, cols), part.dtype),)
    return call(prepare_kernel, outs, part, scale, flops=10**0, bytes_accessed=feats * cols, transcendentals=0)


def join(*xs):
    return jnp.concatenate(xs, axis=1)


def build_piece(rows, scale, right, vectors=None, total=None):
    count, cols = rows.shape[1], right.shape[1]
    outs = (jax.ShapeDtypeStruct((2 * count, cols), jnp.bfloat16),)
    cost = dict(flops=2 * count * cols * 416, bytes_accessed=4 * count * cols, transcendentals=count * cols)
    args = (rows, scale, right)
    if vectors is not None:
        outs, args = (*outs, jax.ShapeDtypeStruct(total.shape, jnp.float32)), (*args, vectors, total)
    return call(build_kernel, outs, *args, **cost)


def stack(vectors):
    return jnp.concatenate([parts_of(x) for x in vectors], axis=0)


def parts_of(vectors):
    high, mid, low = split(vectors, 3)
    return jnp.concatenate([high, mid, low], axis=0)


def apply_parts(parts, piece):
    return jnp.dot(jnp.concatenate([parts, parts], axis=1), piece, preferred_element_type=jnp.float32)


def apply_piece(vectors, piece):
    return apply_parts(parts_of(vectors), piece)


def cut(x):
    middle = x.shape[1] // 2
    return x[:, :middle], x[:, middle:]


def collect(total):
    probes = total.shape[0] // 3
    return total[:probes] + (total[probes : 2 * probes] + total[2 * probes :])


def solution(mesh):
    n = mesh.shape["blk"]
    strides = [1 << k for k in reversed(range(n.bit_length() - 1))]

    def body(points, lengthscale, noise_var, targets):
        feats, width = points.shape
        probes = targets.shape[0]
        team = min(n, 4)
        while team < n and (n * width) * (n * width) // team * 4 > TILE_BYTES:
            team *= 2
        outer, inner = [s for s in strides if s >= team], [s for s in strides if s < team]

        def arrivals(x):
            pieces, sent = [x, swap(x, n, 1)], [x]
            for stride in inner[:-1]:
                came = swap(sent[0] if len(sent) == 1 else jnp.concatenate(sent, axis=1), n, stride)
                sent.append(came)
                pieces += [came, swap(came, n, 1)]
            return pieces

        scale = (POINT_SCALE / lengthscale)[:, None]
        used = feats + probes + 1
        spare = jnp.pad(noise_var[None, :], ((0, -used % 8), (0, 0)))
        block = lax.optimization_barrier(jnp.concatenate([points, targets, spare], axis=0))
        fence = lax.optimization_barrier
        tile = []

        def build(x, total):
            piece, total = build_piece(x[:feats], scale, right, x[feats:], total)
            tile.append(piece)
            return total

        if len(outer) == 2 and len(inner) == 2:
            far, near, side = outer[0], outer[1], inner[0]
            by_far = swap(block, n, far)
            right_own, copy = prepare(block, scale, used)
            near_own = swap(copy, n, near)
            side_own = swap(copy, n, side)
            near_far = swap(by_far, n, near)
            right_far, copy = prepare(by_far, scale, used)
            side_far = swap(copy, n, side)
            right_near, by_near = prepare(join(near_own, near_far[:used]), scale, used)
            last, side_own = fence((by_near, side_own))
            side_last = swap(last, n, side)
            right = join(right_own, right_far, right_near)
            mine = join(block[:used], by_far[:used], by_near)
            noise, mine = mine[-1:], mine[:-1]
            across = swap(mine, n, 1)
            my_applied = build(mine, noise * mine[feats:])
            my_applied = build(across, my_applied)
            side_last, side_far, my_applied = fence((side_last, side_far, my_applied))
            beside = join(side_own, side_far, side_last)
            noise_beside, beside = beside[-1:], beside[:-1]
            beside_across = swap(beside, n, 1)
            my_far = build(beside, jnp.zeros_like(my_applied))
            my_far = build(beside_across, my_far)
            my_applied = my_applied + my_far
            first = [mine, across, beside, beside_across]
            far_rows = [beside[:feats], beside_across[:feats]]
        else:
            mine = block
            for stride in outer:
                mine = join(mine, swap(mine, n, stride))
            mine = mine[:used]
            (right,), noise, first = prepare(mine, scale), mine[-1:], arrivals(mine[:-1])
            my_applied = noise * first[0][feats:]
            for x in first:
                my_applied = build(x, my_applied)
            my_far, far_rows = my_applied, []
        cols = noise.shape[1]
        starts = [x[feats:] for x in first]

        far_tile, right_far = [], None
        first_core = lax.axis_index("blk") % 2 == 0

        def paired(x):
            low, high = cut(x)
            return jnp.where(first_core, low, high), jnp.where(first_core, high, low)

        def far_own_product(vectors):
            return [collect(x) for x in jnp.split(apply_parts(stack(vectors), far_tile[0]), len(vectors))]

        def far_cross_product(vectors):
            return join(*[collect(apply_piece(x, piece)) for x, piece in zip(cut(vectors), far_tile[1])])

        def far_build():
            nonlocal right_far
            if right_far is None:
                (right_far,) = prepare(far_rows[0], scale)
                return build_piece(far_rows[0], scale, right_far)[0]
            return [build_piece(x, scale, y)[0] for x, y in zip(cut(far_rows[1]), paired(right_far))]

        def exchange(x, residual, direction, last):
            nonlocal far_rows
            parts, passed = fence((parts_of(x), x))
            pieces, sent, known = [x, swap(passed, n, 1)], [x], []
            near = fence(apply_parts(parts, tile[0]))
            near = fence(near + apply_piece(pieces[1], tile[1]))
            far = jnp.zeros_like(near) if len(inner) == 1 else None
            for k, stride in enumerate(inner[:-1]):
                arrived = swap(join(*sent), n, stride)
                if far_rows and not last:
                    far_rows, near = fence((far_rows, near))
                    piece, near = fence((far_build(), near))
                    far_tile.append(piece)
                elif far_rows:
                    state, near = fence(([residual, direction], near))
                    known, near = fence((far_own_product([v[:, 2 * cols : 3 * cols] for v in state]), near))
                arrived, near = fence((arrived, near))
                sent.append(arrived)
                pieces.append(arrived)
                term = apply_piece(arrived, tile[2 + 2 * k])
                far = fence(term if far is None else far + term)
                pieces.append(swap(arrived, n, 1))
                if k < len(inner) - 2:
                    far = fence(far + apply_piece(pieces[-1], tile[3 + 2 * k]))
            if known:
                own_term, far = fence((far_own_product([arrived])[0], far))
            before = join(*pieces[:-1])
            curve = jnp.sum(direction[:, : before.shape[1]] * before, axis=1)
            curve, far = fence((curve, far))
            curve = curve + jnp.sum(direction[:, before.shape[1] :] * pieces[-1], axis=1)
            if len(inner) > 1:
                far = far + apply_piece(pieces[-1], tile[-1])
            if known:
                known.append(own_term)
            return collect(far), collect(near) + collect(far) + noise * x, join(*pieces), curve, known

        residual = direction = join(*starts)
        my_solution = jnp.zeros_like(direction[:, :width])
        norm_now = jnp.sum(residual * residual, axis=1)
        my_image, far_image = my_applied, my_far
        for iteration in range(ITERS - 1):
            far_next, my_next, applied, curve, known = exchange(my_applied, residual, direction, iteration == ITERS - 2)
            step_size = (norm_now / curve)[:, None]
            my_solution = my_solution + step_size * direction[:, :width]
            residual = residual - step_size * applied
            norm_next = jnp.sum(residual * residual, axis=1)
            ratio = (norm_next / norm_now)[:, None]
            my_image = my_image - step_size * my_next
            my_applied = my_image + ratio * my_applied
            far_image = far_image - step_size * far_next
            my_far = far_image + ratio * my_far
            direction = residual + ratio * direction
            norm_now = norm_next
        mine = direction[:, :cols]
        if far_rows:
            of_residual, of_direction, of_applied = known
            own_part = of_residual + ratio * of_direction - step_size * of_applied
            side, cross = direction[:, 2 * cols : 3 * cols], far_cross_product(direction[:, 3 * cols :])
            far_terms = side * (own_part + noise_beside * side) + 2.0 * join(*paired(side)) * cross
            curve = add_up(jnp.sum(mine * (my_applied + my_far) + far_terms, axis=1), n, [1])
        else:
            curve = add_up(jnp.sum(mine * my_applied, axis=1), n, inner)
        step_size = (norm_now / curve)[:, None]
        my_solution = my_solution + step_size * direction[:, :width]
        return my_solution, residual[:, :width] - step_size * my_applied[:, :width]

    in_specs = (P("groups", "blk"), P("groups"), P(("groups", "blk")), P("groups", "blk"))
    out_specs = (P("groups", "blk"), P("groups", "blk"))
    return jax.shard_map(body, mesh=mesh, in_specs=in_specs, out_specs=out_specs, check_vma=False)
```

```python
import math

import jax
import jax.numpy as jnp
from jax import lax
from jax.experimental import pallas as pl
from jax.experimental.pallas import tpu as pltpu
from jax.sharding import PartitionSpec as P

ITERS = 4
TILE_BYTES = 16 << 20
VMEM_BYTES = 16 << 20
NORM_ROWS = 64
BUILD_ROWS = 1024
POINT_SCALE = math.sqrt(math.log2(math.e))


def swap(x, n, stride):
    return lax.ppermute(x, "blk", [(i, i ^ stride) for i in range(n)])


def add_up(x, n, strides):
    for stride in strides:
        x = x + swap(x, n, stride)
    return x


def split(x, parts):
    out = []
    for _ in range(parts):
        high = lax.reduce_precision(x, 8, 7)
        out.append(high.astype(jnp.bfloat16))
        x = x - high
    return out


def halve(x):
    high = x.astype(jnp.bfloat16)
    return high, x - high.astype(jnp.float32)


def operands(pts):
    high, rest = halve(pts)
    mid, rest = halve(rest)
    low = rest.astype(jnp.bfloat16)
    norms = -0.5 * jnp.sum(pts * pts, axis=0, keepdims=True)
    row = lax.broadcasted_iota(jnp.int32, (NORM_ROWS, pts.shape[1]), 0)
    left = jnp.where((row >= 3) & (row < 6), 1.0, 0.0)
    right = jnp.where(row < 3, 1.0, 0.0)
    for k in range(3):
        part, norms = halve(norms)
        part = part.astype(jnp.float32)
        left = jnp.where(row == k, part, left)
        right = jnp.where(row == 3 + k, part, right)
    left = jnp.concatenate([high, high, mid, high, low, mid, left.astype(jnp.bfloat16)], axis=0)
    right = jnp.concatenate([high, mid, high, low, high, mid, right.astype(jnp.bfloat16)], axis=0)
    return left, right


def prepare_kernel(part_ref, scale_ref, right_ref, *copy_ref):
    feats = scale_ref.shape[0]
    right_ref[...] = operands(part_ref[:feats] * scale_ref[...])[1]
    for ref in copy_ref:
        ref[...] = part_ref[: ref.shape[0]]


def build_kernel(rows_ref, scale_ref, right_ref, *refs):
    applies = len(refs) > 1
    vectors_ref, sum_ref, tile_ref, out_ref = refs if applies else (None, None, *refs, None)
    total, cols = rows_ref.shape[1], right_ref.shape[1]
    block, step = min(total, BUILD_ROWS), min(cols, 256)
    if applies:
        probes = vectors_ref.shape[0]
        high, rest = halve(vectors_ref[...])
        mid, rest = halve(rest)
        thrice = jnp.concatenate([high, mid, rest.astype(jnp.bfloat16)], axis=0)
    steps = [(top, at) for top in range(0, total, block) for at in range(0, cols, step)]
    lefts, powers, parts = {}, {}, {}

    def contract(top, at):
        if top not in lefts:
            lefts[top] = jnp.transpose(operands(rows_ref[:, top : top + block] * scale_ref[...])[0])
        powers[top, at] = jnp.dot(lefts[top], right_ref[:, at : at + step], preferred_element_type=jnp.float32)

    def raise_power(top, at):
        high, rest = halve(jnp.exp2(powers.pop((top, at))))
        low = rest.astype(jnp.bfloat16)
        tile_ref[top : top + block, at : at + step] = high
        tile_ref[total + top : total + top + block, at : at + step] = low
        parts[top, at] = high, low

    def apply(top, at):
        down, here = slice(top, top + block), slice(at, at + step)
        vectors = jnp.concatenate([thrice[:, down]] * 2, axis=1)
        both = jnp.concatenate(parts.pop((top, at)), axis=0)
        term = jnp.dot(vectors, both, preferred_element_type=jnp.float32)
        term = term[:probes] + (term[probes : 2 * probes] + term[2 * probes :])
        before = sum_ref if top == 0 else out_ref
        out_ref[:, here] = before[:, here] + term

    contract(*steps[0])
    for k, chunk in enumerate(steps):
        if k + 1 < len(steps):
            contract(*steps[k + 1])
        raise_power(*chunk)
        if k and applies:
            apply(*steps[k - 1])
    if applies:
        apply(*steps[-1])


def call(kernel, outs, *args, **cost):
    whole = pl.BlockSpec(memory_space=pltpu.VMEM)
    return pl.pallas_call(
        kernel,
        out_shape=outs,
        in_specs=[whole] * len(args),
        out_specs=jax.tree.map(lambda _: whole, outs),
        compiler_params=pltpu.CompilerParams(vmem_limit_bytes=VMEM_BYTES),
        cost_estimate=pl.CostEstimate(**cost),
    )(*args)


def prepare(part, scale, copy=0):
    feats, cols = scale.shape[0], part.shape[1]
    outs = (jax.ShapeDtypeStruct((6 * feats + NORM_ROWS, cols), jnp.bfloat16),)
    if copy:
        outs += (jax.ShapeDtypeStruct((copy, cols), part.dtype),)
    return call(prepare_kernel, outs, part, scale, flops=10**0, bytes_accessed=feats * cols, transcendentals=0)


def join(*xs):
    return jnp.concatenate(xs, axis=1)


def build_piece(rows, scale, right, vectors=None, total=None):
    count, cols = rows.shape[1], right.shape[1]
    outs = (jax.ShapeDtypeStruct((2 * count, cols), jnp.bfloat16),)
    cost = dict(flops=2 * count * cols * 416, bytes_accessed=4 * count * cols, transcendentals=count * cols)
    args = (rows, scale, right)
    if vectors is not None:
        outs, args = (*outs, jax.ShapeDtypeStruct(total.shape, jnp.float32)), (*args, vectors, total)
    return call(build_kernel, outs, *args, **cost)


def parts_of(vectors):
    high, mid, low = split(vectors, 3)
    return jnp.concatenate([high, mid, low], axis=0)


def apply_parts(parts, piece):
    return jnp.dot(jnp.concatenate([parts, parts], axis=1), piece, preferred_element_type=jnp.float32)


def apply_piece(vectors, piece):
    return apply_parts(parts_of(vectors), piece)


def collect(total):
    probes = total.shape[0] // 3
    return total[:probes] + (total[probes : 2 * probes] + total[2 * probes :])


def solution(mesh):
    n = mesh.shape["blk"]
    strides = [1 << k for k in reversed(range(n.bit_length() - 1))]

    def body(points, lengthscale, noise_var, targets):
        feats, width = points.shape
        probes = targets.shape[0]
        team = min(n, 4)
        while team < n and (n * width) * (n * width) // team * 4 > TILE_BYTES:
            team *= 2
        outer, inner = [s for s in strides if s >= team], [s for s in strides if s < team]

        def arrivals(x):
            pieces, sent = [x, swap(x, n, 1)], [x]
            for stride in inner[:-1]:
                came = swap(sent[0] if len(sent) == 1 else jnp.concatenate(sent, axis=1), n, stride)
                sent.append(came)
                pieces += [came, swap(came, n, 1)]
            return pieces

        scale = (POINT_SCALE / lengthscale)[:, None]
        used = feats + probes + 1
        spare = jnp.pad(noise_var[None, :], ((0, -used % 8), (0, 0)))
        block = lax.optimization_barrier(jnp.concatenate([points, targets, spare], axis=0))
        fence = lax.optimization_barrier
        tile = []

        def build(x, total):
            piece, total = build_piece(x[:feats], scale, right, x[feats:], total)
            tile.append(piece)
            return total

        if len(outer) == 2 and len(inner) == 2:
            far, near, side = outer[0], outer[1], inner[0]
            by_far = swap(block, n, far)
            right_own, copy = prepare(block, scale, used)
            near_own = swap(copy, n, near)
            side_own = swap(copy, n, side)
            near_far = swap(by_far, n, near)
            right_far, copy = prepare(by_far, scale, used)
            side_far = swap(copy, n, side)
            right_near, by_near = prepare(join(near_own, near_far[:used]), scale, used)
            last, side_own = fence((by_near, side_own))
            side_last = swap(last, n, side)
            right = join(right_own, right_far, right_near)
            mine = join(block[:used], by_far[:used], by_near)
            noise, mine = mine[-1:], mine[:-1]
            across = swap(mine, n, 1)
            my_applied = build(mine, noise * mine[feats:])
            my_applied = build(across, my_applied)
            side_last, side_far, my_applied = fence((side_last, side_far, my_applied))
            beside = join(side_own, side_far, side_last)
            noise_beside, beside = beside[-1:], beside[:-1]
            beside_across = swap(beside, n, 1)
            my_far = build(beside, jnp.zeros_like(my_applied))
            my_far = build(beside_across, my_far)
            my_applied = my_applied + my_far
            first = [mine, across, beside, beside_across]
            far_rows = [beside[:feats], beside_across[:feats]]
        else:
            mine = block
            for stride in outer:
                mine = join(mine, swap(mine, n, stride))
            mine = mine[:used]
            (right,), noise, first = prepare(mine, scale), mine[-1:], arrivals(mine[:-1])
            my_applied = noise * first[0][feats:]
            for x in first:
                my_applied = build(x, my_applied)
            my_far, far_rows = my_applied, []
        cols = noise.shape[1]
        starts = [x[feats:] for x in first]

        far_tile, right_far = [], None

        def exchange(x, direction):
            nonlocal right_far
            parts, passed = fence((parts_of(x), x))
            pieces, sent = [x, swap(passed, n, 1)], [x]
            near = fence(apply_parts(parts, tile[0]))
            near = fence(near + apply_piece(pieces[1], tile[1]))
            far = jnp.zeros_like(near) if len(inner) == 1 else None
            near = fence(collect(near) + noise * x)
            for k, stride in enumerate(inner[:-1]):
                arrived = swap(join(*sent), n, stride)
                if len(far_tile) < len(far_rows):
                    rows, columns, near = fence((far_rows[len(far_tile)], far_rows[0], near))
                    if right_far is None:
                        (right_far,) = prepare(columns, scale)
                    (piece,) = build_piece(rows, scale, right_far)
                    piece, right_far, near = fence((piece, right_far, near))
                    far_tile.append(piece)
                arrived, near = fence((arrived, near))
                sent.append(arrived)
                pieces.append(arrived)
                term = apply_piece(arrived, tile[2 + 2 * k])
                far = fence(term if far is None else far + term)
                pieces.append(swap(arrived, n, 1))
                if k < len(inner) - 2:
                    far = fence(far + apply_piece(pieces[-1], tile[3 + 2 * k]))
            before = join(*pieces[:-1])
            curve = jnp.sum(direction[:, : before.shape[1]] * before, axis=1)
            curve, far = fence((curve, far))
            curve = curve + jnp.sum(direction[:, before.shape[1] :] * pieces[-1], axis=1)
            if len(inner) > 1:
                far = far + apply_piece(pieces[-1], tile[-1])
            return collect(far), near + collect(far), join(*pieces), curve

        residual = direction = join(*starts)
        my_solution = jnp.zeros_like(direction[:, :width])
        norm_now = jnp.sum(residual * residual, axis=1)
        my_image, far_image = my_applied, my_far
        for iteration in range(ITERS - 1):
            far_next, my_next, applied, curve = exchange(my_applied, direction)
            step_size = (norm_now / curve)[:, None]
            my_solution = my_solution + step_size * direction[:, :width]
            residual = residual - step_size * applied
            norm_next = jnp.sum(residual * residual, axis=1)
            ratio = (norm_next / norm_now)[:, None]
            my_image = my_image - step_size * my_next
            my_applied = my_image + ratio * my_applied
            far_image = far_image - step_size * far_next
            my_far = far_image + ratio * my_far
            direction = residual + ratio * direction
            norm_now = norm_next
        mine = direction[:, :cols]
        if far_rows:
            side, beside = direction[:, 2 * cols : 3 * cols], direction[:, 3 * cols :]
            image = collect(apply_piece(side, far_tile[0]) + apply_piece(beside, far_tile[1])) + noise_beside * side
            curve = add_up(jnp.sum(mine * (my_applied + my_far) + side * image, axis=1), n, [1])
        else:
            curve = add_up(jnp.sum(mine * my_applied, axis=1), n, inner)
        step_size = (norm_now / curve)[:, None]
        my_solution = my_solution + step_size * direction[:, :width]
        return my_solution, residual[:, :width] - step_size * my_applied[:, :width]

    in_specs = (P("groups", "blk"), P("groups"), P(("groups", "blk")), P("groups", "blk"))
    out_specs = (P("groups", "blk"), P("groups", "blk"))
    return jax.shard_map(body, mesh=mesh, in_specs=in_specs, out_specs=out_specs, check_vma=False)
```

```python
import math

import jax
import jax.numpy as jnp
from jax import lax
from jax.experimental import pallas as pl
from jax.experimental.pallas import tpu as pltpu
from jax.sharding import PartitionSpec as P

ITERS = 4
TILE_BYTES = 16 << 20
VMEM_BYTES = 16 << 20
NORM_ROWS = 64
BUILD_ROWS = 1024
POINT_SCALE = math.sqrt(math.log2(math.e))


def swap(x, n, stride):
    return lax.ppermute(x, "blk", [(i, i ^ stride) for i in range(n)])


def add_up(x, n, strides):
    for stride in strides:
        x = x + swap(x, n, stride)
    return x


def split(x, parts):
    out = []
    for _ in range(parts):
        high = lax.reduce_precision(x, 8, 7)
        out.append(high.astype(jnp.bfloat16))
        x = x - high
    return out


def halve(x):
    high = x.astype(jnp.bfloat16)
    return high, x - high.astype(jnp.float32)


def operands(pts):
    high, rest = halve(pts)
    mid, rest = halve(rest)
    low = rest.astype(jnp.bfloat16)
    norms = -0.5 * jnp.sum(pts * pts, axis=0, keepdims=True)
    row = lax.broadcasted_iota(jnp.int32, (NORM_ROWS, pts.shape[1]), 0)
    left = jnp.where((row >= 3) & (row < 6), 1.0, 0.0)
    right = jnp.where(row < 3, 1.0, 0.0)
    for k in range(3):
        part, norms = halve(norms)
        part = part.astype(jnp.float32)
        left = jnp.where(row == k, part, left)
        right = jnp.where(row == 3 + k, part, right)
    left = jnp.concatenate([high, high, mid, high, low, mid, left.astype(jnp.bfloat16)], axis=0)
    right = jnp.concatenate([high, mid, high, low, high, mid, right.astype(jnp.bfloat16)], axis=0)
    return left, right


def prepare_kernel(part_ref, scale_ref, right_ref, *copy_ref):
    feats = scale_ref.shape[0]
    right_ref[...] = operands(part_ref[:feats] * scale_ref[...])[1]
    for ref in copy_ref:
        ref[...] = part_ref[: ref.shape[0]]


def build_kernel(rows_ref, scale_ref, right_ref, *refs):
    applies = len(refs) > 1
    vectors_ref, sum_ref, tile_ref, out_ref = refs if applies else (None, None, *refs, None)
    total, cols = rows_ref.shape[1], right_ref.shape[1]
    block, step = min(total, BUILD_ROWS), min(cols, 512)
    if applies:
        probes = vectors_ref.shape[0]
        high, rest = halve(vectors_ref[...])
        mid, rest = halve(rest)
        thrice = jnp.concatenate([high, mid, rest.astype(jnp.bfloat16)], axis=0)
    steps = [(top, at) for top in range(0, total, block) for at in range(0, cols, step)]
    lefts, powers, parts = {}, {}, {}

    def contract(top, at):
        if top not in lefts:
            lefts[top] = jnp.transpose(operands(rows_ref[:, top : top + block] * scale_ref[...])[0])
        powers[top, at] = jnp.dot(lefts[top], right_ref[:, at : at + step], preferred_element_type=jnp.float32)

    def raise_power(top, at):
        high, rest = halve(jnp.exp2(powers.pop((top, at))))
        low = rest.astype(jnp.bfloat16)
        tile_ref[top : top + block, at : at + step] = high
        tile_ref[total + top : total + top + block, at : at + step] = low
        parts[top, at] = high, low

    def apply(top, at):
        down, here = slice(top, top + block), slice(at, at + step)
        vectors = jnp.concatenate([thrice[:, down]] * 2, axis=1)
        both = jnp.concatenate(parts.pop((top, at)), axis=0)
        term = jnp.dot(vectors, both, preferred_element_type=jnp.float32)
        term = term[:probes] + (term[probes : 2 * probes] + term[2 * probes :])
        before = sum_ref if top == 0 else out_ref
        out_ref[:, here] = before[:, here] + term

    contract(*steps[0])
    for k, chunk in enumerate(steps):
        if k + 1 < len(steps):
            contract(*steps[k + 1])
        raise_power(*chunk)
        if k and applies:
            apply(*steps[k - 1])
    if applies:
        apply(*steps[-1])


def call(kernel, outs, *args, **cost):
    whole = pl.BlockSpec(memory_space=pltpu.VMEM)
    return pl.pallas_call(
        kernel,
        out_shape=outs,
        in_specs=[whole] * len(args),
        out_specs=jax.tree.map(lambda _: whole, outs),
        compiler_params=pltpu.CompilerParams(vmem_limit_bytes=VMEM_BYTES),
        cost_estimate=pl.CostEstimate(**cost),
    )(*args)


def prepare(part, scale, copy=0):
    feats, cols = scale.shape[0], part.shape[1]
    outs = (jax.ShapeDtypeStruct((6 * feats + NORM_ROWS, cols), jnp.bfloat16),)
    if copy:
        outs += (jax.ShapeDtypeStruct((copy, cols), part.dtype),)
    return call(prepare_kernel, outs, part, scale, flops=10**0, bytes_accessed=feats * cols, transcendentals=0)


def join(*xs):
    return jnp.concatenate(xs, axis=1)


def build_piece(rows, scale, right, vectors=None, total=None):
    count, cols = rows.shape[1], right.shape[1]
    outs = (jax.ShapeDtypeStruct((2 * count, cols), jnp.bfloat16),)
    cost = dict(flops=2 * count * cols * 416, bytes_accessed=4 * count * cols, transcendentals=count * cols)
    args = (rows, scale, right)
    if vectors is not None:
        outs, args = (*outs, jax.ShapeDtypeStruct(total.shape, jnp.float32)), (*args, vectors, total)
    return call(build_kernel, outs, *args, **cost)


def parts_of(vectors):
    high, mid, low = split(vectors, 3)
    return jnp.concatenate([high, mid, low], axis=0)


def apply_parts(parts, piece):
    return jnp.dot(jnp.concatenate([parts, parts], axis=1), piece, preferred_element_type=jnp.float32)


def apply_piece(vectors, piece):
    return apply_parts(parts_of(vectors), piece)


def collect(total):
    probes = total.shape[0] // 3
    return total[:probes] + (total[probes : 2 * probes] + total[2 * probes :])


def solution(mesh):
    n = mesh.shape["blk"]
    strides = [1 << k for k in reversed(range(n.bit_length() - 1))]

    def body(points, lengthscale, noise_var, targets):
        feats, width = points.shape
        probes = targets.shape[0]
        team = min(n, 4)
        while team < n and (n * width) * (n * width) // team * 4 > TILE_BYTES:
            team *= 2
        outer, inner = [s for s in strides if s >= team], [s for s in strides if s < team]

        def arrivals(x):
            pieces, sent = [x, swap(x, n, 1)], [x]
            for stride in inner[:-1]:
                came = swap(sent[0] if len(sent) == 1 else jnp.concatenate(sent, axis=1), n, stride)
                sent.append(came)
                pieces += [came, swap(came, n, 1)]
            return pieces

        scale = (POINT_SCALE / lengthscale)[:, None]
        used = feats + probes + 1
        spare = jnp.pad(noise_var[None, :], ((0, -used % 8), (0, 0)))
        block = lax.optimization_barrier(jnp.concatenate([points, targets, spare], axis=0))
        fence = lax.optimization_barrier
        tile = []

        def build(x, total):
            piece, total = build_piece(x[:feats], scale, right, x[feats:], total)
            tile.append(piece)
            return total

        if len(outer) == 2 and len(inner) == 2:
            far, near, side = outer[0], outer[1], inner[0]
            by_far = swap(block, n, far)
            right_own, copy = prepare(block, scale, used)
            near_own = swap(copy, n, near)
            side_own = swap(copy, n, side)
            near_far = swap(by_far, n, near)
            right_far, copy = prepare(by_far, scale, used)
            side_far = swap(copy, n, side)
            right_near, by_near = prepare(join(near_own, near_far[:used]), scale, used)
            last, side_own = fence((by_near, side_own))
            side_last = swap(last, n, side)
            right = join(right_own, right_far, right_near)
            mine = join(block[:used], by_far[:used], by_near)
            noise, mine = mine[-1:], mine[:-1]
            across = swap(mine, n, 1)
            my_applied = build(mine, noise * mine[feats:])
            my_applied = build(across, my_applied)
            side_last, side_far, my_applied = fence((side_last, side_far, my_applied))
            beside = join(side_own, side_far, side_last)
            noise_beside, beside = beside[-1:], beside[:-1]
            beside_across = swap(beside, n, 1)
            my_far = build(beside, jnp.zeros_like(my_applied))
            my_far = build(beside_across, my_far)
            my_applied = my_applied + my_far
            first = [mine, across, beside, beside_across]
            far_rows = [beside[:feats], beside_across[:feats]]
        else:
            mine = block
            for stride in outer:
                mine = join(mine, swap(mine, n, stride))
            mine = mine[:used]
            (right,), noise, first = prepare(mine, scale), mine[-1:], arrivals(mine[:-1])
            my_applied = noise * first[0][feats:]
            for x in first:
                my_applied = build(x, my_applied)
            my_far, far_rows = my_applied, []
        cols = noise.shape[1]
        starts = [x[feats:] for x in first]

        far_tile, right_far = [], None

        def exchange(x, direction):
            nonlocal right_far
            parts, passed = fence((parts_of(x), x))
            pieces, sent = [x, swap(passed, n, 1)], [x]
            near = fence(apply_parts(parts, tile[0]))
            near = fence(near + apply_piece(pieces[1], tile[1]))
            far = jnp.zeros_like(near) if len(inner) == 1 else None
            for k, stride in enumerate(inner[:-1]):
                arrived = swap(join(*sent), n, stride)
                if len(far_tile) < len(far_rows):
                    rows, columns, near = fence((far_rows[len(far_tile)], far_rows[0], near))
                    if right_far is None:
                        (right_far,) = prepare(columns, scale)
                    (piece,) = build_piece(rows, scale, right_far)
                    piece, right_far, near = fence((piece, right_far, near))
                    far_tile.append(piece)
                arrived, near = fence((arrived, near))
                sent.append(arrived)
                pieces.append(arrived)
                term = apply_piece(arrived, tile[2 + 2 * k])
                far = fence(term if far is None else far + term)
                pieces.append(swap(arrived, n, 1))
                if k < len(inner) - 2:
                    far = fence(far + apply_piece(pieces[-1], tile[3 + 2 * k]))
            before = join(*pieces[:-1])
            curve = jnp.sum(direction[:, : before.shape[1]] * before, axis=1)
            curve, far = fence((curve, far))
            curve = curve + jnp.sum(direction[:, before.shape[1] :] * pieces[-1], axis=1)
            if len(inner) > 1:
                far = far + apply_piece(pieces[-1], tile[-1])
            return collect(far), collect(near) + collect(far) + noise * x, join(*pieces), curve

        residual = direction = join(*starts)
        my_solution = jnp.zeros_like(direction[:, :width])
        norm_now = jnp.sum(residual * residual, axis=1)
        my_image, far_image = my_applied, my_far
        for iteration in range(ITERS - 1):
            far_next, my_next, applied, curve = exchange(my_applied, direction)
            step_size = (norm_now / curve)[:, None]
            my_solution = my_solution + step_size * direction[:, :width]
            residual = residual - step_size * applied
            norm_next = jnp.sum(residual * residual, axis=1)
            ratio = (norm_next / norm_now)[:, None]
            my_image = my_image - step_size * my_next
            my_applied = my_image + ratio * my_applied
            far_image = far_image - step_size * far_next
            my_far = far_image + ratio * my_far
            direction = residual + ratio * direction
            norm_now = norm_next
        mine = direction[:, :cols]
        if far_rows:
            side, beside = direction[:, 2 * cols : 3 * cols], direction[:, 3 * cols :]
            image = collect(apply_piece(side, far_tile[0]) + apply_piece(beside, far_tile[1])) + noise_beside * side
            curve = add_up(jnp.sum(mine * (my_applied + my_far) + side * image, axis=1), n, [1])
        else:
            curve = add_up(jnp.sum(mine * my_applied, axis=1), n, inner)
        step_size = (norm_now / curve)[:, None]
        my_solution = my_solution + step_size * direction[:, :width]
        return my_solution, residual[:, :width] - step_size * my_applied[:, :width]

    in_specs = (P("groups", "blk"), P("groups"), P(("groups", "blk")), P("groups", "blk"))
    out_specs = (P("groups", "blk"), P("groups", "blk"))
    return jax.shard_map(body, mesh=mesh, in_specs=in_specs, out_specs=out_specs, check_vma=False)
```

```python
import math

import jax
import jax.numpy as jnp
from jax import lax
from jax.experimental import pallas as pl
from jax.experimental.pallas import tpu as pltpu
from jax.sharding import PartitionSpec as P

ITERS = 4
TILE_BYTES = 16 << 20
VMEM_BYTES = 16 << 20
NORM_ROWS = 64
BUILD_ROWS = 1024
POINT_SCALE = math.sqrt(math.log2(math.e))


def swap(x, n, stride):
    return lax.ppermute(x, "blk", [(i, i ^ stride) for i in range(n)])


def add_up(x, n, strides):
    for stride in strides:
        x = x + swap(x, n, stride)
    return x


def split(x, parts):
    out = []
    for _ in range(parts):
        high = lax.reduce_precision(x, 8, 7)
        out.append(high.astype(jnp.bfloat16))
        x = x - high
    return out


def halve(x):
    high = x.astype(jnp.bfloat16)
    return high, x - high.astype(jnp.float32)


def operands(pts):
    high, rest = halve(pts)
    mid, rest = halve(rest)
    low = rest.astype(jnp.bfloat16)
    norms = -0.5 * jnp.sum(pts * pts, axis=0, keepdims=True)
    row = lax.broadcasted_iota(jnp.int32, (NORM_ROWS, pts.shape[1]), 0)
    left = jnp.where((row >= 3) & (row < 6), 1.0, 0.0)
    right = jnp.where(row < 3, 1.0, 0.0)
    for k in range(3):
        part, norms = halve(norms)
        part = part.astype(jnp.float32)
        left = jnp.where(row == k, part, left)
        right = jnp.where(row == 3 + k, part, right)
    left = jnp.concatenate([high, high, mid, high, low, mid, left.astype(jnp.bfloat16)], axis=0)
    right = jnp.concatenate([high, mid, high, low, high, mid, right.astype(jnp.bfloat16)], axis=0)
    return left, right


def prepare_kernel(part_ref, scale_ref, right_ref, *copy_ref):
    feats = scale_ref.shape[0]
    right_ref[...] = operands(part_ref[:feats] * scale_ref[...])[1]
    for ref in copy_ref:
        ref[...] = part_ref[: ref.shape[0]]


def build_kernel(rows_ref, scale_ref, right_ref, *refs):
    applies = len(refs) > 1
    vectors_ref, sum_ref, tile_ref, out_ref = refs if applies else (None, None, *refs, None)
    total, cols = rows_ref.shape[1], right_ref.shape[1]
    block, step = min(total, BUILD_ROWS), min(cols, 256)
    if applies:
        probes = vectors_ref.shape[0]
        high, rest = halve(vectors_ref[...])
        mid, rest = halve(rest)
        thrice = jnp.concatenate([high, mid, rest.astype(jnp.bfloat16)], axis=0)
    steps = [(top, at, block) for top in range(0, total, block) for at in range(0, cols, step)]
    if len(steps) > 1:
        top, at, _ = steps.pop()
        steps += [(top, at, block // 2), (top + block // 2, at, block // 2)]
    lefts, powers, parts = {}, {}, {}
    fresh = {(0, at) for at in range(0, cols, step)}

    def contract(top, at, size):
        base = top // block * block
        if base not in lefts:
            lefts[base] = jnp.transpose(operands(rows_ref[:, base : base + block] * scale_ref[...])[0])
        powers[top, at] = jnp.dot(lefts[base][top - base : top - base + size], right_ref[:, at : at + step], preferred_element_type=jnp.float32)

    def raise_power(top, at, block):
        high, rest = halve(jnp.exp2(powers.pop((top, at))))
        low = rest.astype(jnp.bfloat16)
        tile_ref[top : top + block, at : at + step] = high
        tile_ref[total + top : total + top + block, at : at + step] = low
        parts[top, at] = high, low

    def apply(top, at, block):
        down, here = slice(top, top + block), slice(at, at + step)
        vectors = jnp.concatenate([thrice[:, down]] * 2, axis=1)
        both = jnp.concatenate(parts.pop((top, at)), axis=0)
        term = jnp.dot(vectors, both, preferred_element_type=jnp.float32)
        term = term[:probes] + (term[probes : 2 * probes] + term[2 * probes :])
        before = sum_ref if (top, at) in fresh else out_ref
        out_ref[:, here] = before[:, here] + term

    contract(*steps[0])
    for k, chunk in enumerate(steps):
        if k + 1 < len(steps):
            contract(*steps[k + 1])
        raise_power(*chunk)
        if k and applies:
            apply(*steps[k - 1])
    if applies:
        apply(*steps[-1])


def call(kernel, outs, *args, **cost):
    whole = pl.BlockSpec(memory_space=pltpu.VMEM)
    return pl.pallas_call(
        kernel,
        out_shape=outs,
        in_specs=[whole] * len(args),
        out_specs=jax.tree.map(lambda _: whole, outs),
        compiler_params=pltpu.CompilerParams(vmem_limit_bytes=VMEM_BYTES),
        cost_estimate=pl.CostEstimate(**cost),
    )(*args)


def prepare(part, scale, copy=0):
    feats, cols = scale.shape[0], part.shape[1]
    outs = (jax.ShapeDtypeStruct((6 * feats + NORM_ROWS, cols), jnp.bfloat16),)
    if copy:
        outs += (jax.ShapeDtypeStruct((copy, cols), part.dtype),)
    return call(prepare_kernel, outs, part, scale, flops=10**0, bytes_accessed=feats * cols, transcendentals=0)


def join(*xs):
    return jnp.concatenate(xs, axis=1)


def build_piece(rows, scale, right, vectors=None, total=None):
    count, cols = rows.shape[1], right.shape[1]
    outs = (jax.ShapeDtypeStruct((2 * count, cols), jnp.bfloat16),)
    cost = dict(flops=2 * count * cols * 416, bytes_accessed=4 * count * cols, transcendentals=count * cols)
    args = (rows, scale, right)
    if vectors is not None:
        outs, args = (*outs, jax.ShapeDtypeStruct(total.shape, jnp.float32)), (*args, vectors, total)
    return call(build_kernel, outs, *args, **cost)


def parts_of(vectors):
    high, mid, low = split(vectors, 3)
    return jnp.concatenate([high, mid, low], axis=0)


def apply_parts(parts, piece):
    return jnp.dot(jnp.concatenate([parts, parts], axis=1), piece, preferred_element_type=jnp.float32)


def apply_piece(vectors, piece):
    return apply_parts(parts_of(vectors), piece)


def collect(total):
    probes = total.shape[0] // 3
    return total[:probes] + (total[probes : 2 * probes] + total[2 * probes :])


def solution(mesh):
    n = mesh.shape["blk"]
    strides = [1 << k for k in reversed(range(n.bit_length() - 1))]

    def body(points, lengthscale, noise_var, targets):
        feats, width = points.shape
        probes = targets.shape[0]
        team = min(n, 4)
        while team < n and (n * width) * (n * width) // team * 4 > TILE_BYTES:
            team *= 2
        outer, inner = [s for s in strides if s >= team], [s for s in strides if s < team]

        def arrivals(x):
            pieces, sent = [x, swap(x, n, 1)], [x]
            for stride in inner[:-1]:
                came = swap(sent[0] if len(sent) == 1 else jnp.concatenate(sent, axis=1), n, stride)
                sent.append(came)
                pieces += [came, swap(came, n, 1)]
            return pieces

        scale = (POINT_SCALE / lengthscale)[:, None]
        used = feats + probes + 1
        spare = jnp.pad(noise_var[None, :], ((0, -used % 8), (0, 0)))
        block = lax.optimization_barrier(jnp.concatenate([points, targets, spare], axis=0))
        fence = lax.optimization_barrier
        tile = []

        def build(x, total):
            piece, total = build_piece(x[:feats], scale, right, x[feats:], total)
            tile.append(piece)
            return total

        if len(outer) == 2 and len(inner) == 2:
            far, near, side = outer[0], outer[1], inner[0]
            by_far = swap(block, n, far)
            right_own, copy = prepare(block, scale, used)
            near_own = swap(copy, n, near)
            side_own = swap(copy, n, side)
            near_far = swap(by_far, n, near)
            right_far, copy = prepare(by_far, scale, used)
            side_far = swap(copy, n, side)
            right_near, by_near = prepare(join(near_own, near_far[:used]), scale, used)
            last, side_own = fence((by_near, side_own))
            side_last = swap(last, n, side)
            right = join(right_own, right_far, right_near)
            mine = join(block[:used], by_far[:used], by_near)
            noise, mine = mine[-1:], mine[:-1]
            across = swap(mine, n, 1)
            my_applied = build(mine, noise * mine[feats:])
            my_applied = build(across, my_applied)
            side_last, side_far, my_applied = fence((side_last, side_far, my_applied))
            beside = join(side_own, side_far, side_last)
            noise_beside, beside = beside[-1:], beside[:-1]
            beside_across = swap(beside, n, 1)
            my_far = build(beside, jnp.zeros_like(my_applied))
            my_far = build(beside_across, my_far)
            my_applied = my_applied + my_far
            first = [mine, across, beside, beside_across]
            far_rows = [beside[:feats], beside_across[:feats]]
        else:
            mine = block
            for stride in outer:
                mine = join(mine, swap(mine, n, stride))
            mine = mine[:used]
            (right,), noise, first = prepare(mine, scale), mine[-1:], arrivals(mine[:-1])
            my_applied = noise * first[0][feats:]
            for x in first:
                my_applied = build(x, my_applied)
            my_far, far_rows = my_applied, []
        cols = noise.shape[1]
        starts = [x[feats:] for x in first]

        far_tile, right_far = [], None

        def exchange(x, direction):
            nonlocal right_far
            parts, passed = fence((parts_of(x), x))
            pieces, sent = [x, swap(passed, n, 1)], [x]
            near = fence(apply_parts(parts, tile[0]))
            near = fence(near + apply_piece(pieces[1], tile[1]))
            far = jnp.zeros_like(near) if len(inner) == 1 else None
            for k, stride in enumerate(inner[:-1]):
                arrived = swap(join(*sent), n, stride)
                if len(far_tile) < len(far_rows):
                    rows, columns, near = fence((far_rows[len(far_tile)], far_rows[0], near))
                    if right_far is None:
                        (right_far,) = prepare(columns, scale)
                    (piece,) = build_piece(rows, scale, right_far)
                    piece, right_far, near = fence((piece, right_far, near))
                    far_tile.append(piece)
                arrived, near = fence((arrived, near))
                sent.append(arrived)
                pieces.append(arrived)
                term = apply_piece(arrived, tile[2 + 2 * k])
                far = fence(term if far is None else far + term)
                pieces.append(swap(arrived, n, 1))
                if k < len(inner) - 2:
                    far = fence(far + apply_piece(pieces[-1], tile[3 + 2 * k]))
            before = join(*pieces[:-1])
            curve = jnp.sum(direction[:, : before.shape[1]] * before, axis=1)
            curve, far = fence((curve, far))
            curve = curve + jnp.sum(direction[:, before.shape[1] :] * pieces[-1], axis=1)
            if len(inner) > 1:
                far = far + apply_piece(pieces[-1], tile[-1])
            return collect(far), collect(near) + collect(far) + noise * x, join(*pieces), curve

        residual = direction = join(*starts)
        my_solution = jnp.zeros_like(direction[:, :width])
        norm_now = jnp.sum(residual * residual, axis=1)
        my_image, far_image = my_applied, my_far
        for iteration in range(ITERS - 1):
            far_next, my_next, applied, curve = exchange(my_applied, direction)
            step_size = (norm_now / curve)[:, None]
            my_solution = my_solution + step_size * direction[:, :width]
            residual = residual - step_size * applied
            norm_next = jnp.sum(residual * residual, axis=1)
            ratio = (norm_next / norm_now)[:, None]
            my_image = my_image - step_size * my_next
            my_applied = my_image + ratio * my_applied
            far_image = far_image - step_size * far_next
            my_far = far_image + ratio * my_far
            direction = residual + ratio * direction
            norm_now = norm_next
        mine = direction[:, :cols]
        if far_rows:
            side, beside = direction[:, 2 * cols : 3 * cols], direction[:, 3 * cols :]
            image = collect(apply_piece(side, far_tile[0]) + apply_piece(beside, far_tile[1])) + noise_beside * side
            curve = add_up(jnp.sum(mine * (my_applied + my_far) + side * image, axis=1), n, [1])
        else:
            curve = add_up(jnp.sum(mine * my_applied, axis=1), n, inner)
        step_size = (norm_now / curve)[:, None]
        my_solution = my_solution + step_size * direction[:, :width]
        return my_solution, residual[:, :width] - step_size * my_applied[:, :width]

    in_specs = (P("groups", "blk"), P("groups"), P(("groups", "blk")), P("groups", "blk"))
    out_specs = (P("groups", "blk"), P("groups", "blk"))
    return jax.shard_map(body, mesh=mesh, in_specs=in_specs, out_specs=out_specs, check_vma=False)
```

```python
import math

import jax
import jax.numpy as jnp
from jax import lax
from jax.experimental import pallas as pl
from jax.experimental.pallas import tpu as pltpu
from jax.sharding import PartitionSpec as P

ITERS = 4
TILE_BYTES = 16 << 20
VMEM_BYTES = 16 << 20
NORM_ROWS = 64
BUILD_ROWS = 1024
POINT_SCALE = math.sqrt(math.log2(math.e))


def swap(x, n, stride):
    return lax.ppermute(x, "blk", [(i, i ^ stride) for i in range(n)])


def add_up(x, n, strides):
    for stride in strides:
        x = x + swap(x, n, stride)
    return x


def split(x, parts):
    out = []
    for _ in range(parts):
        high = lax.reduce_precision(x, 8, 7)
        out.append(high.astype(jnp.bfloat16))
        x = x - high
    return out


def halve(x):
    high = x.astype(jnp.bfloat16)
    return high, x - high.astype(jnp.float32)


def operands(pts):
    high, rest = halve(pts)
    mid, rest = halve(rest)
    low = rest.astype(jnp.bfloat16)
    norms = -0.5 * jnp.sum(pts * pts, axis=0, keepdims=True)
    row = lax.broadcasted_iota(jnp.int32, (NORM_ROWS, pts.shape[1]), 0)
    left = jnp.where((row >= 3) & (row < 6), 1.0, 0.0)
    right = jnp.where(row < 3, 1.0, 0.0)
    for k in range(3):
        part, norms = halve(norms)
        part = part.astype(jnp.float32)
        left = jnp.where(row == k, part, left)
        right = jnp.where(row == 3 + k, part, right)
    left = jnp.concatenate([high, high, mid, high, low, mid, left.astype(jnp.bfloat16)], axis=0)
    right = jnp.concatenate([high, mid, high, low, high, mid, right.astype(jnp.bfloat16)], axis=0)
    return left, right


def prepare_kernel(part_ref, scale_ref, right_ref, *copy_ref):
    feats = scale_ref.shape[0]
    right_ref[...] = operands(part_ref[:feats] * scale_ref[...])[1]
    for ref in copy_ref:
        ref[...] = part_ref[: ref.shape[0]]


def build_kernel(rows_ref, scale_ref, right_ref, *refs):
    applies = len(refs) > 1
    vectors_ref, sum_ref, tile_ref, out_ref = refs if applies else (None, None, *refs, None)
    total, cols = rows_ref.shape[1], right_ref.shape[1]
    block, step = min(total, BUILD_ROWS), min(cols, 256)
    if applies:
        probes = vectors_ref.shape[0]
        high, rest = halve(vectors_ref[...])
        mid, rest = halve(rest)
        thrice = jnp.concatenate([high, mid, rest.astype(jnp.bfloat16)], axis=0)
    steps = [(top, at, block) for top in range(0, total, block) for at in range(0, cols, step)]
    if len(steps) > 1:
        top, at, _ = steps.pop()
        steps += [(top, at, block // 2), (top + block // 2, at, block // 2)]
    lefts, powers, parts = {}, {}, {}
    fresh = {(0, at) for at in range(0, cols, step)}

    def contract(top, at, size):
        base = top // block * block
        if base not in lefts:
            lefts[base] = jnp.transpose(operands(rows_ref[:, base : base + block] * scale_ref[...])[0])
        powers[top, at] = jnp.dot(lefts[base][top - base : top - base + size], right_ref[:, at : at + step], preferred_element_type=jnp.float32)

    def raise_power(top, at, block):
        high, rest = halve(jnp.exp2(powers.pop((top, at))))
        low = rest.astype(jnp.bfloat16)
        tile_ref[top : top + block, at : at + step] = high
        tile_ref[total + top : total + top + block, at : at + step] = low
        parts[top, at] = high, low

    def apply(top, at, block):
        down, here = slice(top, top + block), slice(at, at + step)
        vectors = jnp.concatenate([thrice[:, down]] * 2, axis=1)
        both = jnp.concatenate(parts.pop((top, at)), axis=0)
        term = jnp.dot(vectors, both, preferred_element_type=jnp.float32)
        term = term[:probes] + (term[probes : 2 * probes] + term[2 * probes :])
        before = sum_ref if (top, at) in fresh else out_ref
        out_ref[:, here] = before[:, here] + term

    contract(*steps[0])
    for k, chunk in enumerate(steps):
        if k + 1 < len(steps):
            contract(*steps[k + 1])
        raise_power(*chunk)
        if k and applies:
            apply(*steps[k - 1])
    if applies:
        apply(*steps[-1])


def call(kernel, outs, *args, **cost):
    whole = pl.BlockSpec(memory_space=pltpu.VMEM)
    return pl.pallas_call(
        kernel,
        out_shape=outs,
        in_specs=[whole] * len(args),
        out_specs=jax.tree.map(lambda _: whole, outs),
        compiler_params=pltpu.CompilerParams(vmem_limit_bytes=VMEM_BYTES),
        cost_estimate=pl.CostEstimate(**cost),
    )(*args)


def prepare(part, scale, copy=0):
    feats, cols = scale.shape[0], part.shape[1]
    outs = (jax.ShapeDtypeStruct((6 * feats + NORM_ROWS, cols), jnp.bfloat16),)
    if copy:
        outs += (jax.ShapeDtypeStruct((copy, cols), part.dtype),)
    return call(prepare_kernel, outs, part, scale, flops=10**0, bytes_accessed=feats * cols, transcendentals=0)


def join(*xs):
    return jnp.concatenate(xs, axis=1)


def build_piece(rows, scale, right, vectors=None, total=None):
    count, cols = rows.shape[1], right.shape[1]
    outs = (jax.ShapeDtypeStruct((2 * count, cols), jnp.bfloat16),)
    cost = dict(flops=2 * count * cols * 416, bytes_accessed=4 * count * cols, transcendentals=count * cols)
    args = (rows, scale, right)
    if vectors is not None:
        outs, args = (*outs, jax.ShapeDtypeStruct(total.shape, jnp.float32)), (*args, vectors, total)
    return call(build_kernel, outs, *args, **cost)


def parts_of(vectors):
    high, mid, low = split(vectors, 3)
    return jnp.concatenate([high, mid, low], axis=0)


def apply_parts(parts, piece):
    return jnp.dot(jnp.concatenate([parts, parts], axis=1), piece, preferred_element_type=jnp.float32)


def apply_piece(vectors, piece):
    return apply_parts(parts_of(vectors), piece)


def collect(total):
    probes = total.shape[0] // 3
    return total[:probes] + (total[probes : 2 * probes] + total[2 * probes :])


def solution(mesh):
    n = mesh.shape["blk"]
    strides = [1 << k for k in reversed(range(n.bit_length() - 1))]

    def body(points, lengthscale, noise_var, targets):
        feats, width = points.shape
        probes = targets.shape[0]
        team = min(n, 4)
        while team < n and (n * width) * (n * width) // team * 4 > TILE_BYTES:
            team *= 2
        outer, inner = [s for s in strides if s >= team], [s for s in strides if s < team]

        def arrivals(x):
            pieces, sent = [x, swap(x, n, 1)], [x]
            for stride in inner[:-1]:
                came = swap(sent[0] if len(sent) == 1 else jnp.concatenate(sent, axis=1), n, stride)
                sent.append(came)
                pieces += [came, swap(came, n, 1)]
            return pieces

        scale = (POINT_SCALE / lengthscale)[:, None]
        used = feats + probes + 1
        spare = jnp.pad(noise_var[None, :], ((0, -used % 8), (0, 0)))
        block = lax.optimization_barrier(jnp.concatenate([points, targets, spare], axis=0))
        fence = lax.optimization_barrier
        tile = []

        def build(x, total):
            piece, total = build_piece(x[:feats], scale, right, x[feats:], total)
            tile.append(piece)
            return total

        if len(outer) == 2 and len(inner) == 2:
            far, near, side = outer[0], outer[1], inner[0]
            by_far = swap(block, n, far)
            right_own, copy = prepare(block, scale, used)
            near_own = swap(copy, n, near)
            side_own = swap(copy, n, side)
            near_far = swap(by_far, n, near)
            right_far, copy = prepare(by_far, scale, used)
            side_far = swap(copy, n, side)
            right_near, by_near = prepare(join(near_own, near_far[:used]), scale, used)
            last, side_own = fence((by_near, side_own))
            side_last = swap(last, n, side)
            right = join(right_own, right_far, right_near)
            mine = join(block[:used], by_far[:used], by_near)
            noise, mine = mine[-1:], mine[:-1]
            across = swap(mine, n, 1)
            my_applied = build(mine, noise * mine[feats:])
            my_applied = build(across, my_applied)
            side_last, side_far, my_applied = fence((side_last, side_far, my_applied))
            beside = join(side_own, side_far, side_last)
            noise_beside, beside = beside[-1:], beside[:-1]
            beside_across = swap(beside, n, 1)
            my_far = build(beside, jnp.zeros_like(my_applied))
            my_far = build(beside_across, my_far)
            my_applied = my_applied + my_far
            first = [mine, across, beside, beside_across]
            far_rows = [beside[:feats], beside_across[:feats]]
        else:
            mine = block
            for stride in outer:
                mine = join(mine, swap(mine, n, stride))
            mine = mine[:used]
            (right,), noise, first = prepare(mine, scale), mine[-1:], arrivals(mine[:-1])
            my_applied = noise * first[0][feats:]
            for x in first:
                my_applied = build(x, my_applied)
            my_far, far_rows = my_applied, []
        cols = noise.shape[1]
        starts = [x[feats:] for x in first]

        far_tile, right_far = [], None

        def exchange(x, direction):
            nonlocal right_far
            parts, passed = fence((parts_of(x), x))
            pieces, sent = [x, swap(passed, n, 1)], [x]
            near = fence(apply_parts(parts, tile[0]))
            near = fence(near + apply_piece(pieces[1], tile[1]))
            far = jnp.zeros_like(near) if len(inner) == 1 else None
            near = fence(collect(near) + noise * x)
            for k, stride in enumerate(inner[:-1]):
                arrived = swap(join(*sent), n, stride)
                if len(far_tile) < len(far_rows):
                    rows, columns, near = fence((far_rows[len(far_tile)], far_rows[0], near))
                    if right_far is None:
                        (right_far,) = prepare(columns, scale)
                    (piece,) = build_piece(rows, scale, right_far)
                    piece, right_far, near = fence((piece, right_far, near))
                    far_tile.append(piece)
                arrived, near = fence((arrived, near))
                sent.append(arrived)
                pieces.append(arrived)
                term = apply_piece(arrived, tile[2 + 2 * k])
                far = fence(term if far is None else far + term)
                pieces.append(swap(arrived, n, 1))
                if k < len(inner) - 2:
                    far = fence(far + apply_piece(pieces[-1], tile[3 + 2 * k]))
            before = join(*pieces[:-1])
            curve = jnp.sum(direction[:, : before.shape[1]] * before, axis=1)
            curve, far = fence((curve, far))
            curve = curve + jnp.sum(direction[:, before.shape[1] :] * pieces[-1], axis=1)
            if len(inner) > 1:
                far = far + apply_piece(pieces[-1], tile[-1])
            return collect(far), near + collect(far), join(*pieces), curve

        residual = direction = join(*starts)
        my_solution = jnp.zeros_like(direction[:, :width])
        norm_now = jnp.sum(residual * residual, axis=1)
        my_image, far_image = my_applied, my_far
        for iteration in range(ITERS - 1):
            far_next, my_next, applied, curve = exchange(my_applied, direction)
            step_size = (norm_now / curve)[:, None]
            my_solution = my_solution + step_size * direction[:, :width]
            residual = residual - step_size * applied
            norm_next = jnp.sum(residual * residual, axis=1)
            ratio = (norm_next / norm_now)[:, None]
            my_image = my_image - step_size * my_next
            my_applied = my_image + ratio * my_applied
            far_image = far_image - step_size * far_next
            my_far = far_image + ratio * my_far
            direction = residual + ratio * direction
            norm_now = norm_next
        mine = direction[:, :cols]
        if far_rows:
            side, beside = direction[:, 2 * cols : 3 * cols], direction[:, 3 * cols :]
            image = collect(apply_piece(side, far_tile[0]) + apply_piece(beside, far_tile[1])) + noise_beside * side
            curve = add_up(jnp.sum(mine * (my_applied + my_far) + side * image, axis=1), n, [1])
        else:
            curve = add_up(jnp.sum(mine * my_applied, axis=1), n, inner)
        step_size = (norm_now / curve)[:, None]
        my_solution = my_solution + step_size * direction[:, :width]
        return my_solution, residual[:, :width] - step_size * my_applied[:, :width]

    in_specs = (P("groups", "blk"), P("groups"), P(("groups", "blk")), P("groups", "blk"))
    out_specs = (P("groups", "blk"), P("groups", "blk"))
    return jax.shard_map(body, mesh=mesh, in_specs=in_specs, out_specs=out_specs, check_vma=False)
```
